32 devices in a mesh: seq: 2 (over y), ctx: 4 (over x, core), fsdp: 4 (over z).
Axes of the slice: x: 2, y: 2, z: 4, core: 2. Of those that a mesh axis runs over, the one named last changes fastest.
Arguments:
- layer_input: bfloat16 [8, 768, 2048], P(('seq', 'fsdp'), 'ctx'), may hold values from -48 to 48
- document_ids: int32 [8, 768], P(('seq', 'fsdp')), may hold values from 0 to 5, as said below
- cotangent: bfloat16 [8, 768, 2048], P(('seq', 'fsdp'), 'ctx'), may hold values from -6 to 6
- attention_gain: bfloat16 [2048], P(('ctx', 'fsdp')), may hold values from 0.5 to 1.5
- query_weight: bfloat16 [2048, 2048], P(('ctx', 'fsdp')), may hold values from -0.125 to 0.125
- key_weight: bfloat16 [2048, 2048], P(('ctx', 'fsdp')), may hold values from -0.125 to 0.125
- value_weight: bfloat16 [2048, 2048], P(('ctx', 'fsdp')), may hold values from -0.125 to 0.125
- output_weight: bfloat16 [2048, 2048], P(('ctx', 'fsdp')), may hold values from -0.375 to 0.375
- feedforward_gain: bfloat16 [2048], P(('ctx', 'fsdp')), may hold values from 0.5 to 1.5
- gate_weight: bfloat16 [2048, 8192], P(('ctx', 'fsdp')), may hold values from -0.125 to 0.125
- up_weight: bfloat16 [2048, 8192], P(('ctx', 'fsdp')), may hold values from -0.125 to 0.125
- down_weight: bfloat16 [8192, 2048], P(('ctx', 'fsdp')), may hold values from -0.0625 to 0.0625
Outputs:
- layer_output: bfloat16 [8, 768, 2048], P(('seq', 'fsdp'), 'ctx')
- input_grad: bfloat16 [8, 768, 2048], P(('seq', 'fsdp'), 'ctx')
- attention_gain_grad: float32 [2048], P(('ctx', 'fsdp'))
- query_weight_grad: float32 [2048, 2048], P(('ctx', 'fsdp'))
- key_weight_grad: float32 [2048, 2048], P(('ctx', 'fsdp'))
- value_weight_grad: float32 [2048, 2048], P(('ctx', 'fsdp'))
- output_weight_grad: float32 [2048, 2048], P(('ctx', 'fsdp'))
- feedforward_gain_grad: float32 [2048], P(('ctx', 'fsdp'))
- gate_weight_grad: float32 [2048, 8192], P(('ctx', 'fsdp'))
- up_weight_grad: float32 [2048, 8192], P(('ctx', 'fsdp'))
- down_weight_grad: float32 [8192, 2048], P(('ctx', 'fsdp'))
The draws below stay inside these ranges and needn't reach their ends.
Inputs may be any that keep to these rules, and one draw needn't show every extreme that they name: `document_ids`: along each sequence the ids never fall; document 0 covers at least the first half of the sequence.
All inputs are finite; a program needn't handle non-finite values.
Results may differ from the reference program's by a relative error of at most 0.02.
Values may be sent and summed in bfloat16 or wider, within the bound.
No kernel may reach another device: no remote copies, remote signals or barrier semaphores. Data moves between devices by JAX's collectives and lax.ppermute only.
A program may use at most 576 MiB of HBM per device.

```python
import jax
import jax.numpy as jnp
from jax import lax

D = 2048
FF = 8192
HEADS = 32
HEAD_DIM = 64
BLOCK = 96
TOK_DEV = 192
LENGTH = 768
SEQS = 8
N_CTX = 4


def draw_layer_input(key, part):
    key = jax.random.fold_in(key, 11)
    key_rows, key_cols, key_base = jax.random.split(key, 3)
    row_scale = jnp.exp(jax.random.uniform(key_rows, (SEQS, LENGTH, 1), jnp.float32, jnp.log(0.4), jnp.log(4.0)))
    col_scale = jnp.exp(jax.random.uniform(key_cols, (1, 1, D), jnp.float32, jnp.log(0.5), jnp.log(2.0)))
    base_values = jnp.clip(jax.random.normal(key_base, (SEQS, LENGTH, D), jnp.float32), -6.0, 6.0)
    return (base_values * row_scale * col_scale).astype(jnp.bfloat16)


def draw_document_ids(key, part):
    key = jax.random.fold_in(key, 23)
    key_first, key_cuts = jax.random.split(key)
    first_end = LENGTH // 2 + jax.random.randint(key_first, (SEQS, 1), 0, LENGTH // 4 + 1)
    cuts = jax.random.randint(key_cuts, (SEQS, 4), first_end + 1, LENGTH)
    positions = jnp.arange(LENGTH, dtype=jnp.int32)
    first_part = (positions[None, :] >= first_end).astype(jnp.int32)
    later = jnp.sum((positions[None, :, None] >= cuts[:, None, :]).astype(jnp.int32), axis=-1)
    return (first_part + later).astype(jnp.int32)


def level_of(key, shape, cuts, low, high):
    def one(dim, blocks):
        steps = jax.random.uniform(jax.random.fold_in(jax.random.fold_in(key, 6), dim), (blocks,), jnp.float32, low / len(cuts), high / len(cuts))
        return jnp.repeat(jnp.exp(steps), shape[dim] // blocks).reshape((-1,) + (1,) * (len(shape) - dim - 1))

    level = one(*cuts[0])
    for cut in cuts[1:]:
        level = level * one(*cut)
    return level


def centred(key, shape, width, reach, pieces=(), kind=jnp.bfloat16):
    entries = width * jax.random.normal(key, shape, jnp.float32)
    if pieces:
        entries = entries * level_of(key, shape, pieces, -0.22, 0.18)
    return jnp.clip(entries, -reach, reach).astype(kind)


def setup_inputs(seed: int = 0) -> dict:
    arg_keys = jax.random.split(jax.random.key(seed), 13)
    layer_input = draw_layer_input(jax.random.fold_in(arg_keys[12], 71), 0)
    document_ids = draw_document_ids(jax.random.fold_in(arg_keys[12], 71), 0)
    cotangent = centred(arg_keys[2], (SEQS, LENGTH, D), 1.0, 6.0, ((0, 8), (1, 4)))
    attention_gain = jnp.clip(1.0 + 0.1 * jax.random.normal(arg_keys[3], (D,), jnp.float32), 0.5, 1.5).astype(jnp.bfloat16)
    query_weight = centred(arg_keys[4], (D, D), D ** -0.5, 0.125, ((0, 16),))
    key_weight = centred(arg_keys[5], (D, D), D ** -0.5, 0.125, ((0, 16),))
    value_weight = centred(arg_keys[6], (D, D), D ** -0.5, 0.125, ((0, 16),))
    output_weight = centred(arg_keys[7], (D, D), (D // 8) ** -0.5, 0.375, ((0, 16),))
    feedforward_gain = jnp.clip(1.0 + 0.1 * jax.random.normal(arg_keys[8], (D,), jnp.float32), 0.5, 1.5).astype(jnp.bfloat16)
    gate_weight = centred(arg_keys[9], (D, FF), D ** -0.5, 0.125, ((0, 16),))
    up_weight = centred(arg_keys[10], (D, FF), D ** -0.5, 0.125, ((0, 16),))
    down_weight = centred(arg_keys[11], (FF, D), FF ** -0.5, 0.0625, ((0, 16),))
    return dict(layer_input=layer_input, document_ids=document_ids, cotangent=cotangent, attention_gain=attention_gain, query_weight=query_weight, key_weight=key_weight, value_weight=value_weight, output_weight=output_weight, feedforward_gain=feedforward_gain, gate_weight=gate_weight, up_weight=up_weight, down_weight=down_weight)


@jax.custom_vjp
def low(v):
    return lax.optimization_barrier(v.astype(jnp.bfloat16)).astype(jnp.float32)

@jax.custom_vjp
def low_back(v):
    return v

def low_keep(v):
    return (low(v), None)

def low_pass(kept, grad):
    return (grad,)

def back_keep(v):
    return (v, None)

def back_low(kept, grad):
    return (low(grad),)
low.defvjp(low_keep, low_pass)
low_back.defvjp(back_keep, back_low)
epsilon = 1e-05
rotary_base = 130000.0
masked_score = -1e+30

def matmul(left_side, right_side):
    return jnp.dot(left_side, right_side, precision=lax.Precision.HIGHEST)

def norm_scale(values, gain):
    inverse = lax.rsqrt(lax.optimization_barrier(jnp.mean(values * values, axis=-1, keepdims=True)) + epsilon)
    return values * inverse * gain

def rotation(positions, head_size):
    half_dim = head_size // 2
    frequency = rotary_base ** (-(jnp.arange(half_dim, dtype=jnp.float32) * 2.0) / head_size)
    angles = positions.astype(jnp.float32)[:, None] * frequency[None, :]
    return (jnp.cos(angles), jnp.sin(angles))

def rotate(values, cosine, sine_table):
    half_dim = values.shape[-1] // 2
    front_part = values[..., :half_dim]
    second = values[..., half_dim:]
    cos_wide = cosine[:, None, :]
    sin_wide = sine_table[:, None, :]
    return jnp.concatenate([front_part * cos_wide - second * sin_wide, second * cos_wide + front_part * sin_wide], axis=-1)

def block_forward(params, inputs, allowed, cosine, sine_table):
    attention_gain, query_weight, key_weight, value_weight, output_weight, feedforward_gain, gate_weight, up_weight, down_weight = params
    length = inputs.shape[0]
    normed = low(norm_scale(inputs, attention_gain))
    queries = low(rotate(low_back(matmul(normed, query_weight)).reshape(length, HEADS, HEAD_DIM), cosine, sine_table))
    keys = low(rotate(low_back(matmul(normed, key_weight)).reshape(length, HEADS, HEAD_DIM), cosine, sine_table))
    values = low(low_back(matmul(normed, value_weight))).reshape(length, HEADS, HEAD_DIM)

    def single_head(operands):
        head_query, head_key, head_value = operands
        scores = low_back(matmul(head_query, head_key.T) * 0.125)
        scores = jnp.where(allowed, scores, masked_score)
        row_peak = lax.optimization_barrier(jnp.max(scores, axis=-1, keepdims=True))
        weights = jnp.exp(scores - row_peak)
        softmax_weights = weights / lax.optimization_barrier(jnp.sum(weights, axis=-1, keepdims=True))
        return matmul(low(softmax_weights), head_value)
    attention_out = lax.map(jax.checkpoint(single_head), (queries.transpose(1, 0, 2), keys.transpose(1, 0, 2), values.transpose(1, 0, 2)))
    attended = low(low_back(attention_out.transpose(1, 0, 2).reshape(length, HEADS * HEAD_DIM)))
    hidden = inputs + low_back(matmul(attended, output_weight))
    normed_mlp = low(norm_scale(hidden, feedforward_gain))
    gate_pre = low_back(matmul(normed_mlp, gate_weight))
    upward = low_back(matmul(normed_mlp, up_weight))
    product = low(jax.nn.silu(gate_pre) * upward)
    return hidden + low_back(matmul(product, down_weight))

def reference(layer_input, document_ids, cotangent, attention_gain, query_weight, key_weight, value_weight, output_weight, feedforward_gain, gate_weight, up_weight, down_weight):
    natural = jnp.arange(LENGTH, dtype=jnp.int32)
    block_index = natural // BLOCK
    within = natural % BLOCK
    device = jnp.where(block_index < N_CTX, block_index, 2 * N_CTX - 1 - block_index)
    second_half = (block_index >= N_CTX).astype(jnp.int32)
    stored = (device * TOK_DEV + second_half * BLOCK + within).astype(jnp.int32)
    placed = jnp.arange(LENGTH, dtype=jnp.int32)
    holder = placed // TOK_DEV
    offset = placed % TOK_DEV
    position = jnp.where(offset < BLOCK, holder * BLOCK + offset, (2 * N_CTX - 1 - holder) * BLOCK + offset - BLOCK).astype(jnp.int32)
    params = tuple((weight.astype(jnp.float32) for weight in (attention_gain, query_weight, key_weight, value_weight, output_weight, feedforward_gain, gate_weight, up_weight, down_weight)))
    cosine, sine_table = rotation(natural, HEAD_DIM)

    def per_sequence(totals, operands):
        inputs, documents, upstream = operands
        inputs_nat = jnp.take(inputs, stored, axis=0).astype(jnp.float32)
        upstream_nat = jnp.take(upstream, stored, axis=0).astype(jnp.float32)
        allowed = (natural[None, :] <= natural[:, None]) & (documents[:, None] == documents[None, :])
        outputs, pullback = jax.vjp(lambda weights, values: block_forward(weights, values, allowed, cosine, sine_table), params, inputs_nat)
        weight_grads, inputs_grad = pullback(upstream_nat)
        totals = jax.tree.map(lambda running, gradient: running + gradient, totals, weight_grads)
        return (totals, (jnp.take(outputs, position, axis=0).astype(jnp.bfloat16), jnp.take(inputs_grad, position, axis=0).astype(jnp.bfloat16)))
    start_sums = tuple((jnp.zeros(weight.shape, jnp.float32) for weight in params))
    totals, (layer_output, input_grad) = lax.scan(per_sequence, start_sums, (layer_input, document_ids, cotangent))
    return (layer_output, input_grad, totals[0], totals[1], totals[2], totals[3], totals[4], totals[5], totals[6], totals[7], totals[8])
```

```python
import functools
import math

import jax
import jax.numpy as jnp
from jax import lax
from jax.experimental import pallas as pl
from jax.experimental.pallas import tpu as pltpu
from jax.sharding import Mesh, PartitionSpec as P

HEADS = 32
HEAD_DIM = 64


epsilon = 1e-05
rotary_base = 130000.0
masked_score = -1e30


def norm_scale(values, gain):
    inverse = lax.rsqrt(jnp.mean(values * values, axis=-1, keepdims=True) + epsilon)
    return values * inverse * gain


def rotation(positions, head_size):
    half_dim = head_size // 2
    frequency = rotary_base ** (-(jnp.arange(half_dim, dtype=jnp.float32) * 2.0) / head_size)
    angles = positions.astype(jnp.float32)[:, None] * frequency[None, :]
    return (jnp.cos(angles), jnp.sin(angles))


def rotate(values, cosine, sine_table):
    half_dim = values.shape[-1] // 2
    front_part = values[..., :half_dim]
    second = values[..., half_dim:]
    cos_wide = cosine[:, None, :]
    sin_wide = sine_table[:, None, :]
    return jnp.concatenate(
        [front_part * cos_wide - second * sin_wide, second * cos_wide + front_part * sin_wide],
        axis=-1,
    )


def place_of(holder, offset, block_rows, ctx_count):
    return jnp.where(
        offset < block_rows,
        holder * block_rows + offset,
        (2 * ctx_count - 1 - holder) * block_rows + offset - block_rows,
    )


def per_device(
    layer_input,
    document_ids,
    cotangent,
    attention_gain,
    query_weight,
    key_weight,
    value_weight,
    output_weight,
    feedforward_gain,
    gate_weight,
    up_weight,
    down_weight,
):
    ctx_count = lax.axis_size("ctx")
    device = lax.axis_index("ctx")
    inputs = layer_input[0].astype(jnp.float32)
    upstream = cotangent[0]
    tok_count = inputs.shape[0]
    model_width = inputs.shape[1]
    block_rows = tok_count // 2
    group_heads = math.gcd(8, HEADS)
    group_count = HEADS // group_heads
    group_width = group_heads * HEAD_DIM
    key_count = ctx_count * tok_count
    local_pos = place_of(device, jnp.arange(tok_count, dtype=jnp.int32), block_rows, ctx_count)
    key_index = jnp.arange(key_count, dtype=jnp.int32)
    key_pos = place_of(key_index // tok_count, key_index % tok_count, block_rows, ctx_count)
    documents = document_ids[0]
    same_doc = jnp.take(documents, local_pos)[:, None] == jnp.take(documents, key_pos)[None, :]
    allowed = (key_pos[None, :] <= local_pos[:, None]) & same_doc
    cosine, sine_table = rotation(local_pos, HEAD_DIM)
    attention_set = (
        lax.all_gather(attention_gain, ("ctx", "fsdp"), axis=0, tiled=True),
        lax.all_gather(query_weight, ("ctx", "fsdp"), axis=0, tiled=True),
        lax.all_gather(key_weight, ("ctx", "fsdp"), axis=0, tiled=True),
        lax.all_gather(value_weight, ("ctx", "fsdp"), axis=0, tiled=True),
        lax.all_gather(output_weight, ("ctx", "fsdp"), axis=0, tiled=True),
    )
    attn_gain_full = attention_set[0].astype(jnp.float32)
    normed_low = norm_scale(inputs, attn_gain_full).astype(jnp.bfloat16)
    query_pre = jnp.dot(normed_low, attention_set[1], preferred_element_type=jnp.float32)
    key_pre = jnp.dot(normed_low, attention_set[2], preferred_element_type=jnp.float32)
    value_pre = jnp.dot(normed_low, attention_set[3], preferred_element_type=jnp.float32)
    queries = (
        rotate(query_pre.reshape(tok_count, HEADS, HEAD_DIM), cosine, sine_table)
        .reshape(tok_count, model_width)
        .astype(jnp.bfloat16)
    )
    keys_local = (
        rotate(key_pre.reshape(tok_count, HEADS, HEAD_DIM), cosine, sine_table)
        .reshape(tok_count, model_width)
        .astype(jnp.bfloat16)
    )
    values_local = value_pre.astype(jnp.bfloat16)
    all_keys, all_values = (
        lax.all_gather(keys_local, "ctx", axis=0, tiled=True),
        lax.all_gather(values_local, "ctx", axis=0, tiled=True),
    )

    def group_parts(group_index):
        column_start = group_index * group_width
        query_part = lax.dynamic_slice_in_dim(queries, column_start, group_width, 1).reshape(
            tok_count, group_heads, HEAD_DIM
        )
        key_part = lax.dynamic_slice_in_dim(all_keys, column_start, group_width, 1).reshape(
            key_count, group_heads, HEAD_DIM
        )
        value_part = lax.dynamic_slice_in_dim(all_values, column_start, group_width, 1).reshape(
            key_count, group_heads, HEAD_DIM
        )
        scores = (
            jnp.einsum("qhd,khd->hqk", query_part, key_part, preferred_element_type=jnp.float32)
            * 0.125
        )
        scores = jnp.where(allowed[None], scores, masked_score)
        return (query_part, key_part, value_part, scores)

    def group_forward(group_index):
        query_part, key_part, value_part, scores = group_parts(group_index)
        row_peak = jnp.max(scores, axis=-1, keepdims=True)
        exponent = jnp.exp(scores - row_peak)
        row_total = jnp.sum(exponent, axis=-1, keepdims=True)
        softmax_weights = exponent / row_total
        log_total = row_peak[..., 0] + jnp.log(row_total[..., 0])
        attended = jnp.einsum(
            "hqk,khd->qhd",
            softmax_weights.astype(jnp.bfloat16),
            value_part,
            preferred_element_type=jnp.float32,
        )
        return (attended.reshape(tok_count, group_width), log_total)

    group_index_all = jnp.arange(group_count, dtype=jnp.int32)
    attended_groups, log_totals = lax.map(group_forward, group_index_all)
    attended_low = (
        jnp.transpose(attended_groups, (1, 0, 2))
        .reshape(tok_count, model_width)
        .astype(jnp.bfloat16)
    )
    hidden = inputs + jnp.dot(attended_low, attention_set[4], preferred_element_type=jnp.float32)
    feedforward_set = (
        lax.all_gather(feedforward_gain, ("ctx", "fsdp"), axis=0, tiled=True),
        lax.all_gather(gate_weight, ("ctx", "fsdp"), axis=0, tiled=True),
        lax.all_gather(up_weight, ("ctx", "fsdp"), axis=0, tiled=True),
        lax.all_gather(down_weight, ("ctx", "fsdp"), axis=0, tiled=True),
    )
    mlp_low = norm_scale(hidden, feedforward_set[0].astype(jnp.float32)).astype(jnp.bfloat16)
    gate_pre = jnp.dot(mlp_low, feedforward_set[1], preferred_element_type=jnp.float32)
    up_pre = jnp.dot(mlp_low, feedforward_set[2], preferred_element_type=jnp.float32)
    product_low = (jax.nn.silu(gate_pre) * up_pre).astype(jnp.bfloat16)
    layer_output = (
        hidden + jnp.dot(product_low, feedforward_set[3], preferred_element_type=jnp.float32)
    ).astype(jnp.bfloat16)
    feedforward_back = (
        lax.all_gather(feedforward_gain, ("ctx", "fsdp"), axis=0, tiled=True),
        lax.all_gather(gate_weight, ("ctx", "fsdp"), axis=0, tiled=True),
        lax.all_gather(up_weight, ("ctx", "fsdp"), axis=0, tiled=True),
        lax.all_gather(down_weight, ("ctx", "fsdp"), axis=0, tiled=True),
    )
    attention_back = (
        lax.all_gather(attention_gain, ("ctx", "fsdp"), axis=0, tiled=True),
        lax.all_gather(query_weight, ("ctx", "fsdp"), axis=0, tiled=True),
        lax.all_gather(key_weight, ("ctx", "fsdp"), axis=0, tiled=True),
        lax.all_gather(value_weight, ("ctx", "fsdp"), axis=0, tiled=True),
        lax.all_gather(output_weight, ("ctx", "fsdp"), axis=0, tiled=True),
    )
    piece = product_low
    down_shard = lax.psum_scatter(
        jnp.einsum("tf,td->fd", piece, upstream, preferred_element_type=jnp.float32),
        ("ctx", "fsdp"),
        scatter_dimension=0,
        tiled=True,
    )
    product_grad = jnp.einsum(
        "td,fd->tf", upstream, feedforward_back[3], preferred_element_type=jnp.float32
    )
    silu_out, silu_pullback = jax.vjp(
        lambda gate_in, up_in: jax.nn.silu(gate_in) * up_in, gate_pre, up_pre
    )
    gate_grad, up_grad = silu_pullback(product_grad)
    gate_grad_low = gate_grad.astype(jnp.bfloat16)
    up_grad_low = up_grad.astype(jnp.bfloat16)
    joined_grads = jnp.concatenate([gate_grad_low, up_grad_low], axis=1)
    piece = mlp_low
    joined_shard = lax.psum_scatter(
        jnp.einsum("td,tf->df", piece, joined_grads, preferred_element_type=jnp.float32),
        ("ctx", "fsdp"),
        scatter_dimension=0,
        tiled=True,
    )
    ff_width = gate_weight.shape[1]
    gate_shard = joined_shard[:, :ff_width]
    up_shard = joined_shard[:, ff_width:]
    mlp_normed_grad = jnp.einsum(
        "tf,df->td", gate_grad_low, feedforward_back[1], preferred_element_type=jnp.float32
    )
    mlp_normed_grad = mlp_normed_grad + jnp.einsum(
        "tf,df->td", up_grad_low, feedforward_back[2], preferred_element_type=jnp.float32
    )
    mlp_norm_out, mlp_norm_pullback = jax.vjp(
        norm_scale, hidden, feedforward_back[0].astype(jnp.float32)
    )
    hidden_from_norm, ff_gain_term = mlp_norm_pullback(mlp_normed_grad)
    hidden_grad = upstream.astype(jnp.float32) + hidden_from_norm
    hidden_low = hidden_grad.astype(jnp.bfloat16)
    output_term = jnp.einsum(
        "td,te->de", attended_low, hidden_low, preferred_element_type=jnp.float32
    )
    attended_grad_low = jnp.einsum(
        "te,de->td", hidden_low, attention_back[4], preferred_element_type=jnp.float32
    ).astype(jnp.bfloat16)

    def group_backward(operands):
        group_index, log_total = operands
        query_part, key_part, value_part, scores = group_parts(group_index)
        softmax_weights = jnp.exp(scores - log_total[:, :, None])
        column_start = group_index * group_width
        grad_part = lax.dynamic_slice_in_dim(
            attended_grad_low, column_start, group_width, 1
        ).reshape(tok_count, group_heads, HEAD_DIM)
        value_grad = jnp.einsum(
            "hqk,qhd->khd",
            softmax_weights.astype(jnp.bfloat16),
            grad_part,
            preferred_element_type=jnp.float32,
        )
        weight_grad = jnp.einsum(
            "qhd,khd->hqk", grad_part, value_part, preferred_element_type=jnp.float32
        )
        row_inner = jnp.sum(weight_grad * softmax_weights, axis=-1, keepdims=True)
        score_grad = (softmax_weights * (weight_grad - row_inner)).astype(jnp.bfloat16)
        query_grad = (
            jnp.einsum("hqk,khd->qhd", score_grad, key_part, preferred_element_type=jnp.float32)
            * 0.125
        )
        key_grad = (
            jnp.einsum("hqk,qhd->khd", score_grad, query_part, preferred_element_type=jnp.float32)
            * 0.125
        )
        return (
            query_grad.reshape(tok_count, group_width),
            key_grad.reshape(key_count, group_width),
            value_grad.reshape(key_count, group_width),
        )

    query_groups, key_groups, value_groups = lax.map(group_backward, (group_index_all, log_totals))
    query_grad_all = jnp.transpose(query_groups, (1, 0, 2)).reshape(tok_count, model_width)
    key_grad_all = jnp.transpose(key_groups, (1, 0, 2)).reshape(key_count, model_width)
    value_grad_all = jnp.transpose(value_groups, (1, 0, 2)).reshape(key_count, model_width)
    key_grad_local, value_grad_local = (
        lax.psum_scatter(
            key_grad_all.astype(jnp.bfloat16), "ctx", scatter_dimension=0, tiled=True
        ).astype(jnp.float32),
        lax.psum_scatter(
            value_grad_all.astype(jnp.bfloat16), "ctx", scatter_dimension=0, tiled=True
        ).astype(jnp.float32),
    )
    negative_sine = -sine_table
    query_pre_grad = (
        rotate(query_grad_all.reshape(tok_count, HEADS, HEAD_DIM), cosine, negative_sine)
        .reshape(tok_count, model_width)
        .astype(jnp.bfloat16)
    )
    key_pre_grad = (
        rotate(key_grad_local.reshape(tok_count, HEADS, HEAD_DIM), cosine, negative_sine)
        .reshape(tok_count, model_width)
        .astype(jnp.bfloat16)
    )
    value_pre_grad = value_grad_local.astype(jnp.bfloat16)
    query_term = jnp.einsum(
        "td,te->de", normed_low, query_pre_grad, preferred_element_type=jnp.float32
    )
    key_term = jnp.einsum("td,te->de", normed_low, key_pre_grad, preferred_element_type=jnp.float32)
    value_term = jnp.einsum(
        "td,te->de", normed_low, value_pre_grad, preferred_element_type=jnp.float32
    )
    attn_normed_grad = jnp.einsum(
        "te,de->td", query_pre_grad, attention_back[1], preferred_element_type=jnp.float32
    )
    attn_normed_grad = attn_normed_grad + jnp.einsum(
        "te,de->td", key_pre_grad, attention_back[2], preferred_element_type=jnp.float32
    )
    attn_normed_grad = attn_normed_grad + jnp.einsum(
        "te,de->td", value_pre_grad, attention_back[3], preferred_element_type=jnp.float32
    )
    attn_norm_out, attn_norm_pullback = jax.vjp(
        norm_scale, inputs, attention_back[0].astype(jnp.float32)
    )
    inputs_from_norm, attn_gain_term = attn_norm_pullback(attn_normed_grad)
    input_grad = (hidden_grad + inputs_from_norm).astype(jnp.bfloat16)
    attn_shards = (
        lax.psum_scatter(attn_gain_term, ("ctx", "fsdp"), scatter_dimension=0, tiled=True),
        lax.psum_scatter(ff_gain_term, ("ctx", "fsdp"), scatter_dimension=0, tiled=True),
        lax.psum_scatter(query_term, ("ctx", "fsdp"), scatter_dimension=0, tiled=True),
        lax.psum_scatter(key_term, ("ctx", "fsdp"), scatter_dimension=0, tiled=True),
        lax.psum_scatter(value_term, ("ctx", "fsdp"), scatter_dimension=0, tiled=True),
        lax.psum_scatter(output_term, ("ctx", "fsdp"), scatter_dimension=0, tiled=True),
    )
    summed = (
        lax.psum(attn_shards[0].astype(jnp.bfloat16), "seq").astype(jnp.float32),
        lax.psum(attn_shards[2].astype(jnp.bfloat16), "seq").astype(jnp.float32),
        lax.psum(attn_shards[3].astype(jnp.bfloat16), "seq").astype(jnp.float32),
        lax.psum(attn_shards[4].astype(jnp.bfloat16), "seq").astype(jnp.float32),
        lax.psum(attn_shards[5].astype(jnp.bfloat16), "seq").astype(jnp.float32),
        lax.psum(attn_shards[1].astype(jnp.bfloat16), "seq").astype(jnp.float32),
        lax.psum(gate_shard.astype(jnp.bfloat16), "seq").astype(jnp.float32),
        lax.psum(up_shard.astype(jnp.bfloat16), "seq").astype(jnp.float32),
        lax.psum(down_shard.astype(jnp.bfloat16), "seq").astype(jnp.float32),
    )
    return (
        layer_output[None],
        input_grad[None],
        summed[0],
        summed[1],
        summed[2],
        summed[3],
        summed[4],
        summed[5],
        summed[6],
        summed[7],
        summed[8],
    )


def gathered(mesh):
    return jax.shard_map(
        per_device,
        mesh=mesh,
        in_specs=(
            P(("seq", "fsdp"), "ctx", None),
            P(("seq", "fsdp"), None),
            P(("seq", "fsdp"), "ctx", None),
            P(("ctx", "fsdp")),
            P(("ctx", "fsdp"), None),
            P(("ctx", "fsdp"), None),
            P(("ctx", "fsdp"), None),
            P(("ctx", "fsdp"), None),
            P(("ctx", "fsdp")),
            P(("ctx", "fsdp"), None),
            P(("ctx", "fsdp"), None),
            P(("ctx", "fsdp"), None),
        ),
        out_specs=(
            P(("seq", "fsdp"), "ctx", None),
            P(("seq", "fsdp"), "ctx", None),
            P(("ctx", "fsdp")),
            P(("ctx", "fsdp"), None),
            P(("ctx", "fsdp"), None),
            P(("ctx", "fsdp"), None),
            P(("ctx", "fsdp"), None),
            P(("ctx", "fsdp")),
            P(("ctx", "fsdp"), None),
            P(("ctx", "fsdp"), None),
            P(("ctx", "fsdp"), None),
        ),
        check_vma=False,
    )


BIG = pltpu.CompilerParams(vmem_limit_bytes=56 * 1024 * 1024)
BF16 = jnp.bfloat16
F32 = jnp.float32


def swap(value, axis):
    return lax.ppermute(value, axis, [(0, 1), (1, 0)])


def swap_both(value, first, second):
    return lax.ppermute(value, (first, second), [(0, 3), (1, 2), (2, 1), (3, 0)])


def after(value, *earlier):
    return lax.optimization_barrier((value, *earlier))[0]


def gather_square(block):
    half = block.shape[0] // 2
    along_x = swap(block, "x")
    along_seq = swap(block, "seq")
    upper = swap(along_seq[:half], "x")
    lower = swap(along_x[half:], "seq")
    return [block, along_x, along_seq, jnp.concatenate([upper, lower], axis=0)]


def gather_blocks(block):
    across = swap(block, "zl")
    return gather_square(block) + gather_square(across)


def add_low(first, *others):
    total = first.astype(F32)
    for other in others:
        total = total + other.astype(F32)
    return total


def scatter_square(own, to_x, to_seq, opposite):
    half = own.shape[0] // 2
    by_x = swap(opposite[:half], "x")
    by_seq = swap(opposite[half:], "seq")
    to_seq = jnp.concatenate([add_low(to_seq[:half], by_x).astype(BF16), to_seq[half:]], axis=0)
    to_x = jnp.concatenate([to_x[:half], add_low(to_x[half:], by_seq).astype(BF16)], axis=0)
    return add_low(own, swap(to_x, "x"), swap(to_seq, "seq"))


def scatter_blocks(terms):
    blocks = [terms[i * (terms.shape[0] // 8) : (i + 1) * (terms.shape[0] // 8)] for i in range(8)]
    across = scatter_square(*blocks[4:]).astype(BF16)
    near = scatter_square(*blocks[:4])
    return near + swap(across, "zl").astype(F32)


def copies_kernel(plan, table_ref, *refs):
    sources, target, sems = refs[:-2], refs[-2], refs[-1]
    copies = []
    for i, (source, from_index, to_index) in enumerate(plan):
        copy = pltpu.make_async_copy(
            sources[source].at[from_index(table_ref)], target.at[to_index(table_ref)], sems.at[i]
        )
        copy.start()
        copies.append(copy)
    for copy in copies:
        copy.wait()


def copies(plan, table, out_shape, *sources):
    moved = 2 * math.prod(out_shape) * 2
    return pl.pallas_call(
        functools.partial(copies_kernel, plan),
        out_shape=jax.ShapeDtypeStruct(out_shape, BF16),
        in_specs=[pl.BlockSpec(memory_space=pltpu.SMEM)] + [pl.BlockSpec(memory_space=pl.ANY)] * len(sources),
        out_specs=pl.BlockSpec(memory_space=pl.ANY),
        scratch_shapes=[pltpu.SemaphoreType.DMA((len(plan),))],
        cost_estimate=pl.CostEstimate(flops=0, bytes_accessed=moved, transcendentals=0),
        name="place_blocks",
    )(table, *sources)


class Place:
    def __init__(self):
        self.seq = lax.axis_index("seq")
        self.x = lax.axis_index("x")
        self.core = lax.axis_index("core")
        self.zh = lax.axis_index("zh")
        self.zl = lax.axis_index("zl")

    def block(self, x, core, zh, zl):
        return ((x * 2 + core) * 2 + zh) * 2 + zl


def column_slices(place, weights, width):
    rows = weights[0].shape[0]
    table = jnp.stack(
        [
            place.block(place.x ^ dx, core, place.seq, place.zl ^ dz)
            for dx in range(2)
            for dz in range(2)
            for core in range(2)
        ]
    ).astype(jnp.int32)
    plan = []
    for target in range(4):
        for w in range(len(weights)):
            for core in range(2):

                def from_index(ref, entry=target * 2 + core):
                    return (slice(None), pl.ds(pl.multiple_of(ref[entry] * width, width), width))

                def to_index(ref, target=target, start=(w * 2 + core) * width):
                    return (target, slice(None), pl.ds(start, width))

                plan.append((w, from_index, to_index))
    return copies(plan, table, (4, rows, 2 * width * len(weights)), *weights)


def chip_columns(place, weights, width):
    slices = column_slices(place, weights, width)
    near = jnp.stack(
        [slices[0], swap(slices[1], "zl"), swap(slices[2], "x"), swap_both(slices[3], "x", "zl")]
    )
    far = swap(near, "zh")
    near_other = swap(near, "core")
    far_other = swap(far, "core")
    table = jnp.stack(
        [
            place.block(place.x ^ dx, place.core ^ dc, place.zh ^ dh, place.zl ^ dz)
            for dc in range(2)
            for dh in range(2)
            for dx in range(2)
            for dz in range(2)
        ]
    ).astype(jnp.int32)
    plan = []
    for part in range(4):
        for i in range(4):

            def from_index(ref, i=i):
                return (i,)

            def to_index(ref, entry=part * 4 + i):
                return (ref[entry],)

            plan.append((part, from_index, to_index))
    rows, wide = near.shape[1:]
    whole = copies(plan, table, (16, rows, wide), near, far, near_other, far_other)
    return whole.reshape(16 * rows, wide)


def chip_rows(place, weight):
    moved = lax.ppermute(weight, ("seq", "zh"), [(0, 1), (3, 2)])
    own = jnp.where(place.zh == place.seq, weight, moved)
    other = swap(own, "core")
    first = place.core == 0
    return jnp.concatenate([jnp.where(first, own, other), jnp.where(first, other, own)], axis=0)


def sum_rows(place, terms):
    rows = terms.shape[0] // 2
    parts = terms.reshape(2, rows, terms.shape[1])
    received = swap(lax.dynamic_index_in_dim(parts, 1 - place.core, 0, False), "core")
    own = add_low(lax.dynamic_index_in_dim(parts, place.core, 0, False), received)
    far = lax.ppermute(own.astype(BF16), ("seq", "zh"), [(1, 0), (2, 3)])
    total = (own + far.astype(F32)).astype(BF16)
    copied = lax.ppermute(total, ("seq", "zh"), [(0, 2), (3, 1)])
    return jnp.where(place.zh == place.seq, total, copied).astype(F32)


def sum_columns(place, terms):
    rows, wide = terms.shape[0] // 16, terms.shape[1]
    parts = terms.reshape(2, 2, 2, 2, rows, wide)
    received = swap(lax.dynamic_index_in_dim(parts, 1 - place.core, 1, False), "core")
    own = add_low(lax.dynamic_index_in_dim(parts, place.core, 1, False), received).astype(BF16)
    received = swap(lax.dynamic_index_in_dim(own, 1 - place.zh, 1, False), "zh")
    own = add_low(lax.dynamic_index_in_dim(own, place.zh, 1, False), received).astype(BF16)

    def piece(dx, dz):
        return lax.dynamic_slice(own, (place.x ^ dx, place.zl ^ dz, 0, 0), (1, 1, rows, wide))[0, 0]

    near = jnp.stack(
        [piece(0, 0), swap(piece(0, 1), "zl"), swap(piece(1, 0), "x"), swap_both(piece(1, 1), "x", "zl")]
    )
    return near, swap(near, "seq")


def finish_kernel(count, choice_ref, dy_ref, *refs):
    near, far, weights, outs = refs[: 2 * count][0::2], refs[: 2 * count][1::2], refs[2 * count : 3 * count], refs[3 * count :]
    j = pl.program_id(0)
    use_near = dy_ref[j] == 0
    total = None
    for i in range(count):
        grad = jnp.where(use_near, near[i][0].astype(F32), far[i][0].astype(F32))
        outs[i][...] = grad
        term = grad * weights[i][...].astype(F32)
        total = term if total is None else total + term

    @pl.when(j == 0)
    def _():
        outs[count][...] = jnp.zeros_like(outs[count])

    outs[count][...] += total


def finish_columns(place, near, far, weights, width):
    count, rows = len(weights), weights[0].shape[0]
    chips, picks = [], []
    for x in range(2):
        for core in range(2):
            for zh in range(2):
                for zl in range(2):
                    chips.append((place.x ^ x) * 2 + (place.zl ^ zl))
                    picks.append(place.seq ^ zh)
    choice = jnp.stack(chips).astype(jnp.int32)
    pick = jnp.stack(picks).astype(jnp.int32)

    def piece_spec(w):
        return pl.BlockSpec((1, rows, width), lambda j, choice, pick: (choice[j], 0, 2 * w + (j // 4) % 2))

    column_spec = pl.BlockSpec((rows, width), lambda j, choice, pick: (0, j))
    in_specs, operands = [], []
    for w in range(count):
        in_specs += [piece_spec(w), piece_spec(w)]
        operands += [near, far]
    outs = pl.pallas_call(
        functools.partial(finish_kernel, count),
        grid_spec=pltpu.PrefetchScalarGridSpec(
            num_scalar_prefetch=2,
            grid=(16,),
            in_specs=in_specs + [column_spec] * count,
            out_specs=[column_spec] * count + [pl.BlockSpec((rows, width), lambda j, choice, pick: (0, 0))],
        ),
        out_shape=[jax.ShapeDtypeStruct((rows, 16 * width), F32)] * count + [jax.ShapeDtypeStruct((rows, width), F32)],
        compiler_params=BIG,
        cost_estimate=pl.CostEstimate(flops=0, bytes_accessed=12 * count * rows * 16 * width, transcendentals=0),
        name="finish_columns",
    )(choice, pick, *operands, *weights)
    return outs[:count], jnp.sum(outs[count], axis=1)


def turn(value, cosine, sine):
    lane = lax.broadcasted_iota(jnp.int32, value.shape, 1)
    partner = jnp.where(lane % HEAD_DIM < HEAD_DIM // 2, pltpu.roll(value, 96, 1), pltpu.roll(value, 32, 1))
    return value * cosine + partner * sine


def project_kernel(x_ref, w_ref, gain_ref, cos_ref, sin_ref, a_ref, q_ref, k_ref, v_ref):
    x = x_ref[...].astype(F32)
    inverse = lax.rsqrt(jnp.mean(x * x, axis=-1, keepdims=True) + epsilon)
    a = (x * inverse * gain_ref[...].astype(F32)).astype(BF16)
    a_ref[...] = a
    joined = jnp.dot(a, w_ref[...], preferred_element_type=F32)
    wide = q_ref.shape[1]
    cosine, sine = cos_ref[...], sin_ref[...]
    for i in range(wide // 128):
        at = slice(i * 128, (i + 1) * 128)
        q_ref[:, at] = turn(joined[:, at], cosine, sine).astype(BF16)
        k_ref[:, at] = turn(joined[:, wide + i * 128 : wide + (i + 1) * 128], cosine, sine).astype(BF16)
    v_ref[...] = joined[:, 2 * wide :].astype(BF16)


def project(x_all, weight, gain, cosine, sine):
    tokens, model = x_all.shape
    wide = weight.shape[1] // 3
    tile = cosine.shape[0]
    whole = lambda shape: pl.BlockSpec(shape, lambda i: (0, 0))
    by_tile = lambda columns: pl.BlockSpec((tile, columns), lambda i: (i, 0))
    return pl.pallas_call(
        project_kernel,
        grid=(tokens // tile,),
        in_specs=[by_tile(model), whole(weight.shape), whole((1, model)), whole(cosine.shape), whole(sine.shape)],
        out_specs=[by_tile(model), by_tile(wide), by_tile(wide), by_tile(wide)],
        out_shape=[jax.ShapeDtypeStruct((tokens, model), BF16)] + [jax.ShapeDtypeStruct((tokens, wide), BF16)] * 3,
        compiler_params=BIG,
        cost_estimate=pl.CostEstimate(
            flops=2 * tokens * model * 3 * wide, bytes_accessed=4 * tokens * model, transcendentals=0
        ),
        name="norm_project",
    )(x_all, weight, gain, cosine, sine)


def head_lanes(value, odd):
    lane = lax.broadcasted_iota(jnp.int32, value.shape, 1)
    return jnp.where((lane >= HEAD_DIM) == odd, value, jnp.zeros_like(value))


def probabilities(query, key, mask):
    scores = lax.dot_general(query, key, (((1,), (1,)), ((), ())), preferred_element_type=F32) * 0.125
    scores = jnp.where(mask, scores, masked_score)
    weights = jnp.exp(scores - jnp.max(scores, axis=-1, keepdims=True))
    return weights * (1.0 / jnp.sum(weights, axis=-1, keepdims=True))


def allowed_keys(qpos_ref, start_ref, kpos_ref):
    kpos = kpos_ref[...]
    return (kpos <= qpos_ref[...]) & (kpos >= start_ref[0])


def attend_kernel(q_ref, k_ref, k2_ref, v_ref, v2_ref, qpos_ref, start_ref, kpos_ref, o_ref):
    mask = allowed_keys(qpos_ref, start_ref, kpos_ref)
    for pair in range(q_ref.shape[1] // 128):
        at = slice(pair * 128, (pair + 1) * 128)
        query = q_ref[:, at]
        key = jnp.concatenate([k_ref[:, at], k2_ref[:, at]], axis=0)
        value = jnp.concatenate([v_ref[:, at], v2_ref[:, at]], axis=0)
        total = None
        for odd in (False, True):
            weights = probabilities(head_lanes(query, odd), key, mask).astype(BF16)
            term = jnp.dot(weights, head_lanes(value, odd), preferred_element_type=F32)
            total = term if total is None else total + term
        o_ref[:, at] = total.astype(BF16)


def attend_back_kernel(
    q_ref, k_ref, k2_ref, v_ref, v2_ref, do_ref, qpos_ref, start_ref, kpos_ref, cos_ref, sin_ref,
    dq_ref, dk_ref, dk2_ref, dv_ref, dv2_ref,
):
    mask = allowed_keys(qpos_ref, start_ref, kpos_ref)
    rows = q_ref.shape[0]
    for pair in range(q_ref.shape[1] // 128):
        at = slice(pair * 128, (pair + 1) * 128)
        query, grad = q_ref[:, at], do_ref[:, at]
        key = jnp.concatenate([k_ref[:, at], k2_ref[:, at]], axis=0)
        value = jnp.concatenate([v_ref[:, at], v2_ref[:, at]], axis=0)
        dq = dk = dv = 0.0
        for odd in (False, True):
            query_one, grad_one = head_lanes(query, odd), head_lanes(grad, odd)
            weights = probabilities(query_one, key, mask)
            dp = lax.dot_general(grad_one, value, (((1,), (1,)), ((), ())), preferred_element_type=F32)
            inner = jnp.sum(dp * weights, axis=-1, keepdims=True)
            ds = (weights * (dp - inner)).astype(BF16)
            low = weights.astype(BF16)
            dq = dq + jnp.dot(ds, head_lanes(key, odd), preferred_element_type=F32)
            dk = dk + lax.dot_general(ds, query_one, (((0,), (0,)), ((), ())), preferred_element_type=F32)
            dv = dv + lax.dot_general(low, grad_one, (((0,), (0,)), ((), ())), preferred_element_type=F32)
        dq_ref[:, at] = turn(dq * 0.125, cos_ref[...], -sin_ref[...]).astype(BF16)
        dk_ref[:, at] = dk[:rows] * 0.125
        dk2_ref[:, at] = (dk[rows:] * 0.125).astype(BF16)
        dv_ref[:, at] = dv[:rows]
        dv2_ref[:, at] = dv[rows:].astype(BF16)


def join_kernel(dq_ref, dk_ref, dk2_ref, dv_ref, dv2_ref, cos_ref, sin_ref, out_ref):
    wide = dq_ref.shape[1]
    out_ref[:, :wide] = dq_ref[...]
    for i in range(wide // 128):
        at = slice(i * 128, (i + 1) * 128)
        dk = dk_ref[:, at] + dk2_ref[:, at].astype(F32)
        out_ref[:, wide + i * 128 : wide + (i + 1) * 128] = turn(dk, cos_ref[...], -sin_ref[...]).astype(BF16)
    out_ref[:, 2 * wide :] = (dv_ref[...] + dv2_ref[...].astype(F32)).astype(BF16)


def by_sequence(kernel, name, operands, outs, flops):
    rows = next(a.shape[0] for a, kind in operands if kind == "rows") // 4

    def spec(shape, kind):
        if kind == "rows":
            return pl.BlockSpec((rows, shape[1]), lambda i: (i, 0))
        if kind == "one":
            return pl.BlockSpec((1,) + shape[1:], lambda i: (i,) + (0,) * (len(shape) - 1))
        return pl.BlockSpec(shape, lambda i: (0,) * len(shape))

    return pl.pallas_call(
        kernel,
        grid=(4,),
        in_specs=[spec(a.shape, kind) for a, kind in operands],
        out_specs=[spec(s.shape, "rows") for s in outs],
        out_shape=outs,
        compiler_params=BIG,
        cost_estimate=pl.CostEstimate(flops=flops, bytes_accessed=8_000_000, transcendentals=0),
        name=name,
    )(*[a for a, _ in operands])


def hidden_kernel(b_ref, dy_ref, w_ref, down_ref, z_ref, d_ref):
    width = z_ref.shape[1]
    chunk = math.gcd(width, 512)
    b, dy = b_ref[...], dy_ref[...]
    for i in range(width // chunk):
        at = slice(i * chunk, (i + 1) * chunk)
        up_at = slice(width + i * chunk, width + (i + 1) * chunk)
        gate = jnp.dot(b, w_ref[:, at], preferred_element_type=F32)
        up = jnp.dot(b, w_ref[:, up_at], preferred_element_type=F32)
        dz = lax.dot_general(dy, down_ref[at, :], (((1,), (1,)), ((), ())), preferred_element_type=F32)
        sig = jax.nn.sigmoid(gate)
        silu = gate * sig
        z_ref[:, at] = (silu * up).astype(BF16)
        d_ref[:, at] = (dz * up * sig * (1.0 + gate * (1.0 - sig))).astype(BF16)
        d_ref[:, up_at] = (dz * silu).astype(BF16)


def hidden_units(b_all, dy_all, weight, down):
    tokens, model = b_all.shape
    width = down.shape[0]
    tile = math.gcd(tokens, 256)
    whole = lambda shape: pl.BlockSpec(shape, lambda i: (0, 0))
    by_tile = lambda columns: pl.BlockSpec((tile, columns), lambda i: (i, 0))
    return pl.pallas_call(
        hidden_kernel,
        grid=(tokens // tile,),
        in_specs=[by_tile(model), by_tile(model), whole(weight.shape), whole(down.shape)],
        out_specs=[by_tile(width), by_tile(2 * width)],
        out_shape=[jax.ShapeDtypeStruct((tokens, width), BF16), jax.ShapeDtypeStruct((tokens, 2 * width), BF16)],
        compiler_params=BIG,
        cost_estimate=pl.CostEstimate(
            flops=6 * tokens * model * width, bytes_accessed=8 * tokens * model, transcendentals=0
        ),
        name="hidden_units",
    )(b_all, dy_all, weight, down)


def norm_back(values, grad, gain):
    inverse = lax.rsqrt(jnp.mean(values * values, axis=-1, keepdims=True) + epsilon)
    normed = values * inverse
    scaled = grad * gain
    return inverse * (scaled - normed * jnp.mean(scaled * normed, axis=-1, keepdims=True))


def dot_low(left, right, left_dim, right_dim):
    return lax.dot_general(
        left, right, (((left_dim,), (right_dim,)), ((), ())), preferred_element_type=F32
    ).astype(BF16)


def paired_device(
    layer_input, document_ids, cotangent, attention_gain, query_weight, key_weight, value_weight, output_weight,
    feedforward_gain, gate_weight, up_weight, down_weight,
):
    place = Place()
    x_own, dy_own = layer_input[0], cotangent[0]
    tok_count, model = x_own.shape
    block_rows = tok_count // 2
    length = document_ids.shape[1]
    block_count = length // block_rows
    rows = query_weight.shape[0]
    hidden_rows = down_weight.shape[0]

    def positions(dx, dc):
        holder = (place.x ^ dx) * 2 + (place.core ^ dc)
        return place_of(holder, jnp.arange(tok_count, dtype=jnp.int32), block_rows, block_count // 2)

    qpos = jnp.concatenate([positions(0, 0), positions(1, 0)])
    kpos = jnp.concatenate([positions(0, 0), positions(1, 0), positions(0, 1), positions(1, 1)])
    cosine, sine = rotation(qpos, HEAD_DIM)
    cosine = jnp.concatenate([cosine] * 4, axis=1)
    sine = jnp.concatenate([-sine, sine] * 2, axis=1)
    documents = document_ids[0]
    first = jnp.sum((documents[None, :] < documents[:, None]).astype(jnp.int32), axis=1)
    firsts = jnp.stack([first, swap(first, "seq")])
    firsts = jnp.concatenate([firsts, swap(firsts, "zl")]).reshape(4, block_count, block_rows)
    starts = []
    for dx in range(2):
        holder = (place.x ^ dx) * 2 + place.core
        for index in (holder, block_count - 1 - holder):
            starts.append(lax.dynamic_index_in_dim(firsts, index, 1, False))
    start = jnp.concatenate(starts, axis=1)[:, :, None]
    qpos, kpos = qpos[:, None], kpos[None, :]

    gains = lax.all_gather(
        jnp.stack([attention_gain, feedforward_gain]), ("x", "core", "zh", "zl"), axis=1, tiled=True
    )
    attn_gain, ff_gain = gains[:1], gains[1:].astype(F32)

    qkv_weight = chip_columns(place, [query_weight, key_weight, value_weight], rows)
    x_all = jnp.concatenate(gather_blocks(x_own), axis=0)
    x_all = after(x_all, qkv_weight)
    gate_weight, up_weight, down_weight, output_weight, dy_start, _ = lax.optimization_barrier(
        (gate_weight, up_weight, down_weight, output_weight, dy_own, x_all)
    )
    out_rows = chip_rows(place, output_weight)
    gate_up = chip_columns(place, [gate_weight, up_weight], hidden_rows)
    down_rows = chip_rows(place, down_weight)
    dy_all = jnp.concatenate(gather_blocks(dy_start), axis=0)

    a_all, q_all, k_all, v_all = project(x_all, qkv_weight, attn_gain, cosine, sine)
    k_other, v_other = swap(k_all, "core"), swap(v_all, "core")
    common = [(q_all, "rows"), (k_all, "rows"), (k_other, "rows"), (v_all, "rows"), (v_other, "rows")]
    where = [(qpos, "whole"), (start, "one"), (kpos, "whole")]
    token_total = q_all.shape[0]
    wide = q_all.shape[1]
    score_flops = 2 * token_total * length * wide
    (o_all,) = by_sequence(
        attend_kernel, "attend", common + where, [jax.ShapeDtypeStruct((token_total, wide), BF16)], 2 * score_flops
    )
    hidden = x_own.astype(F32) + scatter_blocks(dot_low(o_all, out_rows, 1, 0))
    inverse = lax.rsqrt(jnp.mean(hidden * hidden, axis=-1, keepdims=True) + epsilon)
    b_own = (hidden * inverse * ff_gain).astype(BF16)
    b_all = jnp.concatenate(gather_blocks(b_own), axis=0)

    z_all, d_all = hidden_units(b_all, dy_all, gate_up, down_rows)
    db = scatter_blocks(dot_low(d_all, gate_up, 1, 1))
    z_late = after(z_all, db)
    layer_output = (hidden + scatter_blocks(dot_low(z_late, down_rows, 1, 0))).astype(BF16)
    dh = dy_own.astype(F32) + norm_back(hidden, db, ff_gain)
    dh_all = jnp.concatenate(gather_blocks(dh.astype(BF16)), axis=0)

    gate_up_near, gate_up_far = sum_columns(place, dot_low(b_all, d_all, 0, 0))
    (gate_grad, up_grad), ff_sum = finish_columns(
        place, gate_up_near, gate_up_far, [gate_weight, up_weight], hidden_rows
    )
    down_grad = sum_rows(place, dot_low(z_all, dy_all, 0, 0))
    output_grad = sum_rows(place, dot_low(o_all, dh_all, 0, 0))

    do_all = dot_low(dh_all, out_rows, 1, 1)
    low = jax.ShapeDtypeStruct((token_total, wide), BF16)
    high = jax.ShapeDtypeStruct((token_total, wide), F32)
    tables = [(cosine, "whole"), (sine, "whole")]
    dq, dk, dk_other, dv, dv_other = by_sequence(
        attend_back_kernel, "attend_back", common + [(do_all, "rows")] + where + tables,
        [low, high, low, high, low], 5 * score_flops,
    )
    dk_other, dv_other = swap(dk_other, "core"), swap(dv_other, "core")
    (d_qkv,) = by_sequence(
        join_kernel, "join_grads",
        [(dq, "rows"), (dk, "rows"), (dk_other, "rows"), (dv, "rows"), (dv_other, "rows")] + tables,
        [jax.ShapeDtypeStruct((token_total, 3 * wide), BF16)], 0,
    )
    da = scatter_blocks(dot_low(d_qkv, qkv_weight, 1, 1))
    qkv_near, qkv_far = sum_columns(place, dot_low(a_all, d_qkv, 0, 0))
    (query_grad, key_grad, value_grad), attn_sum = finish_columns(
        place, qkv_near, qkv_far, [query_weight, key_weight, value_weight], rows
    )
    input_grad = (dh + norm_back(x_own.astype(F32), da, attn_gain.astype(F32))).astype(BF16)
    attn_gain_grad = attn_sum / attention_gain.astype(F32)
    ff_gain_grad = ff_sum / feedforward_gain.astype(F32)
    return (
        layer_output[None], input_grad[None], attn_gain_grad, query_grad, key_grad, value_grad, output_grad,
        ff_gain_grad, gate_grad, up_grad, down_grad,
    )


def paired(mesh):
    fine = Mesh(mesh.devices.reshape(2, 2, 2, 2, 2), ("seq", "x", "core", "zh", "zl"))
    tokens = P(("seq", "zh", "zl"), ("x", "core"), None)
    matrix, vector = P(("x", "core", "zh", "zl"), None), P(("x", "core", "zh", "zl"))
    return jax.shard_map(
        paired_device,
        mesh=fine,
        in_specs=(tokens, P(("seq", "zh", "zl"), None), tokens, vector) + (matrix,) * 4 + (vector,) + (matrix,) * 3,
        out_specs=(tokens, tokens, vector) + (matrix,) * 4 + (vector,) + (matrix,) * 3,
        check_vma=False,
    )


def solution(mesh):
    if tuple(mesh.shape[axis] for axis in ("seq", "ctx", "fsdp")) == (2, 4, 4):
        return paired(mesh)
    return gathered(mesh)
```

```python
import functools
import math

import jax
import jax.numpy as jnp
from jax import lax
from jax.experimental import pallas as pl
from jax.experimental.pallas import tpu as pltpu
from jax.sharding import Mesh, PartitionSpec as P

HEADS = 32
HEAD_DIM = 64


epsilon = 1e-05
rotary_base = 130000.0
masked_score = -1e30


def norm_scale(values, gain):
    inverse = lax.rsqrt(jnp.mean(values * values, axis=-1, keepdims=True) + epsilon)
    return values * inverse * gain


def rotation(positions, head_size):
    half_dim = head_size // 2
    frequency = rotary_base ** (-(jnp.arange(half_dim, dtype=jnp.float32) * 2.0) / head_size)
    angles = positions.astype(jnp.float32)[:, None] * frequency[None, :]
    return (jnp.cos(angles), jnp.sin(angles))


def rotate(values, cosine, sine_table):
    half_dim = values.shape[-1] // 2
    front_part = values[..., :half_dim]
    second = values[..., half_dim:]
    cos_wide = cosine[:, None, :]
    sin_wide = sine_table[:, None, :]
    return jnp.concatenate(
        [front_part * cos_wide - second * sin_wide, second * cos_wide + front_part * sin_wide],
        axis=-1,
    )


def place_of(holder, offset, block_rows, ctx_count):
    return jnp.where(
        offset < block_rows,
        holder * block_rows + offset,
        (2 * ctx_count - 1 - holder) * block_rows + offset - block_rows,
    )


def per_device(
    layer_input,
    document_ids,
    cotangent,
    attention_gain,
    query_weight,
    key_weight,
    value_weight,
    output_weight,
    feedforward_gain,
    gate_weight,
    up_weight,
    down_weight,
):
    ctx_count = lax.axis_size("ctx")
    device = lax.axis_index("ctx")
    inputs = layer_input[0].astype(jnp.float32)
    upstream = cotangent[0]
    tok_count = inputs.shape[0]
    model_width = inputs.shape[1]
    block_rows = tok_count // 2
    group_heads = math.gcd(8, HEADS)
    group_count = HEADS // group_heads
    group_width = group_heads * HEAD_DIM
    key_count = ctx_count * tok_count
    local_pos = place_of(device, jnp.arange(tok_count, dtype=jnp.int32), block_rows, ctx_count)
    key_index = jnp.arange(key_count, dtype=jnp.int32)
    key_pos = place_of(key_index // tok_count, key_index % tok_count, block_rows, ctx_count)
    documents = document_ids[0]
    same_doc = jnp.take(documents, local_pos)[:, None] == jnp.take(documents, key_pos)[None, :]
    allowed = (key_pos[None, :] <= local_pos[:, None]) & same_doc
    cosine, sine_table = rotation(local_pos, HEAD_DIM)
    attention_set = (
        lax.all_gather(attention_gain, ("ctx", "fsdp"), axis=0, tiled=True),
        lax.all_gather(query_weight, ("ctx", "fsdp"), axis=0, tiled=True),
        lax.all_gather(key_weight, ("ctx", "fsdp"), axis=0, tiled=True),
        lax.all_gather(value_weight, ("ctx", "fsdp"), axis=0, tiled=True),
        lax.all_gather(output_weight, ("ctx", "fsdp"), axis=0, tiled=True),
    )
    attn_gain_full = attention_set[0].astype(jnp.float32)
    normed_low = norm_scale(inputs, attn_gain_full).astype(jnp.bfloat16)
    query_pre = jnp.dot(normed_low, attention_set[1], preferred_element_type=jnp.float32)
    key_pre = jnp.dot(normed_low, attention_set[2], preferred_element_type=jnp.float32)
    value_pre = jnp.dot(normed_low, attention_set[3], preferred_element_type=jnp.float32)
    queries = (
        rotate(query_pre.reshape(tok_count, HEADS, HEAD_DIM), cosine, sine_table)
        .reshape(tok_count, model_width)
        .astype(jnp.bfloat16)
    )
    keys_local = (
        rotate(key_pre.reshape(tok_count, HEADS, HEAD_DIM), cosine, sine_table)
        .reshape(tok_count, model_width)
        .astype(jnp.bfloat16)
    )
    values_local = value_pre.astype(jnp.bfloat16)
    all_keys, all_values = (
        lax.all_gather(keys_local, "ctx", axis=0, tiled=True),
        lax.all_gather(values_local, "ctx", axis=0, tiled=True),
    )

    def group_parts(group_index):
        column_start = group_index * group_width
        query_part = lax.dynamic_slice_in_dim(queries, column_start, group_width, 1).reshape(
            tok_count, group_heads, HEAD_DIM
        )
        key_part = lax.dynamic_slice_in_dim(all_keys, column_start, group_width, 1).reshape(
            key_count, group_heads, HEAD_DIM
        )
        value_part = lax.dynamic_slice_in_dim(all_values, column_start, group_width, 1).reshape(
            key_count, group_heads, HEAD_DIM
        )
        scores = (
            jnp.einsum("qhd,khd->hqk", query_part, key_part, preferred_element_type=jnp.float32)
            * 0.125
        )
        scores = jnp.where(allowed[None], scores, masked_score)
        return (query_part, key_part, value_part, scores)

    def group_forward(group_index):
        query_part, key_part, value_part, scores = group_parts(group_index)
        row_peak = jnp.max(scores, axis=-1, keepdims=True)
        exponent = jnp.exp(scores - row_peak)
        row_total = jnp.sum(exponent, axis=-1, keepdims=True)
        softmax_weights = exponent / row_total
        log_total = row_peak[..., 0] + jnp.log(row_total[..., 0])
        attended = jnp.einsum(
            "hqk,khd->qhd",
            softmax_weights.astype(jnp.bfloat16),
            value_part,
            preferred_element_type=jnp.float32,
        )
        return (attended.reshape(tok_count, group_width), log_total)

    group_index_all = jnp.arange(group_count, dtype=jnp.int32)
    attended_groups, log_totals = lax.map(group_forward, group_index_all)
    attended_low = (
        jnp.transpose(attended_groups, (1, 0, 2))
        .reshape(tok_count, model_width)
        .astype(jnp.bfloat16)
    )
    hidden = inputs + jnp.dot(attended_low, attention_set[4], preferred_element_type=jnp.float32)
    feedforward_set = (
        lax.all_gather(feedforward_gain, ("ctx", "fsdp"), axis=0, tiled=True),
        lax.all_gather(gate_weight, ("ctx", "fsdp"), axis=0, tiled=True),
        lax.all_gather(up_weight, ("ctx", "fsdp"), axis=0, tiled=True),
        lax.all_gather(down_weight, ("ctx", "fsdp"), axis=0, tiled=True),
    )
    mlp_low = norm_scale(hidden, feedforward_set[0].astype(jnp.float32)).astype(jnp.bfloat16)
    gate_pre = jnp.dot(mlp_low, feedforward_set[1], preferred_element_type=jnp.float32)
    up_pre = jnp.dot(mlp_low, feedforward_set[2], preferred_element_type=jnp.float32)
    product_low = (jax.nn.silu(gate_pre) * up_pre).astype(jnp.bfloat16)
    layer_output = (
        hidden + jnp.dot(product_low, feedforward_set[3], preferred_element_type=jnp.float32)
    ).astype(jnp.bfloat16)
    feedforward_back = (
        lax.all_gather(feedforward_gain, ("ctx", "fsdp"), axis=0, tiled=True),
        lax.all_gather(gate_weight, ("ctx", "fsdp"), axis=0, tiled=True),
        lax.all_gather(up_weight, ("ctx", "fsdp"), axis=0, tiled=True),
        lax.all_gather(down_weight, ("ctx", "fsdp"), axis=0, tiled=True),
    )
    attention_back = (
        lax.all_gather(attention_gain, ("ctx", "fsdp"), axis=0, tiled=True),
        lax.all_gather(query_weight, ("ctx", "fsdp"), axis=0, tiled=True),
        lax.all_gather(key_weight, ("ctx", "fsdp"), axis=0, tiled=True),
        lax.all_gather(value_weight, ("ctx", "fsdp"), axis=0, tiled=True),
        lax.all_gather(output_weight, ("ctx", "fsdp"), axis=0, tiled=True),
    )
    piece = product_low
    down_shard = lax.psum_scatter(
        jnp.einsum("tf,td->fd", piece, upstream, preferred_element_type=jnp.float32),
        ("ctx", "fsdp"),
        scatter_dimension=0,
        tiled=True,
    )
    product_grad = jnp.einsum(
        "td,fd->tf", upstream, feedforward_back[3], preferred_element_type=jnp.float32
    )
    silu_out, silu_pullback = jax.vjp(
        lambda gate_in, up_in: jax.nn.silu(gate_in) * up_in, gate_pre, up_pre
    )
    gate_grad, up_grad = silu_pullback(product_grad)
    gate_grad_low = gate_grad.astype(jnp.bfloat16)
    up_grad_low = up_grad.astype(jnp.bfloat16)
    joined_grads = jnp.concatenate([gate_grad_low, up_grad_low], axis=1)
    piece = mlp_low
    joined_shard = lax.psum_scatter(
        jnp.einsum("td,tf->df", piece, joined_grads, preferred_element_type=jnp.float32),
        ("ctx", "fsdp"),
        scatter_dimension=0,
        tiled=True,
    )
    ff_width = gate_weight.shape[1]
    gate_shard = joined_shard[:, :ff_width]
    up_shard = joined_shard[:, ff_width:]
    mlp_normed_grad = jnp.einsum(
        "tf,df->td", gate_grad_low, feedforward_back[1], preferred_element_type=jnp.float32
    )
    mlp_normed_grad = mlp_normed_grad + jnp.einsum(
        "tf,df->td", up_grad_low, feedforward_back[2], preferred_element_type=jnp.float32
    )
    mlp_norm_out, mlp_norm_pullback = jax.vjp(
        norm_scale, hidden, feedforward_back[0].astype(jnp.float32)
    )
    hidden_from_norm, ff_gain_term = mlp_norm_pullback(mlp_normed_grad)
    hidden_grad = upstream.astype(jnp.float32) + hidden_from_norm
    hidden_low = hidden_grad.astype(jnp.bfloat16)
    output_term = jnp.einsum(
        "td,te->de", attended_low, hidden_low, preferred_element_type=jnp.float32
    )
    attended_grad_low = jnp.einsum(
        "te,de->td", hidden_low, attention_back[4], preferred_element_type=jnp.float32
    ).astype(jnp.bfloat16)

    def group_backward(operands):
        group_index, log_total = operands
        query_part, key_part, value_part, scores = group_parts(group_index)
        softmax_weights = jnp.exp(scores - log_total[:, :, None])
        column_start = group_index * group_width
        grad_part = lax.dynamic_slice_in_dim(
            attended_grad_low, column_start, group_width, 1
        ).reshape(tok_count, group_heads, HEAD_DIM)
        value_grad = jnp.einsum(
            "hqk,qhd->khd",
            softmax_weights.astype(jnp.bfloat16),
            grad_part,
            preferred_element_type=jnp.float32,
        )
        weight_grad = jnp.einsum(
            "qhd,khd->hqk", grad_part, value_part, preferred_element_type=jnp.float32
        )
        row_inner = jnp.sum(weight_grad * softmax_weights, axis=-1, keepdims=True)
        score_grad = (softmax_weights * (weight_grad - row_inner)).astype(jnp.bfloat16)
        query_grad = (
            jnp.einsum("hqk,khd->qhd", score_grad, key_part, preferred_element_type=jnp.float32)
            * 0.125
        )
        key_grad = (
            jnp.einsum("hqk,qhd->khd", score_grad, query_part, preferred_element_type=jnp.float32)
            * 0.125
        )
        return (
            query_grad.reshape(tok_count, group_width),
            key_grad.reshape(key_count, group_width),
            value_grad.reshape(key_count, group_width),
        )

    query_groups, key_groups, value_groups = lax.map(group_backward, (group_index_all, log_totals))
    query_grad_all = jnp.transpose(query_groups, (1, 0, 2)).reshape(tok_count, model_width)
    key_grad_all = jnp.transpose(key_groups, (1, 0, 2)).reshape(key_count, model_width)
    value_grad_all = jnp.transpose(value_groups, (1, 0, 2)).reshape(key_count, model_width)
    key_grad_local, value_grad_local = (
        lax.psum_scatter(
            key_grad_all.astype(jnp.bfloat16), "ctx", scatter_dimension=0, tiled=True
        ).astype(jnp.float32),
        lax.psum_scatter(
            value_grad_all.astype(jnp.bfloat16), "ctx", scatter_dimension=0, tiled=True
        ).astype(jnp.float32),
    )
    negative_sine = -sine_table
    query_pre_grad = (
        rotate(query_grad_all.reshape(tok_count, HEADS, HEAD_DIM), cosine, negative_sine)
        .reshape(tok_count, model_width)
        .astype(jnp.bfloat16)
    )
    key_pre_grad = (
        rotate(key_grad_local.reshape(tok_count, HEADS, HEAD_DIM), cosine, negative_sine)
        .reshape(tok_count, model_width)
        .astype(jnp.bfloat16)
    )
    value_pre_grad = value_grad_local.astype(jnp.bfloat16)
    query_term = jnp.einsum(
        "td,te->de", normed_low, query_pre_grad, preferred_element_type=jnp.float32
    )
    key_term = jnp.einsum("td,te->de", normed_low, key_pre_grad, preferred_element_type=jnp.float32)
    value_term = jnp.einsum(
        "td,te->de", normed_low, value_pre_grad, preferred_element_type=jnp.float32
    )
    attn_normed_grad = jnp.einsum(
        "te,de->td", query_pre_grad, attention_back[1], preferred_element_type=jnp.float32
    )
    attn_normed_grad = attn_normed_grad + jnp.einsum(
        "te,de->td", key_pre_grad, attention_back[2], preferred_element_type=jnp.float32
    )
    attn_normed_grad = attn_normed_grad + jnp.einsum(
        "te,de->td", value_pre_grad, attention_back[3], preferred_element_type=jnp.float32
    )
    attn_norm_out, attn_norm_pullback = jax.vjp(
        norm_scale, inputs, attention_back[0].astype(jnp.float32)
    )
    inputs_from_norm, attn_gain_term = attn_norm_pullback(attn_normed_grad)
    input_grad = (hidden_grad + inputs_from_norm).astype(jnp.bfloat16)
    attn_shards = (
        lax.psum_scatter(attn_gain_term, ("ctx", "fsdp"), scatter_dimension=0, tiled=True),
        lax.psum_scatter(ff_gain_term, ("ctx", "fsdp"), scatter_dimension=0, tiled=True),
        lax.psum_scatter(query_term, ("ctx", "fsdp"), scatter_dimension=0, tiled=True),
        lax.psum_scatter(key_term, ("ctx", "fsdp"), scatter_dimension=0, tiled=True),
        lax.psum_scatter(value_term, ("ctx", "fsdp"), scatter_dimension=0, tiled=True),
        lax.psum_scatter(output_term, ("ctx", "fsdp"), scatter_dimension=0, tiled=True),
    )
    summed = (
        lax.psum(attn_shards[0].astype(jnp.bfloat16), "seq").astype(jnp.float32),
        lax.psum(attn_shards[2].astype(jnp.bfloat16), "seq").astype(jnp.float32),
        lax.psum(attn_shards[3].astype(jnp.bfloat16), "seq").astype(jnp.float32),
        lax.psum(attn_shards[4].astype(jnp.bfloat16), "seq").astype(jnp.float32),
        lax.psum(attn_shards[5].astype(jnp.bfloat16), "seq").astype(jnp.float32),
        lax.psum(attn_shards[1].astype(jnp.bfloat16), "seq").astype(jnp.float32),
        lax.psum(gate_shard.astype(jnp.bfloat16), "seq").astype(jnp.float32),
        lax.psum(up_shard.astype(jnp.bfloat16), "seq").astype(jnp.float32),
        lax.psum(down_shard.astype(jnp.bfloat16), "seq").astype(jnp.float32),
    )
    return (
        layer_output[None],
        input_grad[None],
        summed[0],
        summed[1],
        summed[2],
        summed[3],
        summed[4],
        summed[5],
        summed[6],
        summed[7],
        summed[8],
    )


def gathered(mesh):
    return jax.shard_map(
        per_device,
        mesh=mesh,
        in_specs=(
            P(("seq", "fsdp"), "ctx", None),
            P(("seq", "fsdp"), None),
            P(("seq", "fsdp"), "ctx", None),
            P(("ctx", "fsdp")),
            P(("ctx", "fsdp"), None),
            P(("ctx", "fsdp"), None),
            P(("ctx", "fsdp"), None),
            P(("ctx", "fsdp"), None),
            P(("ctx", "fsdp")),
            P(("ctx", "fsdp"), None),
            P(("ctx", "fsdp"), None),
            P(("ctx", "fsdp"), None),
        ),
        out_specs=(
            P(("seq", "fsdp"), "ctx", None),
            P(("seq", "fsdp"), "ctx", None),
            P(("ctx", "fsdp")),
            P(("ctx", "fsdp"), None),
            P(("ctx", "fsdp"), None),
            P(("ctx", "fsdp"), None),
            P(("ctx", "fsdp"), None),
            P(("ctx", "fsdp")),
            P(("ctx", "fsdp"), None),
            P(("ctx", "fsdp"), None),
            P(("ctx", "fsdp"), None),
        ),
        check_vma=False,
    )


HIDDEN_PIECES = 2
BIG = pltpu.CompilerParams(vmem_limit_bytes=56 * 1024 * 1024)
BF16 = jnp.bfloat16
F32 = jnp.float32


def swap(value, axis):
    return lax.ppermute(value, axis, [(0, 1), (1, 0)])


def fence(late, early):
    return list(lax.optimization_barrier((tuple(late), tuple(early)))[0])


def opposite(along_x, along_seq):
    half = along_x.shape[0] // 2
    return [swap(along_seq[:half], "x"), swap(along_x[half:], "seq")]


def along(block):
    return [swap(block, "x"), swap(block, "seq")]


def add_low(first, *others):
    total = first.astype(F32)
    for other in others:
        total = total + other.astype(F32)
    return total


def return_halves(upper, lower):
    return [swap(upper, "x"), swap(lower, "seq")]


def return_along(to_x, to_seq, by_x, by_seq):
    half = to_x.shape[0] // 2
    to_seq = jnp.concatenate([add_low(to_seq[:half], by_x).astype(BF16), to_seq[half:]], axis=0)
    to_x = jnp.concatenate([to_x[:half], add_low(to_x[half:], by_seq).astype(BF16)], axis=0)
    return [swap(to_x, "x"), swap(to_seq, "seq")]


def return_across(own, by_x, by_seq):
    return swap(add_low(own, by_x, by_seq).astype(BF16), "zl")


def in_order(mine, other, place):
    first = place == 0
    return jnp.stack([jnp.where(first, mine, other), jnp.where(first, other, mine)])


def pair_up(mine, axis):
    return in_order(mine, swap(mine, axis), lax.axis_index(axis))


def slot(count, blocks, joined, w, block):
    return block * count + w if joined else w * blocks + block


def slices_kernel(count, blocks, joined, table_ref, *refs):
    gain, out = refs[-2][...], refs[-1]
    width = refs[0].shape[1]
    for w in range(count):
        for block in range(blocks):
            at = slot(count, blocks, joined, w, block) * width
            out[0, :, at : at + width] = (refs[blocks * w + block][...].astype(F32) * gain).astype(BF16)


def column_slices(table, chips, blocks, column, weights, gain, width, joined):
    rows = weights[0].shape[0]

    def column_spec(block):
        return pl.BlockSpec((rows, width), lambda t, table: (0, column(t, block, table)))

    wide = blocks * width * len(weights)
    return pl.pallas_call(
        functools.partial(slices_kernel, len(weights), blocks, joined),
        grid_spec=pltpu.PrefetchScalarGridSpec(
            num_scalar_prefetch=1,
            grid=(chips,),
            in_specs=[column_spec(block) for _ in weights for block in range(blocks)]
            + [pl.BlockSpec((rows, 1), lambda t, table: (0, 0))],
            out_specs=pl.BlockSpec((1, rows, wide), lambda t, table: (t, 0, 0)),
        ),
        out_shape=jax.ShapeDtypeStruct((chips, rows, wide), BF16),
        compiler_params=BIG,
        cost_estimate=pl.CostEstimate(flops=0, bytes_accessed=1_000_000, transcendentals=0),
        name="column_slices",
    )(table, *[w for w in weights for _ in range(blocks)], gain)


def hidden_slices(place, weights, gain, width):
    def column(t, zh, table):
        return (((t % 2) * 2 + table[0]) * 2 + zh) * 2 + t // 2

    table = jnp.stack([place.seq]).astype(jnp.int32)
    return column_slices(table, 4, 2, column, weights, gain, width, True)


def head_slices(place, weights, gain, width):
    def column(t, z, table):
        return ((table[1] + t - 2 * table[1] * t) * 2 + table[0]) * 4 + z

    table = jnp.stack([place.seq, place.x]).astype(jnp.int32)
    return column_slices(table, 2, 4, column, weights, gain, width, False)


def share_columns(slices):
    return lax.all_to_all(slices, ("zl", "x"), split_axis=0, concat_axis=0, tiled=True)


def chip_half(place, weight):
    half = weight.shape[0] // 2
    moved = lax.ppermute(
        lax.dynamic_slice_in_dim(weight, (1 - place.core) * half, half, 0), ("seq", "core"), [(0, 1), (3, 2)]
    )
    own = lax.dynamic_slice_in_dim(weight, place.core * half, half, 0)
    return jnp.where(place.core == place.seq, own, moved)


def chip_rows(place, mine, other):
    first = place.core == 0
    halves = jnp.stack([jnp.where(first, mine, other), jnp.where(first, other, mine)], axis=1)
    return halves.reshape(-1, mine.shape[-1])


def add_core(place, parts, axis):
    received = swap(lax.dynamic_index_in_dim(parts, 1 - place.core, axis, False), "core")
    return add_low(lax.dynamic_index_in_dim(parts, place.core, axis, False), received).astype(BF16)


def to_far(place, sums):
    return lax.dynamic_index_in_dim(sums, 1 - place.zh, 0, False)


def add_far(place, sums, received):
    return add_low(lax.dynamic_index_in_dim(sums, place.zh, 0, False), received).astype(BF16)


def own_rows(place, total, other):
    mine = place.core == place.seq
    received = swap(jnp.where(mine, other, total), "core")
    kept = jnp.where(mine, total, other)
    first = place.core == 0
    return jnp.concatenate([jnp.where(first, kept, received), jnp.where(first, received, kept)]).astype(F32)


def finish_kernel(count, *refs):
    grads, weights, gain, outs = refs[:count], refs[count : 2 * count], refs[2 * count], refs[2 * count + 1 :]
    j = pl.program_id(0)
    total = None
    for i in range(count):
        grad = grads[i][0, 0].astype(F32)
        outs[i][...] = grad * gain[...]
        term = grad * weights[i][...].astype(F32)
        total = term if total is None else total + term

    @pl.when(j == 0)
    def _():
        outs[count][...] = jnp.zeros_like(outs[count])

    outs[count][...] += total


def finish_columns(pieces, weights, gain, width, joined):
    count, rows = len(weights), weights[0].shape[0]

    def piece_spec(w):
        def index(j):
            x, seq, zh, zl = j // 8, (j // 4) % 2, (j // 2) % 2, j % 2
            if joined:
                return seq, zl * 2 + x, 0, slot(count, 2, joined, w, zh)
            return seq, x, 0, slot(count, 4, joined, w, zh * 2 + zl)

        return pl.BlockSpec((1, 1, rows, width), index)

    column_spec = pl.BlockSpec((rows, width), lambda j: (0, j))
    outs = pl.pallas_call(
        functools.partial(finish_kernel, count),
        grid=(16,),
        in_specs=[piece_spec(w) for w in range(count)]
        + [column_spec] * count
        + [pl.BlockSpec((rows, 1), lambda j: (0, 0))],
        out_specs=[column_spec] * count + [pl.BlockSpec((rows, width), lambda j: (0, 0))],
        out_shape=[jax.ShapeDtypeStruct((rows, 16 * width), F32)] * count + [jax.ShapeDtypeStruct((rows, width), F32)],
        compiler_params=BIG,
        cost_estimate=pl.CostEstimate(flops=0, bytes_accessed=1_000_000, transcendentals=0),
        name="finish_columns",
    )(*[pieces] * count, *weights, gain)
    return outs[:count], jnp.sum(outs[count], axis=1)


class Place:
    def __init__(self):
        self.seq = lax.axis_index("seq")
        self.x = lax.axis_index("x")
        self.core = lax.axis_index("core")
        self.zh = lax.axis_index("zh")
        self.zl = lax.axis_index("zl")


def block_columns(value, source):
    wide = value.shape[1] // 16
    return jnp.concatenate([value[:, i * wide : (i + 1) * wide] for i in source], axis=1)


def to_inner(value):
    return block_columns(value, [x * 8 + z for z in range(8) for x in (0, 1)])


def to_outer(value):
    return block_columns(value, [z * 2 + x for x in (0, 1) for z in range(8)])


def turn(value, cosine, sine):
    lane = lax.broadcasted_iota(jnp.int32, value.shape, 1)
    partner = jnp.where(lane % HEAD_DIM < HEAD_DIM // 2, pltpu.roll(value, 96, 1), pltpu.roll(value, 32, 1))
    return value * cosine + partner * sine


def project_kernel(a_ref, w_ref, cos_ref, sin_ref, q_ref, kv_ref):
    joined = jnp.dot(a_ref[...], w_ref[...], preferred_element_type=F32)
    wide = q_ref.shape[1]
    cosine, sine = cos_ref[...], sin_ref[...]
    for i in range(wide // 128):
        at = slice(i * 128, (i + 1) * 128)
        q_ref[:, at] = turn(joined[:, at], cosine, sine).astype(BF16)
        kv_ref[:, at] = turn(joined[:, wide + i * 128 : wide + (i + 1) * 128], cosine, sine).astype(BF16)
    kv_ref[:, wide:] = joined[:, 2 * wide :].astype(BF16)


def whole_spec(array):
    return pl.BlockSpec(array.shape, lambda i: (0,) * array.ndim)


def project(a_all, weight, cosine, sine):
    tokens, model = a_all.shape
    wide = weight.shape[1] // 3
    tile = cosine.shape[0]
    by_tile = lambda columns: pl.BlockSpec((tile, columns), lambda i: (i, 0))
    return pl.pallas_call(
        project_kernel,
        grid=(tokens // tile,),
        in_specs=[by_tile(model), whole_spec(weight), whole_spec(cosine), whole_spec(sine)],
        out_specs=[by_tile(wide), by_tile(2 * wide)],
        out_shape=[jax.ShapeDtypeStruct((tokens, columns), BF16) for columns in (wide, 2 * wide)],
        compiler_params=BIG,
        cost_estimate=pl.CostEstimate(flops=0, bytes_accessed=1_000_000, transcendentals=0),
        name="project",
    )(a_all, weight, cosine, sine)


def head_lanes(value, odd):
    lane = lax.broadcasted_iota(jnp.int32, value.shape, 1)
    return jnp.where((lane >= HEAD_DIM) == odd, value, jnp.zeros_like(value))


def probabilities(query, key, mask):
    scores = lax.dot_general(query, key, (((1,), (1,)), ((), ())), preferred_element_type=F32) * 0.125
    scores = jnp.where(mask, scores, masked_score)
    weights = jnp.exp(scores - jnp.max(scores, axis=-1, keepdims=True))
    return weights * (1.0 / jnp.sum(weights, axis=-1, keepdims=True))


def allowed_keys(qpos_ref, start_ref, kpos_ref):
    kpos = kpos_ref[...]
    return (kpos <= qpos_ref[...]) & (kpos >= start_ref[0])


def attend_kernel(q_ref, kv_ref, kv2_ref, out_ref, qpos_ref, start_ref, kpos_ref, o_ref, *term_refs):
    mask = allowed_keys(qpos_ref, start_ref, kpos_ref)
    wide = q_ref.shape[1]
    for pair in range(wide // 128):
        at = slice(pair * 128, (pair + 1) * 128)
        value_at = slice(wide + pair * 128, wide + (pair + 1) * 128)
        query = q_ref[:, at]
        key = jnp.concatenate([kv_ref[:, at], kv2_ref[:, at]], axis=0)
        value = jnp.concatenate([kv_ref[:, value_at], kv2_ref[:, value_at]], axis=0)
        total = None
        for odd in (False, True):
            weights = probabilities(head_lanes(query, odd), key, mask).astype(BF16)
            term = jnp.dot(weights, head_lanes(value, odd), preferred_element_type=F32)
            total = term if total is None else total + term
        o_ref[:, at] = total.astype(BF16)
    spill(term_refs, jnp.dot(o_ref[...], out_ref[...], preferred_element_type=F32).astype(BF16))


def fill(refs, target):
    at = 0
    for ref in refs:
        target[at : at + ref.shape[0]] = ref[...]
        at += ref.shape[0]


def spill(refs, value):
    at = 0
    for ref in refs:
        ref[...] = value[at : at + ref.shape[0]]
        at += ref.shape[0]


def at_step(step, action, refs, value):
    for k, group in enumerate((refs[:2], refs[2:])):

        @pl.when(step == k)
        def _(group=group):
            action(group, value)


def square_shapes(half, model):
    return [(half, model)] * 3 + [(half // 2, model)] * 2


def whole_shape(shape, **options):
    return pl.BlockSpec(shape, lambda i: (0, 0), **options)


def square_specs(half, model, **options):
    return [whole_shape(shape, **options) for shape in square_shapes(half, model)]


def sequence_shapes(sequence, half, model):
    return square_shapes(half, model)[2 * sequence : 2 + 3 * sequence]


def attend(sequence, q_all, kv_all, kv_other, out_rows, where, o_all):
    (tokens, wide), model = q_all.shape, out_rows.shape[1]
    rows = tokens // 2
    qpos, start, kpos = where
    at = lambda i: (sequence, 0)
    in_specs = [
        pl.BlockSpec((rows, wide), at),
        pl.BlockSpec((rows, 2 * wide), at),
        pl.BlockSpec((rows, 2 * wide), at),
        whole_spec(out_rows),
        whole_spec(qpos),
        pl.BlockSpec((1, rows, 1), lambda i: (sequence, 0, 0)),
        whole_spec(kpos),
    ]
    shapes = sequence_shapes(sequence, rows // 2, model)
    return into(
        attend_kernel, "attend", [q_all, kv_all, kv_other, out_rows, qpos, start, kpos], in_specs,
        [(tokens, wide)] + shapes, [pl.BlockSpec((rows, wide), at)] + [whole_shape(shape) for shape in shapes],
        [o_all], (1,),
    )


def into(kernel, name, operands, in_specs, shapes, out_specs, buffers, grid, types=None):
    count = len(operands)
    given = [b for b in buffers if b is not None]
    types = types or [BF16] * len(shapes)

    def body(*refs):
        return kernel(*refs[:count], *refs[count + len(given) :])

    return pl.pallas_call(
        body,
        grid=grid,
        in_specs=in_specs + [pl.BlockSpec(memory_space=pl.ANY)] * len(given),
        out_specs=out_specs,
        out_shape=[jax.ShapeDtypeStruct(shape, kind) for shape, kind in zip(shapes, types)],
        input_output_aliases={count + i: i for i in range(len(given))},
        compiler_params=BIG,
        cost_estimate=pl.CostEstimate(flops=0, bytes_accessed=1_000_000, transcendentals=0),
        name=name,
    )(*operands, *given)


def hidden_kernel(*refs):
    b_refs, dy_refs, (w_ref, down_ref, z_ref, d_ref, b_ref, dy_ref) = refs[:5], refs[5:10], refs[10:16]
    db_refs, y_refs = refs[16:21], refs[21:]
    step = pl.program_id(0)
    at_step(step, fill, b_refs, b_ref)
    at_step(step, fill, dy_refs, dy_ref)
    piece = z_ref.shape[1] // HIDDEN_PIECES
    for i in range(HIDDEN_PIECES):
        at = slice(i * piece, (i + 1) * piece)
        gate_at, up_at = slice(2 * i * piece, (2 * i + 1) * piece), slice((2 * i + 1) * piece, (2 * i + 2) * piece)
        both = jnp.dot(b_ref[...], w_ref[:, 2 * i * piece : 2 * (i + 1) * piece], preferred_element_type=F32)
        gate, up = both[:, :piece], both[:, piece:]
        dz = lax.dot_general(dy_ref[...], down_ref[at, :], (((1,), (1,)), ((), ())), preferred_element_type=F32)
        sig = jax.nn.sigmoid(gate)
        silu = gate * sig
        z_ref[:, at] = (silu * up).astype(BF16)
        d_ref[:, gate_at] = (dz * up * sig * (1.0 + gate * (1.0 - sig))).astype(BF16)
        d_ref[:, up_at] = (dz * silu).astype(BF16)
    db = lax.dot_general(d_ref[...], w_ref[...], (((1,), (1,)), ((), ())), preferred_element_type=F32).astype(BF16)
    y = jnp.dot(z_ref[...], down_ref[...], preferred_element_type=F32).astype(BF16)

    at_step(step, spill, db_refs, db)
    at_step(step, spill, y_refs, y)


def hidden_units(square, b_blocks, dy_blocks, weight, down, buffers):
    half, model = b_blocks[0].shape
    rows, width = 2 * half, down.shape[0]
    once = dict(pipeline_mode=pl.Buffered(1))
    by_sequence = lambda columns: pl.BlockSpec((rows, columns), lambda i: (2 * square + i, 0))
    return into(
        hidden_kernel, "hidden_units", [*b_blocks, *dy_blocks, weight, down],
        square_specs(half, model, **once) * 2 + [pl.BlockSpec(a.shape, lambda i: (0, 0), **once) for a in (weight, down)],
        [(4 * rows, width), (4 * rows, 2 * width), (4 * rows, model), (4 * rows, model)] + square_shapes(half, model) * 2,
        [by_sequence(width), by_sequence(2 * width), by_sequence(model), by_sequence(model)]
        + square_specs(half, model) * 2,
        buffers, (2,),
    )


def attend_back_kernel(count, *refs):
    out_ref, q_ref, kv_ref, kv2_ref, qpos_ref, start_ref, kpos_ref, cos_ref, sin_ref = refs[count : count + 9]
    dh_ref, dq_ref, dkv_ref, dkv2_ref = refs[count + 9 :]
    mask = allowed_keys(qpos_ref, start_ref, kpos_ref)
    rows, wide = q_ref.shape
    fill(refs[:count], dh_ref)
    do = lax.dot_general(
        dh_ref[...], out_ref[...], (((1,), (1,)), ((), ())), preferred_element_type=F32
    ).astype(BF16)
    for pair in range(wide // 128):
        at = slice(pair * 128, (pair + 1) * 128)
        value_at = slice(wide + pair * 128, wide + (pair + 1) * 128)
        query, grad = q_ref[:, at], do[:, at]
        key = jnp.concatenate([kv_ref[:, at], kv2_ref[:, at]], axis=0)
        value = jnp.concatenate([kv_ref[:, value_at], kv2_ref[:, value_at]], axis=0)
        dq = dk = dv = 0.0
        for odd in (False, True):
            query_one, grad_one = head_lanes(query, odd), head_lanes(grad, odd)
            weights = probabilities(query_one, key, mask)
            dp = lax.dot_general(grad_one, value, (((1,), (1,)), ((), ())), preferred_element_type=F32)
            inner = jnp.sum(dp * weights, axis=-1, keepdims=True)
            ds = (weights * (dp - inner)).astype(BF16)
            low = weights.astype(BF16)
            dq = dq + jnp.dot(ds, head_lanes(key, odd), preferred_element_type=F32)
            dk = dk + lax.dot_general(ds, query_one, (((0,), (0,)), ((), ())), preferred_element_type=F32)
            dv = dv + lax.dot_general(low, grad_one, (((0,), (0,)), ((), ())), preferred_element_type=F32)
        dq_ref[:, at] = turn(dq * 0.125, cos_ref[...], -sin_ref[...]).astype(BF16)
        dkv_ref[:, at] = dk[:rows] * 0.125
        dkv2_ref[:, at] = (dk[rows:] * 0.125).astype(BF16)
        dkv_ref[:, value_at] = dv[:rows]
        dkv2_ref[:, value_at] = dv[rows:].astype(BF16)


def attend_back(sequence, dh_blocks, out_rows, q_all, kv_all, kv_other, where, tables, dh_all):
    model, (tokens, wide) = dh_blocks[0].shape[1], q_all.shape
    rows = tokens // 2
    qpos, start, kpos = where
    at = lambda i: (sequence, 0)
    in_specs = [whole_spec(block) for block in dh_blocks] + [
        whole_spec(out_rows),
        pl.BlockSpec((rows, wide), at),
        pl.BlockSpec((rows, 2 * wide), at),
        pl.BlockSpec((rows, 2 * wide), at),
        whole_spec(qpos),
        pl.BlockSpec((1, rows, 1), lambda i: (sequence, 0, 0)),
        whole_spec(kpos), whole_spec(tables[0]), whole_spec(tables[1]),
    ]
    return into(
        functools.partial(attend_back_kernel, len(dh_blocks)), "attend_back",
        [*dh_blocks, out_rows, q_all, kv_all, kv_other, qpos, start, kpos, *tables],
        in_specs, [(tokens, model), (rows, wide), (rows, 2 * wide), (rows, 2 * wide)],
        [pl.BlockSpec((rows, model), at)] + [whole_shape((rows, n * wide)) for n in (1, 2, 2)],
        [dh_all], (1,), types=[BF16, BF16, F32, BF16],
    )


def join_kernel(dq_ref, dkv_ref, dkv2_ref, w_ref, cos_ref, sin_ref, out_ref, *term_refs):
    wide = dq_ref.shape[1]
    out_ref[:, :wide] = dq_ref[...]
    for i in range(wide // 128):
        at = slice(i * 128, (i + 1) * 128)
        dk = dkv_ref[:, at] + dkv2_ref[:, at].astype(F32)
        out_ref[:, wide + i * 128 : wide + (i + 1) * 128] = turn(dk, cos_ref[...], -sin_ref[...]).astype(BF16)
    out_ref[:, 2 * wide :] = (dkv_ref[:, wide:] + dkv2_ref[:, wide:].astype(F32)).astype(BF16)
    term = lax.dot_general(out_ref[...], w_ref[...], (((1,), (1,)), ((), ())), preferred_element_type=F32)
    spill(term_refs, term.astype(BF16))


def join_grads(sequence, dq, dkv, dkv_other, weight, tables, d_qkv):
    (rows, wide), model = dq.shape, weight.shape[0]
    operands = [dq, dkv, dkv_other, weight, *tables]
    shapes = sequence_shapes(sequence, rows // 2, model)
    return into(
        join_kernel, "join_grads", operands, [whole_spec(a) for a in operands],
        [(2 * rows, 3 * wide)] + shapes,
        [pl.BlockSpec((rows, 3 * wide), lambda i: (sequence, 0))] + [whole_shape(shape) for shape in shapes],
        [d_qkv], (1,),
    )


def on_rows(kernel, name, operands, types):
    rows, model = operands[0].shape
    tile = pl.BlockSpec((rows // 3, model), lambda i: (i, 0))
    return pl.pallas_call(
        kernel,
        grid=(3,),
        in_specs=[tile] * len(operands),
        out_specs=[tile] * len(types),
        out_shape=[jax.ShapeDtypeStruct((rows, model), kind) for kind in types],
        compiler_params=BIG,
        cost_estimate=pl.CostEstimate(flops=0, bytes_accessed=1_000_000, transcendentals=0),
        name=name,
    )(*operands)


def total_of(refs):
    return add_low(*[ref[...] for ref in refs])


def open_kernel(x_ref, a_ref):
    x = x_ref[...].astype(F32)
    inverse = lax.rsqrt(jnp.mean(x * x, axis=-1, keepdims=True) + epsilon)
    a_ref[...] = to_inner((x * inverse).astype(BF16))


def close_attention_kernel(x_ref, *refs):
    hidden_ref, b_ref = refs[-2:]
    hidden = x_ref[...].astype(F32) + total_of(refs[:-2])
    hidden_ref[...] = hidden
    inverse = lax.rsqrt(jnp.mean(hidden * hidden, axis=-1, keepdims=True) + epsilon)
    b_ref[...] = to_inner((hidden * inverse).astype(BF16))


def close_hidden_kernel(dy_ref, hidden_ref, *refs):
    dh_ref, low_ref = refs[-2:]
    dh = dy_ref[...].astype(F32) + norm_back(hidden_ref[...], to_outer(total_of(refs[:-2])))
    dh_ref[...] = dh
    low_ref[...] = dh.astype(BF16)


def close_input_kernel(x_ref, dh_ref, *refs):
    out_ref = refs[-1]
    out_ref[...] = (dh_ref[...] + norm_back(x_ref[...].astype(F32), to_outer(total_of(refs[:-1])))).astype(BF16)


def norm_back(values, scaled):
    inverse = lax.rsqrt(jnp.mean(values * values, axis=-1, keepdims=True) + epsilon)
    normed = values * inverse
    return inverse * (scaled - normed * jnp.mean(scaled * normed, axis=-1, keepdims=True))


def dot_low(left, right, left_dim, right_dim):
    return lax.dot_general(
        left, right, (((left_dim,), (right_dim,)), ((), ())), preferred_element_type=F32
    ).astype(BF16)


def paired_device(
    layer_input, document_ids, cotangent, attention_gain, query_weight, key_weight, value_weight, output_weight,
    feedforward_gain, gate_weight, up_weight, down_weight,
):
    place = Place()
    x_own, dy_own = layer_input[0], cotangent[0]
    tok_count, model = x_own.shape
    block_rows = tok_count // 2
    length = document_ids.shape[1]
    block_count = length // block_rows
    rows = query_weight.shape[0]
    hidden_rows = down_weight.shape[0]

    attn_gain = attention_gain.astype(F32)[:, None]
    ff_gain = feedforward_gain.astype(F32)[:, None]

    mine, sent = head_slices(place, [query_weight, key_weight, value_weight], attn_gain, rows)
    (a_own,) = on_rows(open_kernel, "open_layer", [x_own], [BF16])
    received = swap(sent, "x")
    a_x, a_s = along(a_own)
    gate_up = hidden_slices(place, [gate_weight, up_weight], ff_gain, hidden_rows)
    qkv = in_order(mine, received, place.x)
    a_x, a_s, qkv, gate_up, out_late, dy_late, document_ids = fence(
        [a_x, a_s, qkv, gate_up, output_weight, dy_own, document_ids], []
    )

    by_zh, by_zl = swap(qkv, "zh"), swap(qkv, "zl")
    a_o = opposite(a_x, a_s)
    gate_up = share_columns(gate_up)
    dy_x, dy_s = along(dy_late)
    documents = document_ids[0]
    first = jnp.sum((documents[None, :] < documents[:, None]).astype(jnp.int32), axis=1)
    out_half = chip_half(place, out_late)
    a_all = jnp.concatenate([a_own, a_x, a_s, *a_o], axis=0)
    by_zh, by_zl, a_all, out_half, first, dy_x, dy_s, dy_late, gate_up = fence(
        [by_zh, by_zl, a_all, out_half, first, dy_x, dy_s, dy_late, gate_up], []
    )

    gate_up = lax.all_gather(gate_up, ("core", "zh"), axis=0, tiled=True).reshape(model, -1)
    by_both = swap(by_zh, "zl")
    qkv = in_order(in_order(qkv, by_zl, place.zl), in_order(by_zh, by_both, place.zl), place.zh)
    dy_o = opposite(dy_x, dy_s)
    out_zh, out_zl = swap(out_half, "zh"), swap(out_half, "zl")
    first = jnp.stack([first, swap(first, "seq")])

    def positions(dx, dc):
        holder = (place.x ^ dx) * 2 + (place.core ^ dc)
        return place_of(holder, jnp.arange(tok_count, dtype=jnp.int32), block_rows, block_count // 2)

    qpos = jnp.concatenate([positions(0, 0), positions(1, 0)])
    kpos = jnp.concatenate([positions(0, 0), positions(1, 0), positions(0, 1), positions(1, 1)])
    cosine, sine = rotation(qpos, HEAD_DIM)
    cosine = jnp.concatenate([cosine] * 4, axis=1)
    sine = jnp.concatenate([-sine, sine] * 2, axis=1)
    firsts = first.reshape(2, block_count, block_rows)
    starts = []
    for dx in range(2):
        holder = (place.x ^ dx) * 2 + place.core
        for index in (holder, block_count - 1 - holder):
            starts.append(lax.dynamic_index_in_dim(firsts, index, 1, False))
    start = jnp.concatenate(starts, axis=1)[:, :, None]
    where = (qpos[:, None], start, kpos[None, :])
    tables = (cosine, sine)
    qkv, out_zh, out_zl, dy_late, where, tables = fence([qkv, out_zh, out_zl, dy_late, where, tables], dy_o)

    qkv = in_order(qkv, swap(qkv, "core"), place.core).reshape(model, -1)
    dy_l = swap(dy_late, "zl")
    out_both = swap(out_zh, "zl")
    out_half = in_order(
        in_order(out_half, out_zl, place.zl), in_order(out_zh, out_both, place.zl), place.zh
    ).reshape(4, -1, model)
    qkv, out_half, down_late = fence([qkv, out_half, down_weight], [])

    q_all, kv_all = project(a_all, qkv, *tables)
    out_rows = chip_rows(place, out_half, swap(out_half, "core"))
    down_half = chip_half(place, down_late)
    quarter = down_half.shape[0] // 2
    q_all, kv_all, out_rows, dy_l, down_half = fence([q_all, kv_all, out_rows, dy_l, down_half], [])

    kv_other = swap(kv_all, "core")
    o_all, term_s, *term_o = attend(1, q_all, kv_all, kv_other, out_rows, where, None)
    dy_lx, dy_ls = along(dy_l)
    term_s, term_o, o_all, dy_lx, dy_ls = fence([term_s, term_o, o_all, dy_lx, dy_ls], [])

    o_all, own, term_x = attend(0, q_all, kv_all, kv_other, out_rows, where, o_all)
    halves = return_halves(*term_o)
    dy_lo = opposite(dy_lx, dy_ls)
    own, term_x, halves, down_half = fence([own, term_x, halves, down_half], dy_lo)

    down_far = [swap(down_half[:quarter], "zh")]
    sums = return_along(term_x, term_s, *halves)
    hidden, b_own = on_rows(close_attention_kernel, "close_attention", [x_own, own, *sums], [F32, BF16])
    b_own, down_half = fence([b_own, down_half], [])

    b_x, b_s = along(b_own)
    b_l = swap(b_own, "zl")
    b_x, b_s, b_l, down_half = fence([b_x, b_s, b_l, down_half], down_far)

    down_far += [swap(down_half[quarter:], "zh")]
    b_o = opposite(b_x, b_s)
    (b_l,) = fence([b_l], b_o)

    b_lx, b_ls = along(b_l)
    down_half = in_order(down_half, jnp.concatenate(down_far), place.zh)
    down_rows = chip_rows(place, down_half, swap(down_half, "core"))
    *buffers, d0, d1, d2, d3, d4, y0, y1, y2, y3, y4 = hidden_units(
        0, [b_own, b_x, b_s, *b_o], [dy_own, dy_x, dy_s, *dy_o], gate_up, down_rows, [None] * 4
    )
    b_lo = opposite(b_lx, b_ls)
    near, near_y = [d0, d1, d2, d3, d4], [y0, y1, y2, y3, y4]
    near, b_lx = fence([near, b_lx], b_lo)

    *buffers, d0, d1, d2, d3, d4, y0, y1, y2, y3, y4 = hidden_units(
        1, [b_l, b_lx, b_ls, *b_lo], [dy_l, dy_lx, dy_ls, *dy_lo], gate_up, down_rows, buffers
    )
    z_all, d_all, b_all, dy_all = buffers
    far, far_y = [d0, d1, d2, d3, d4], [y0, y1, y2, y3, y4]
    near_halves = return_halves(*near[3:])
    near_along = return_along(near[1], near[2], *near_halves)
    far, d_all = fence([far, d_all], near_along)

    far_halves = return_halves(*far[3:])
    gate_up_terms = dot_low(b_all, d_all, 0, 0)
    z_all, gate_up_terms, far_halves = fence([z_all, gate_up_terms, far_halves], [])

    far_along = return_along(far[1], far[2], *far_halves)
    gate_up_sums = add_core(place, gate_up_terms.reshape(2, 2, 4, rows, -1), 0)
    down_terms = dot_low(z_all, dy_all, 0, 0)
    gate_up_sums, down_terms, near_y, near0, far_along = fence(
        [gate_up_sums, down_terms, near_y, near[0], far_along], []
    )

    across = return_across(far[0], *far_along)
    near_y_halves = return_halves(*near_y[3:])
    gate_up_near = lax.psum_scatter(gate_up_sums, "zh", scatter_dimension=0, tiled=True)[0]
    down_sums = add_core(place, down_terms.reshape(2, 2, -1, model), 1)
    dh, dh_low = on_rows(
        close_hidden_kernel, "close_hidden", [dy_own, hidden, near0, *near_along, across], [F32, BF16]
    )
    dh_low, down_sums, near_y_halves = fence([dh_low, down_sums, near_y_halves], [])

    dh_x, dh_s = along(dh_low)
    down_to_zh = to_far(place, down_sums)
    dh_x, dh_s, down_to_zh, near_y, far_y = fence([dh_x, dh_s, down_to_zh, near_y, far_y], [])

    dh_o = opposite(dh_x, dh_s)
    dh_all, dq0, dkv0, dkv_other0 = attend_back(
        0, [dh_low, dh_x], out_rows, q_all, kv_all, kv_other, where, tables, None
    )
    near_y_along = return_along(near_y[1], near_y[2], *near_y_halves)
    down_far = [swap(down_to_zh[:quarter], "zh")]
    dkv_other0, dh_s, far_y, down_to_zh = fence([dkv_other0, dh_s, far_y, down_to_zh], dh_o)

    dkv_other0 = swap(dkv_other0, "core")
    dh_all, dq1, dkv1, dkv_other1 = attend_back(
        1, [dh_s, *dh_o], out_rows, q_all, kv_all, kv_other, where, tables, dh_all
    )
    far_y_halves = return_halves(*far_y[3:])
    dkv0, dkv_other0, dkv_other1, dh_all, down_to_zh = fence(
        [dkv0, dkv_other0, dkv_other1, dh_all, down_to_zh], [*near_y_along, *far_y_halves, *down_far]
    )

    dkv_other1 = swap(dkv_other1, "core")
    d_qkv, own, term_x = join_grads(0, dq0, dkv0, dkv_other0, qkv, tables, None)
    d_qkv, term_s, *term_o = join_grads(1, dq1, dkv1, dkv_other1, qkv, tables, d_qkv)
    down_far += [swap(down_to_zh[quarter:], "zh")]
    far_y_along = return_along(far_y[1], far_y[2], *far_y_halves)
    out_terms = dot_low(o_all, dh_all, 0, 0)
    own, term_x, term_s, term_o, d_qkv, out_terms = fence(
        [own, term_x, term_s, term_o, d_qkv, out_terms], far_y_along
    )

    halves = return_halves(*term_o)
    qkv_terms = dot_low(a_all, d_qkv, 0, 0)
    out_sums = add_core(place, out_terms.reshape(4, 2, -1, model), 1).reshape(2, 2, -1, model)
    y_across = return_across(far_y[0], *far_y_along)
    qkv_terms, halves, out_sums = fence([qkv_terms, halves, out_sums], down_far)

    sums = return_along(term_x, term_s, *halves)
    qkv_sums = add_core(place, qkv_terms.reshape(2, 2, 2, 2 * rows, -1), 0)
    qkv_sums, out_sums, sums, gate_up_near = fence([qkv_sums, out_sums, sums, gate_up_near], [y_across])

    def part(sums, zh, zl):
        return lax.dynamic_slice(sums, (place.zh ^ zh, place.zl ^ zl, 0, 0), (1, 1, *sums.shape[2:]))[0, 0]

    qkv_zl, out_zl = swap(part(qkv_sums, 1, 1), "zl"), swap(part(out_sums, 1, 1), "zl")
    gate_up_near = share_columns(gate_up_near)
    (input_grad,) = on_rows(close_input_kernel, "close_input", [x_own, dh, own, *sums], [BF16])
    down_total = add_far(place, down_sums, jnp.concatenate(down_far))
    down_other = swap(down_total, "seq")
    qkv_zl, out_zl, input_grad = fence([qkv_zl, out_zl, input_grad], [])

    qkv_zh = swap(add_low(part(qkv_sums, 1, 0), qkv_zl).astype(BF16), "zh")
    out_zh = swap(add_low(part(out_sums, 1, 0), out_zl).astype(BF16), "zh")
    qkv_zl, out_zl = swap(part(qkv_sums, 0, 1), "zl"), swap(part(out_sums, 0, 1), "zl")
    gate_up_far = swap(gate_up_near, "seq")
    layer_output = add_low(hidden, near_y[0], *near_y_along, y_across).astype(BF16)
    down_grad = own_rows(place, down_total, down_other)
    qkv_zh, out_zh, qkv_zl, out_zl = fence([qkv_zh, out_zh, qkv_zl, out_zl], [layer_output, down_grad])

    qkv_total = add_low(part(qkv_sums, 0, 0), qkv_zl, qkv_zh).astype(BF16).reshape(2, rows, -1)
    out_total = add_low(part(out_sums, 0, 0), out_zl, out_zh).astype(BF16)
    received = swap(lax.dynamic_index_in_dim(qkv_total, 1 - place.x, 0, False), "x")
    out_other = swap(out_total, "seq")
    qkv_near = in_order(lax.dynamic_index_in_dim(qkv_total, place.x, 0, False), received, place.x)
    qkv_near, out_other, gate_up_far = fence([qkv_near, out_other, gate_up_far], [])

    qkv_far = swap(qkv_near, "seq")
    (gate_grad, up_grad), ff_gain_grad = finish_columns(
        in_order(gate_up_near, gate_up_far, place.seq), [gate_weight, up_weight], ff_gain, hidden_rows, True
    )
    output_grad = own_rows(place, out_total, out_other)
    (query_grad, key_grad, value_grad), attn_gain_grad = finish_columns(
        in_order(qkv_near, qkv_far, place.seq), [query_weight, key_weight, value_weight], attn_gain, rows, False
    )
    return (
        layer_output[None], input_grad[None], attn_gain_grad, query_grad, key_grad, value_grad, output_grad,
        ff_gain_grad, gate_grad, up_grad, down_grad,
    )


def paired(mesh):
    fine = Mesh(mesh.devices.reshape(2, 2, 2, 2, 2), ("seq", "x", "core", "zh", "zl"))
    tokens = P(("seq", "zh", "zl"), ("x", "core"), None)
    matrix, vector = P(("x", "core", "zh", "zl"), None), P(("x", "core", "zh", "zl"))
    return jax.shard_map(
        paired_device,
        mesh=fine,
        in_specs=(tokens, P(("seq", "zh", "zl"), None), tokens, vector) + (matrix,) * 4 + (vector,) + (matrix,) * 3,
        out_specs=(tokens, tokens, vector) + (matrix,) * 4 + (vector,) + (matrix,) * 3,
        check_vma=False,
    )


def solution(mesh):
    if tuple(mesh.shape[axis] for axis in ("seq", "ctx", "fsdp")) == (2, 4, 4):
        return paired(mesh)
    return gathered(mesh)
```

```python
import functools
import math

import jax
import jax.numpy as jnp
from jax import lax
from jax.experimental import pallas as pl
from jax.experimental.pallas import tpu as pltpu
from jax.sharding import Mesh, PartitionSpec as P

HEADS = 32
HEAD_DIM = 64


epsilon = 1e-05
rotary_base = 130000.0
masked_score = -1e30


def norm_scale(values, gain):
    inverse = lax.rsqrt(jnp.mean(values * values, axis=-1, keepdims=True) + epsilon)
    return values * inverse * gain


def rotation(positions, head_size):
    half_dim = head_size // 2
    frequency = rotary_base ** (-(jnp.arange(half_dim, dtype=jnp.float32) * 2.0) / head_size)
    angles = positions.astype(jnp.float32)[:, None] * frequency[None, :]
    return (jnp.cos(angles), jnp.sin(angles))


def rotate(values, cosine, sine_table):
    half_dim = values.shape[-1] // 2
    front_part = values[..., :half_dim]
    second = values[..., half_dim:]
    cos_wide = cosine[:, None, :]
    sin_wide = sine_table[:, None, :]
    return jnp.concatenate(
        [front_part * cos_wide - second * sin_wide, second * cos_wide + front_part * sin_wide],
        axis=-1,
    )


def place_of(holder, offset, block_rows, ctx_count):
    return jnp.where(
        offset < block_rows,
        holder * block_rows + offset,
        (2 * ctx_count - 1 - holder) * block_rows + offset - block_rows,
    )


def per_device(
    layer_input,
    document_ids,
    cotangent,
    attention_gain,
    query_weight,
    key_weight,
    value_weight,
    output_weight,
    feedforward_gain,
    gate_weight,
    up_weight,
    down_weight,
):
    ctx_count = lax.axis_size("ctx")
    device = lax.axis_index("ctx")
    inputs = layer_input[0].astype(jnp.float32)
    upstream = cotangent[0]
    tok_count = inputs.shape[0]
    model_width = inputs.shape[1]
    block_rows = tok_count // 2
    group_heads = math.gcd(8, HEADS)
    group_count = HEADS // group_heads
    group_width = group_heads * HEAD_DIM
    key_count = ctx_count * tok_count
    local_pos = place_of(device, jnp.arange(tok_count, dtype=jnp.int32), block_rows, ctx_count)
    key_index = jnp.arange(key_count, dtype=jnp.int32)
    key_pos = place_of(key_index // tok_count, key_index % tok_count, block_rows, ctx_count)
    documents = document_ids[0]
    same_doc = jnp.take(documents, local_pos)[:, None] == jnp.take(documents, key_pos)[None, :]
    allowed = (key_pos[None, :] <= local_pos[:, None]) & same_doc
    cosine, sine_table = rotation(local_pos, HEAD_DIM)
    attention_set = (
        lax.all_gather(attention_gain, ("ctx", "fsdp"), axis=0, tiled=True),
        lax.all_gather(query_weight, ("ctx", "fsdp"), axis=0, tiled=True),
        lax.all_gather(key_weight, ("ctx", "fsdp"), axis=0, tiled=True),
        lax.all_gather(value_weight, ("ctx", "fsdp"), axis=0, tiled=True),
        lax.all_gather(output_weight, ("ctx", "fsdp"), axis=0, tiled=True),
    )
    attn_gain_full = attention_set[0].astype(jnp.float32)
    normed_low = norm_scale(inputs, attn_gain_full).astype(jnp.bfloat16)
    query_pre = jnp.dot(normed_low, attention_set[1], preferred_element_type=jnp.float32)
    key_pre = jnp.dot(normed_low, attention_set[2], preferred_element_type=jnp.float32)
    value_pre = jnp.dot(normed_low, attention_set[3], preferred_element_type=jnp.float32)
    queries = (
        rotate(query_pre.reshape(tok_count, HEADS, HEAD_DIM), cosine, sine_table)
        .reshape(tok_count, model_width)
        .astype(jnp.bfloat16)
    )
    keys_local = (
        rotate(key_pre.reshape(tok_count, HEADS, HEAD_DIM), cosine, sine_table)
        .reshape(tok_count, model_width)
        .astype(jnp.bfloat16)
    )
    values_local = value_pre.astype(jnp.bfloat16)
    all_keys, all_values = (
        lax.all_gather(keys_local, "ctx", axis=0, tiled=True),
        lax.all_gather(values_local, "ctx", axis=0, tiled=True),
    )

    def group_parts(group_index):
        column_start = group_index * group_width
        query_part = lax.dynamic_slice_in_dim(queries, column_start, group_width, 1).reshape(
            tok_count, group_heads, HEAD_DIM
        )
        key_part = lax.dynamic_slice_in_dim(all_keys, column_start, group_width, 1).reshape(
            key_count, group_heads, HEAD_DIM
        )
        value_part = lax.dynamic_slice_in_dim(all_values, column_start, group_width, 1).reshape(
            key_count, group_heads, HEAD_DIM
        )
        scores = (
            jnp.einsum("qhd,khd->hqk", query_part, key_part, preferred_element_type=jnp.float32)
            * 0.125
        )
        scores = jnp.where(allowed[None], scores, masked_score)
        return (query_part, key_part, value_part, scores)

    def group_forward(group_index):
        query_part, key_part, value_part, scores = group_parts(group_index)
        row_peak = jnp.max(scores, axis=-1, keepdims=True)
        exponent = jnp.exp(scores - row_peak)
        row_total = jnp.sum(exponent, axis=-1, keepdims=True)
        softmax_weights = exponent / row_total
        log_total = row_peak[..., 0] + jnp.log(row_total[..., 0])
        attended = jnp.einsum(
            "hqk,khd->qhd",
            softmax_weights.astype(jnp.bfloat16),
            value_part,
            preferred_element_type=jnp.float32,
        )
        return (attended.reshape(tok_count, group_width), log_total)

    group_index_all = jnp.arange(group_count, dtype=jnp.int32)
    attended_groups, log_totals = lax.map(group_forward, group_index_all)
    attended_low = (
        jnp.transpose(attended_groups, (1, 0, 2))
        .reshape(tok_count, model_width)
        .astype(jnp.bfloat16)
    )
    hidden = inputs + jnp.dot(attended_low, attention_set[4], preferred_element_type=jnp.float32)
    feedforward_set = (
        lax.all_gather(feedforward_gain, ("ctx", "fsdp"), axis=0, tiled=True),
        lax.all_gather(gate_weight, ("ctx", "fsdp"), axis=0, tiled=True),
        lax.all_gather(up_weight, ("ctx", "fsdp"), axis=0, tiled=True),
        lax.all_gather(down_weight, ("ctx", "fsdp"), axis=0, tiled=True),
    )
    mlp_low = norm_scale(hidden, feedforward_set[0].astype(jnp.float32)).astype(jnp.bfloat16)
    gate_pre = jnp.dot(mlp_low, feedforward_set[1], preferred_element_type=jnp.float32)
    up_pre = jnp.dot(mlp_low, feedforward_set[2], preferred_element_type=jnp.float32)
    product_low = (jax.nn.silu(gate_pre) * up_pre).astype(jnp.bfloat16)
    layer_output = (
        hidden + jnp.dot(product_low, feedforward_set[3], preferred_element_type=jnp.float32)
    ).astype(jnp.bfloat16)
    feedforward_back = (
        lax.all_gather(feedforward_gain, ("ctx", "fsdp"), axis=0, tiled=True),
        lax.all_gather(gate_weight, ("ctx", "fsdp"), axis=0, tiled=True),
        lax.all_gather(up_weight, ("ctx", "fsdp"), axis=0, tiled=True),
        lax.all_gather(down_weight, ("ctx", "fsdp"), axis=0, tiled=True),
    )
    attention_back = (
        lax.all_gather(attention_gain, ("ctx", "fsdp"), axis=0, tiled=True),
        lax.all_gather(query_weight, ("ctx", "fsdp"), axis=0, tiled=True),
        lax.all_gather(key_weight, ("ctx", "fsdp"), axis=0, tiled=True),
        lax.all_gather(value_weight, ("ctx", "fsdp"), axis=0, tiled=True),
        lax.all_gather(output_weight, ("ctx", "fsdp"), axis=0, tiled=True),
    )
    piece = product_low
    down_shard = lax.psum_scatter(
        jnp.einsum("tf,td->fd", piece, upstream, preferred_element_type=jnp.float32),
        ("ctx", "fsdp"),
        scatter_dimension=0,
        tiled=True,
    )
    product_grad = jnp.einsum(
        "td,fd->tf", upstream, feedforward_back[3], preferred_element_type=jnp.float32
    )
    silu_out, silu_pullback = jax.vjp(
        lambda gate_in, up_in: jax.nn.silu(gate_in) * up_in, gate_pre, up_pre
    )
    gate_grad, up_grad = silu_pullback(product_grad)
    gate_grad_low = gate_grad.astype(jnp.bfloat16)
    up_grad_low = up_grad.astype(jnp.bfloat16)
    joined_grads = jnp.concatenate([gate_grad_low, up_grad_low], axis=1)
    piece = mlp_low
    joined_shard = lax.psum_scatter(
        jnp.einsum("td,tf->df", piece, joined_grads, preferred_element_type=jnp.float32),
        ("ctx", "fsdp"),
        scatter_dimension=0,
        tiled=True,
    )
    ff_width = gate_weight.shape[1]
    gate_shard = joined_shard[:, :ff_width]
    up_shard = joined_shard[:, ff_width:]
    mlp_normed_grad = jnp.einsum(
        "tf,df->td", gate_grad_low, feedforward_back[1], preferred_element_type=jnp.float32
    )
    mlp_normed_grad = mlp_normed_grad + jnp.einsum(
        "tf,df->td", up_grad_low, feedforward_back[2], preferred_element_type=jnp.float32
    )
    mlp_norm_out, mlp_norm_pullback = jax.vjp(
        norm_scale, hidden, feedforward_back[0].astype(jnp.float32)
    )
    hidden_from_norm, ff_gain_term = mlp_norm_pullback(mlp_normed_grad)
    hidden_grad = upstream.astype(jnp.float32) + hidden_from_norm
    hidden_low = hidden_grad.astype(jnp.bfloat16)
    output_term = jnp.einsum(
        "td,te->de", attended_low, hidden_low, preferred_element_type=jnp.float32
    )
    attended_grad_low = jnp.einsum(
        "te,de->td", hidden_low, attention_back[4], preferred_element_type=jnp.float32
    ).astype(jnp.bfloat16)

    def group_backward(operands):
        group_index, log_total = operands
        query_part, key_part, value_part, scores = group_parts(group_index)
        softmax_weights = jnp.exp(scores - log_total[:, :, None])
        column_start = group_index * group_width
        grad_part = lax.dynamic_slice_in_dim(
            attended_grad_low, column_start, group_width, 1
        ).reshape(tok_count, group_heads, HEAD_DIM)
        value_grad = jnp.einsum(
            "hqk,qhd->khd",
            softmax_weights.astype(jnp.bfloat16),
            grad_part,
            preferred_element_type=jnp.float32,
        )
        weight_grad = jnp.einsum(
            "qhd,khd->hqk", grad_part, value_part, preferred_element_type=jnp.float32
        )
        row_inner = jnp.sum(weight_grad * softmax_weights, axis=-1, keepdims=True)
        score_grad = (softmax_weights * (weight_grad - row_inner)).astype(jnp.bfloat16)
        query_grad = (
            jnp.einsum("hqk,khd->qhd", score_grad, key_part, preferred_element_type=jnp.float32)
            * 0.125
        )
        key_grad = (
            jnp.einsum("hqk,qhd->khd", score_grad, query_part, preferred_element_type=jnp.float32)
            * 0.125
        )
        return (
            query_grad.reshape(tok_count, group_width),
            key_grad.reshape(key_count, group_width),
            value_grad.reshape(key_count, group_width),
        )

    query_groups, key_groups, value_groups = lax.map(group_backward, (group_index_all, log_totals))
    query_grad_all = jnp.transpose(query_groups, (1, 0, 2)).reshape(tok_count, model_width)
    key_grad_all = jnp.transpose(key_groups, (1, 0, 2)).reshape(key_count, model_width)
    value_grad_all = jnp.transpose(value_groups, (1, 0, 2)).reshape(key_count, model_width)
    key_grad_local, value_grad_local = (
        lax.psum_scatter(
            key_grad_all.astype(jnp.bfloat16), "ctx", scatter_dimension=0, tiled=True
        ).astype(jnp.float32),
        lax.psum_scatter(
            value_grad_all.astype(jnp.bfloat16), "ctx", scatter_dimension=0, tiled=True
        ).astype(jnp.float32),
    )
    negative_sine = -sine_table
    query_pre_grad = (
        rotate(query_grad_all.reshape(tok_count, HEADS, HEAD_DIM), cosine, negative_sine)
        .reshape(tok_count, model_width)
        .astype(jnp.bfloat16)
    )
    key_pre_grad = (
        rotate(key_grad_local.reshape(tok_count, HEADS, HEAD_DIM), cosine, negative_sine)
        .reshape(tok_count, model_width)
        .astype(jnp.bfloat16)
    )
    value_pre_grad = value_grad_local.astype(jnp.bfloat16)
    query_term = jnp.einsum(
        "td,te->de", normed_low, query_pre_grad, preferred_element_type=jnp.float32
    )
    key_term = jnp.einsum("td,te->de", normed_low, key_pre_grad, preferred_element_type=jnp.float32)
    value_term = jnp.einsum(
        "td,te->de", normed_low, value_pre_grad, preferred_element_type=jnp.float32
    )
    attn_normed_grad = jnp.einsum(
        "te,de->td", query_pre_grad, attention_back[1], preferred_element_type=jnp.float32
    )
    attn_normed_grad = attn_normed_grad + jnp.einsum(
        "te,de->td", key_pre_grad, attention_back[2], preferred_element_type=jnp.float32
    )
    attn_normed_grad = attn_normed_grad + jnp.einsum(
        "te,de->td", value_pre_grad, attention_back[3], preferred_element_type=jnp.float32
    )
    attn_norm_out, attn_norm_pullback = jax.vjp(
        norm_scale, inputs, attention_back[0].astype(jnp.float32)
    )
    inputs_from_norm, attn_gain_term = attn_norm_pullback(attn_normed_grad)
    input_grad = (hidden_grad + inputs_from_norm).astype(jnp.bfloat16)
    attn_shards = (
        lax.psum_scatter(attn_gain_term, ("ctx", "fsdp"), scatter_dimension=0, tiled=True),
        lax.psum_scatter(ff_gain_term, ("ctx", "fsdp"), scatter_dimension=0, tiled=True),
        lax.psum_scatter(query_term, ("ctx", "fsdp"), scatter_dimension=0, tiled=True),
        lax.psum_scatter(key_term, ("ctx", "fsdp"), scatter_dimension=0, tiled=True),
        lax.psum_scatter(value_term, ("ctx", "fsdp"), scatter_dimension=0, tiled=True),
        lax.psum_scatter(output_term, ("ctx", "fsdp"), scatter_dimension=0, tiled=True),
    )
    summed = (
        lax.psum(attn_shards[0].astype(jnp.bfloat16), "seq").astype(jnp.float32),
        lax.psum(attn_shards[2].astype(jnp.bfloat16), "seq").astype(jnp.float32),
        lax.psum(attn_shards[3].astype(jnp.bfloat16), "seq").astype(jnp.float32),
        lax.psum(attn_shards[4].astype(jnp.bfloat16), "seq").astype(jnp.float32),
        lax.psum(attn_shards[5].astype(jnp.bfloat16), "seq").astype(jnp.float32),
        lax.psum(attn_shards[1].astype(jnp.bfloat16), "seq").astype(jnp.float32),
        lax.psum(gate_shard.astype(jnp.bfloat16), "seq").astype(jnp.float32),
        lax.psum(up_shard.astype(jnp.bfloat16), "seq").astype(jnp.float32),
        lax.psum(down_shard.astype(jnp.bfloat16), "seq").astype(jnp.float32),
    )
    return (
        layer_output[None],
        input_grad[None],
        summed[0],
        summed[1],
        summed[2],
        summed[3],
        summed[4],
        summed[5],
        summed[6],
        summed[7],
        summed[8],
    )


def gathered(mesh):
    return jax.shard_map(
        per_device,
        mesh=mesh,
        in_specs=(
            P(("seq", "fsdp"), "ctx", None),
            P(("seq", "fsdp"), None),
            P(("seq", "fsdp"), "ctx", None),
            P(("ctx", "fsdp")),
            P(("ctx", "fsdp"), None),
            P(("ctx", "fsdp"), None),
            P(("ctx", "fsdp"), None),
            P(("ctx", "fsdp"), None),
            P(("ctx", "fsdp")),
            P(("ctx", "fsdp"), None),
            P(("ctx", "fsdp"), None),
            P(("ctx", "fsdp"), None),
        ),
        out_specs=(
            P(("seq", "fsdp"), "ctx", None),
            P(("seq", "fsdp"), "ctx", None),
            P(("ctx", "fsdp")),
            P(("ctx", "fsdp"), None),
            P(("ctx", "fsdp"), None),
            P(("ctx", "fsdp"), None),
            P(("ctx", "fsdp"), None),
            P(("ctx", "fsdp")),
            P(("ctx", "fsdp"), None),
            P(("ctx", "fsdp"), None),
            P(("ctx", "fsdp"), None),
        ),
        check_vma=False,
    )


HIDDEN_PIECES = 2
BIG = pltpu.CompilerParams(vmem_limit_bytes=56 * 1024 * 1024)
BF16 = jnp.bfloat16
F32 = jnp.float32


def swap(value, axis):
    return lax.ppermute(value, axis, [(0, 1), (1, 0)])


def fence(late, early):
    return list(lax.optimization_barrier((tuple(late), tuple(early)))[0])


def opposite(along_x, along_seq):
    half = along_x.shape[0] // 2
    return [swap(along_seq[:half], "x"), swap(along_x[half:], "seq")]


def along(block):
    return [swap(block, "x"), swap(block, "seq")]


def add_low(first, *others):
    total = first.astype(F32)
    for other in others:
        total = total + other.astype(F32)
    return total


def return_halves(upper, lower):
    return [swap(upper, "x"), swap(lower, "seq")]


def return_along(to_x, to_seq, by_x, by_seq):
    half = to_x.shape[0] // 2
    to_seq = jnp.concatenate([add_low(to_seq[:half], by_x).astype(BF16), to_seq[half:]], axis=0)
    to_x = jnp.concatenate([to_x[:half], add_low(to_x[half:], by_seq).astype(BF16)], axis=0)
    return [swap(to_x, "x"), swap(to_seq, "seq")]


def return_across(own, by_x, by_seq):
    return swap(add_low(own, by_x, by_seq).astype(BF16), "zl")


def in_order(mine, other, place):
    first = place == 0
    return jnp.stack([jnp.where(first, mine, other), jnp.where(first, other, mine)])


def pair_up(mine, axis):
    return in_order(mine, swap(mine, axis), lax.axis_index(axis))


def slot(count, blocks, joined, w, block):
    return block * count + w if joined else w * blocks + block


def slices_kernel(count, blocks, joined, table_ref, *refs):
    gain, out = refs[-2][...], refs[-1]
    width = refs[0].shape[1]
    for w in range(count):
        for block in range(blocks):
            at = slot(count, blocks, joined, w, block) * width
            out[0, :, at : at + width] = (refs[blocks * w + block][...].astype(F32) * gain).astype(BF16)


def column_slices(table, chips, blocks, column, weights, gain, width, joined):
    rows = weights[0].shape[0]

    def column_spec(block):
        return pl.BlockSpec((rows, width), lambda t, table: (0, column(t, block, table)))

    wide = blocks * width * len(weights)
    return pl.pallas_call(
        functools.partial(slices_kernel, len(weights), blocks, joined),
        grid_spec=pltpu.PrefetchScalarGridSpec(
            num_scalar_prefetch=1,
            grid=(chips,),
            in_specs=[column_spec(block) for _ in weights for block in range(blocks)]
            + [pl.BlockSpec((rows, 1), lambda t, table: (0, 0))],
            out_specs=pl.BlockSpec((1, rows, wide), lambda t, table: (t, 0, 0)),
        ),
        out_shape=jax.ShapeDtypeStruct((chips, rows, wide), BF16),
        compiler_params=BIG,
        cost_estimate=pl.CostEstimate(flops=0, bytes_accessed=1_000_000, transcendentals=0),
        name="column_slices",
    )(table, *[w for w in weights for _ in range(blocks)], gain)


def hidden_slices(place, weights, gain, width):
    def column(t, zh, table):
        return (((t % 2) * 2 + table[0]) * 2 + zh) * 2 + t // 2

    table = jnp.stack([place.seq]).astype(jnp.int32)
    return column_slices(table, 4, 2, column, weights, gain, width, True)


def head_slices(place, weights, gain, width):
    def column(t, z, table):
        return ((table[1] + t - 2 * table[1] * t) * 2 + table[0]) * 4 + z

    table = jnp.stack([place.seq, place.x]).astype(jnp.int32)
    return column_slices(table, 2, 4, column, weights, gain, width, False)


def share_columns(slices):
    return lax.all_to_all(slices, ("zl", "x"), split_axis=0, concat_axis=0, tiled=True)


def chip_half(place, weight):
    half = weight.shape[0] // 2
    moved = lax.ppermute(
        lax.dynamic_slice_in_dim(weight, (1 - place.core) * half, half, 0), ("seq", "core"), [(0, 1), (3, 2)]
    )
    own = lax.dynamic_slice_in_dim(weight, place.core * half, half, 0)
    return jnp.where(place.core == place.seq, own, moved)


def chip_rows(place, mine, other):
    first = place.core == 0
    halves = jnp.stack([jnp.where(first, mine, other), jnp.where(first, other, mine)], axis=1)
    return halves.reshape(-1, mine.shape[-1])


def add_core(place, parts, axis):
    received = swap(lax.dynamic_index_in_dim(parts, 1 - place.core, axis, False), "core")
    return add_low(lax.dynamic_index_in_dim(parts, place.core, axis, False), received).astype(BF16)


def to_far(place, sums):
    return lax.dynamic_index_in_dim(sums, 1 - place.zh, 0, False)


def add_far(place, sums, received):
    return add_low(lax.dynamic_index_in_dim(sums, place.zh, 0, False), received).astype(BF16)


def own_rows(place, total, other):
    mine = place.core == place.seq
    received = swap(jnp.where(mine, other, total), "core")
    kept = jnp.where(mine, total, other)
    first = place.core == 0
    return jnp.concatenate([jnp.where(first, kept, received), jnp.where(first, received, kept)]).astype(F32)


def finish_kernel(count, *refs):
    grads, weights, gain, outs = refs[:count], refs[count : 2 * count], refs[2 * count], refs[2 * count + 1 :]
    j = pl.program_id(0)
    total = None
    for i in range(count):
        grad = grads[i][0, 0].astype(F32)
        outs[i][...] = grad * gain[...]
        term = grad * weights[i][...].astype(F32)
        total = term if total is None else total + term

    @pl.when(j == 0)
    def _():
        outs[count][...] = jnp.zeros_like(outs[count])

    outs[count][...] += total


def finish_columns(pieces, weights, gain, width, joined):
    count, rows = len(weights), weights[0].shape[0]

    def piece_spec(w):
        def index(j):
            x, seq, zh, zl = j // 8, (j // 4) % 2, (j // 2) % 2, j % 2
            if joined:
                return seq, zl * 2 + x, 0, slot(count, 2, joined, w, zh)
            return seq, x, 0, slot(count, 4, joined, w, zh * 2 + zl)

        return pl.BlockSpec((1, 1, rows, width), index)

    column_spec = pl.BlockSpec((rows, width), lambda j: (0, j))
    outs = pl.pallas_call(
        functools.partial(finish_kernel, count),
        grid=(16,),
        in_specs=[piece_spec(w) for w in range(count)]
        + [column_spec] * count
        + [pl.BlockSpec((rows, 1), lambda j: (0, 0))],
        out_specs=[column_spec] * count + [pl.BlockSpec((rows, width), lambda j: (0, 0))],
        out_shape=[jax.ShapeDtypeStruct((rows, 16 * width), F32)] * count + [jax.ShapeDtypeStruct((rows, width), F32)],
        compiler_params=BIG,
        cost_estimate=pl.CostEstimate(flops=0, bytes_accessed=1_000_000, transcendentals=0),
        name="finish_columns",
    )(*[pieces] * count, *weights, gain)
    return outs[:count], jnp.sum(outs[count], axis=1)


class Place:
    def __init__(self):
        self.seq = lax.axis_index("seq")
        self.x = lax.axis_index("x")
        self.core = lax.axis_index("core")
        self.zh = lax.axis_index("zh")
        self.zl = lax.axis_index("zl")


def block_columns(value, source):
    wide = value.shape[1] // 16
    return jnp.concatenate([value[:, i * wide : (i + 1) * wide] for i in source], axis=1)


def to_inner(value):
    return block_columns(value, [x * 8 + z for z in range(8) for x in (0, 1)])


def to_outer(value):
    return block_columns(value, [z * 2 + x for x in (0, 1) for z in range(8)])


def turn(value, cosine, sine):
    lane = lax.broadcasted_iota(jnp.int32, value.shape, 1)
    partner = jnp.where(lane % HEAD_DIM < HEAD_DIM // 2, pltpu.roll(value, 96, 1), pltpu.roll(value, 32, 1))
    return value * cosine + partner * sine


def project_kernel(core_ref, a_ref, a2_ref, w_ref, w2_ref, cos_ref, sin_ref, q_ref, kv_ref):
    joined = jnp.dot(a_ref[...], w_ref[...], preferred_element_type=F32)
    joined = joined + jnp.dot(a2_ref[...], w2_ref[...], preferred_element_type=F32)
    wide = q_ref.shape[1]
    cosine, sine = cos_ref[...], sin_ref[...]
    for i in range(wide // 128):
        at = slice(i * 128, (i + 1) * 128)
        q_ref[:, at] = turn(joined[:, at], cosine, sine).astype(BF16)
        kv_ref[:, at] = turn(joined[:, wide + i * 128 : wide + (i + 1) * 128], cosine, sine).astype(BF16)
    kv_ref[:, wide:] = joined[:, 2 * wide :].astype(BF16)


def whole_spec(array):
    return pl.BlockSpec(array.shape, lambda i: (0,) * array.ndim)


def project(core, a_all, weight, weight_other, cosine, sine):
    tokens, model = a_all.shape
    wide = weight.shape[1] // 3
    tile, half = cosine.shape[0], model // 2
    by_tile = lambda columns: pl.BlockSpec((tile, columns), lambda i, core: (i, 0))
    whole = lambda array: pl.BlockSpec(array.shape, lambda i, core: (0, 0))
    return pl.pallas_call(
        project_kernel,
        grid_spec=pltpu.PrefetchScalarGridSpec(
            num_scalar_prefetch=1,
            grid=(tokens // tile,),
            in_specs=[
                pl.BlockSpec((tile, half), lambda i, core: (i, core[0])),
                pl.BlockSpec((tile, half), lambda i, core: (i, 1 - core[0])),
                whole(weight), whole(weight_other), whole(cosine), whole(sine),
            ],
            out_specs=[by_tile(wide), by_tile(2 * wide)],
        ),
        out_shape=[jax.ShapeDtypeStruct((tokens, columns), BF16) for columns in (wide, 2 * wide)],
        compiler_params=BIG,
        cost_estimate=pl.CostEstimate(flops=0, bytes_accessed=1_000_000, transcendentals=0),
        name="project",
    )(core, a_all, a_all, weight, weight_other, cosine, sine)


def head_lanes(value, odd):
    lane = lax.broadcasted_iota(jnp.int32, value.shape, 1)
    return jnp.where((lane >= HEAD_DIM) == odd, value, jnp.zeros_like(value))


def probabilities(query, key, mask):
    scores = lax.dot_general(query, key, (((1,), (1,)), ((), ())), preferred_element_type=F32) * 0.125
    scores = jnp.where(mask, scores, masked_score)
    weights = jnp.exp(scores - jnp.max(scores, axis=-1, keepdims=True))
    return weights * (1.0 / jnp.sum(weights, axis=-1, keepdims=True))


def allowed_keys(qpos_ref, start_ref, kpos_ref):
    kpos = kpos_ref[...]
    return (kpos <= qpos_ref[...]) & (kpos >= start_ref[0])


def attend_kernel(q_ref, kv_ref, kv2_ref, out_ref, qpos_ref, start_ref, kpos_ref, o_ref, *term_refs):
    mask = allowed_keys(qpos_ref, start_ref, kpos_ref)
    wide = q_ref.shape[1]
    for pair in range(wide // 128):
        at = slice(pair * 128, (pair + 1) * 128)
        value_at = slice(wide + pair * 128, wide + (pair + 1) * 128)
        query = q_ref[:, at]
        key = jnp.concatenate([kv_ref[:, at], kv2_ref[:, at]], axis=0)
        value = jnp.concatenate([kv_ref[:, value_at], kv2_ref[:, value_at]], axis=0)
        total = None
        for odd in (False, True):
            weights = probabilities(head_lanes(query, odd), key, mask).astype(BF16)
            term = jnp.dot(weights, head_lanes(value, odd), preferred_element_type=F32)
            total = term if total is None else total + term
        o_ref[:, at] = total.astype(BF16)
    spill(term_refs, jnp.dot(o_ref[...], out_ref[...], preferred_element_type=F32).astype(BF16))


def fill(refs, target):
    at = 0
    for ref in refs:
        target[at : at + ref.shape[0]] = ref[...]
        at += ref.shape[0]


def spill(refs, value):
    at = 0
    for ref in refs:
        ref[...] = value[at : at + ref.shape[0]]
        at += ref.shape[0]


def at_step(step, action, refs, value):
    for k, group in enumerate((refs[:2], refs[2:])):

        @pl.when(step == k)
        def _(group=group):
            action(group, value)


def square_shapes(half, model):
    return [(half, model)] * 3 + [(half // 2, model)] * 2


def whole_shape(shape, **options):
    return pl.BlockSpec(shape, lambda i: (0, 0), **options)


def square_specs(half, model, **options):
    return [whole_shape(shape, **options) for shape in square_shapes(half, model)]


def sequence_shapes(sequence, half, model):
    return square_shapes(half, model)[2 * sequence : 2 + 3 * sequence]


def attend(sequence, q_all, kv_all, kv_other, out_rows, where, o_all):
    (tokens, wide), model = q_all.shape, out_rows.shape[1]
    rows = tokens // 2
    qpos, start, kpos = where
    at = lambda i: (sequence, 0)
    in_specs = [
        pl.BlockSpec((rows, wide), at),
        pl.BlockSpec((rows, 2 * wide), at),
        pl.BlockSpec((rows, 2 * wide), at),
        whole_spec(out_rows),
        whole_spec(qpos),
        pl.BlockSpec((1, rows, 1), lambda i: (sequence, 0, 0)),
        whole_spec(kpos),
    ]
    shapes = sequence_shapes(sequence, rows // 2, model)
    return into(
        attend_kernel, "attend", [q_all, kv_all, kv_other, out_rows, qpos, start, kpos], in_specs,
        [(tokens, wide)] + shapes, [pl.BlockSpec((rows, wide), at)] + [whole_shape(shape) for shape in shapes],
        [o_all], (1,),
    )


def into(kernel, name, operands, in_specs, shapes, out_specs, buffers, grid, types=None):
    count = len(operands)
    given = [b for b in buffers if b is not None]
    types = types or [BF16] * len(shapes)

    def body(*refs):
        return kernel(*refs[:count], *refs[count + len(given) :])

    return pl.pallas_call(
        body,
        grid=grid,
        in_specs=in_specs + [pl.BlockSpec(memory_space=pl.ANY)] * len(given),
        out_specs=out_specs,
        out_shape=[jax.ShapeDtypeStruct(shape, kind) for shape, kind in zip(shapes, types)],
        input_output_aliases={count + i: i for i in range(len(given))},
        compiler_params=BIG,
        cost_estimate=pl.CostEstimate(flops=0, bytes_accessed=1_000_000, transcendentals=0),
        name=name,
    )(*operands, *given)


def hidden_kernel(count, *refs):
    (b_refs, dy_refs), (w_ref, down_ref, z_ref, d_ref, b_ref, dy_ref) = (
        (refs[:count], refs[count : 2 * count]),
        refs[2 * count : 2 * count + 6],
    )
    db_refs, y_refs = refs[2 * count + 6 : 3 * count + 6], refs[3 * count + 6 :]
    fill(b_refs, b_ref)
    fill(dy_refs, dy_ref)
    piece = z_ref.shape[1] // HIDDEN_PIECES
    for i in range(HIDDEN_PIECES):
        at = slice(i * piece, (i + 1) * piece)
        gate_at, up_at = slice(2 * i * piece, (2 * i + 1) * piece), slice((2 * i + 1) * piece, (2 * i + 2) * piece)
        both = jnp.dot(b_ref[...], w_ref[:, 2 * i * piece : 2 * (i + 1) * piece], preferred_element_type=F32)
        gate, up = both[:, :piece], both[:, piece:]
        dz = lax.dot_general(dy_ref[...], down_ref[at, :], (((1,), (1,)), ((), ())), preferred_element_type=F32)
        sig = jax.nn.sigmoid(gate)
        silu = gate * sig
        z_ref[:, at] = (silu * up).astype(BF16)
        d_ref[:, gate_at] = (dz * up * sig * (1.0 + gate * (1.0 - sig))).astype(BF16)
        d_ref[:, up_at] = (dz * silu).astype(BF16)
    db = lax.dot_general(d_ref[...], w_ref[...], (((1,), (1,)), ((), ())), preferred_element_type=F32).astype(BF16)
    y = jnp.dot(z_ref[...], down_ref[...], preferred_element_type=F32).astype(BF16)

    spill(db_refs, db)
    spill(y_refs, y)


def hidden_units(index, b_blocks, dy_blocks, weight, down, buffers):
    model, width = weight.shape[0], down.shape[0]
    shapes = [block.shape for block in b_blocks]
    rows = sum(shape[0] for shape in shapes)
    once = dict(pipeline_mode=pl.Buffered(1))
    own = lambda columns: pl.BlockSpec((rows, columns), lambda i: (index, 0))
    operands = [*b_blocks, *dy_blocks, weight, down]
    out = into(
        functools.partial(hidden_kernel, len(shapes)), "hidden_units", operands,
        [whole_shape(a.shape, **once) for a in operands],
        [(4 * rows, width), (4 * rows, 2 * width), (4 * rows, model), (4 * rows, model)] + shapes * 2,
        [own(width), own(2 * width), own(model), own(model)] + [whole_shape(shape) for shape in shapes * 2],
        buffers, (1,),
    )
    return list(out[:4]), list(out[4 : 4 + len(shapes)]), list(out[4 + len(shapes) :])


def attend_back_kernel(count, *refs):
    out_ref, q_ref, kv_ref, kv2_ref, qpos_ref, start_ref, kpos_ref, cos_ref, sin_ref = refs[count : count + 9]
    dh_ref, dq_ref, dkv_ref, dkv2_ref = refs[count + 9 :]
    mask = allowed_keys(qpos_ref, start_ref, kpos_ref)
    rows, wide = q_ref.shape
    fill(refs[:count], dh_ref)
    do = lax.dot_general(
        dh_ref[...], out_ref[...], (((1,), (1,)), ((), ())), preferred_element_type=F32
    ).astype(BF16)
    for pair in range(wide // 128):
        at = slice(pair * 128, (pair + 1) * 128)
        value_at = slice(wide + pair * 128, wide + (pair + 1) * 128)
        query, grad = q_ref[:, at], do[:, at]
        key = jnp.concatenate([kv_ref[:, at], kv2_ref[:, at]], axis=0)
        value = jnp.concatenate([kv_ref[:, value_at], kv2_ref[:, value_at]], axis=0)
        dq = dk = dv = 0.0
        for odd in (False, True):
            query_one, grad_one = head_lanes(query, odd), head_lanes(grad, odd)
            weights = probabilities(query_one, key, mask)
            dp = lax.dot_general(grad_one, value, (((1,), (1,)), ((), ())), preferred_element_type=F32)
            inner = jnp.sum(dp * weights, axis=-1, keepdims=True)
            ds = (weights * (dp - inner)).astype(BF16)
            low = weights.astype(BF16)
            dq = dq + jnp.dot(ds, head_lanes(key, odd), preferred_element_type=F32)
            dk = dk + lax.dot_general(ds, query_one, (((0,), (0,)), ((), ())), preferred_element_type=F32)
            dv = dv + lax.dot_general(low, grad_one, (((0,), (0,)), ((), ())), preferred_element_type=F32)
        dq_ref[:, at] = turn(dq * 0.125, cos_ref[...], -sin_ref[...]).astype(BF16)
        dkv_ref[:, at] = dk[:rows] * 0.125
        dkv2_ref[:, at] = (dk[rows:] * 0.125).astype(BF16)
        dkv_ref[:, value_at] = dv[:rows]
        dkv2_ref[:, value_at] = dv[rows:].astype(BF16)


def attend_back(sequence, dh_blocks, out_rows, q_all, kv_all, kv_other, where, tables, dh_all):
    model, (tokens, wide) = dh_blocks[0].shape[1], q_all.shape
    rows = tokens // 2
    qpos, start, kpos = where
    at = lambda i: (sequence, 0)
    in_specs = [whole_spec(block) for block in dh_blocks] + [
        whole_spec(out_rows),
        pl.BlockSpec((rows, wide), at),
        pl.BlockSpec((rows, 2 * wide), at),
        pl.BlockSpec((rows, 2 * wide), at),
        whole_spec(qpos),
        pl.BlockSpec((1, rows, 1), lambda i: (sequence, 0, 0)),
        whole_spec(kpos), whole_spec(tables[0]), whole_spec(tables[1]),
    ]
    return into(
        functools.partial(attend_back_kernel, len(dh_blocks)), "attend_back",
        [*dh_blocks, out_rows, q_all, kv_all, kv_other, qpos, start, kpos, *tables],
        in_specs, [(tokens, model), (rows, wide), (rows, 2 * wide), (rows, 2 * wide)],
        [pl.BlockSpec((rows, model), at)] + [whole_shape((rows, n * wide)) for n in (1, 2, 2)],
        [dh_all], (1,), types=[BF16, BF16, F32, BF16],
    )


def join_kernel(dq_ref, dkv_ref, dkv2_ref, cos_ref, sin_ref, out_ref):
    wide = dq_ref.shape[1]
    out_ref[:, :wide] = dq_ref[...]
    for i in range(wide // 128):
        at = slice(i * 128, (i + 1) * 128)
        dk = dkv_ref[:, at] + dkv2_ref[:, at].astype(F32)
        out_ref[:, wide + i * 128 : wide + (i + 1) * 128] = turn(dk, cos_ref[...], -sin_ref[...]).astype(BF16)
    out_ref[:, 2 * wide :] = (dkv_ref[:, wide:] + dkv2_ref[:, wide:].astype(F32)).astype(BF16)


def join_grads(sequence, dq, dkv, dkv_other, tables, d_qkv):
    rows, wide = dq.shape
    operands = [dq, dkv, dkv_other, *tables]
    (d_qkv,) = into(
        join_kernel, "join_grads", operands, [whole_spec(a) for a in operands],
        [(2 * rows, 3 * wide)], [pl.BlockSpec((rows, 3 * wide), lambda i: (sequence, 0))], [d_qkv], (1,),
    )
    return d_qkv


def input_terms_kernel(d_ref, w_ref, w2_ref, core_ref, *term_refs):
    mine, other = (
        lax.dot_general(d_ref[...], ref[...], (((1,), (1,)), ((), ())), preferred_element_type=F32).astype(BF16)
        for ref in (w_ref, w2_ref)
    )
    first = core_ref[0] == 0
    terms = jnp.concatenate([jnp.where(first, mine, other), jnp.where(first, other, mine)], axis=1)
    at_step(pl.program_id(0), spill, term_refs, terms)


def input_terms(core, d_qkv, weights):
    tokens, wide = d_qkv.shape
    model = 2 * weights[0].shape[0]
    return into(
        input_terms_kernel, "input_terms", [d_qkv, *weights, core],
        [pl.BlockSpec((tokens // 2, wide), lambda i: (i, 0)), whole_spec(weights[0]), whole_spec(weights[1]),
         pl.BlockSpec(memory_space=pltpu.SMEM)],
        square_shapes(tokens // 4, model), square_specs(tokens // 4, model), [], (2,),
    )


def on_rows(kernel, name, operands, types):
    rows, model = operands[0].shape
    tile = pl.BlockSpec((rows // 3, model), lambda i: (i, 0))
    return pl.pallas_call(
        kernel,
        grid=(3,),
        in_specs=[tile] * len(operands),
        out_specs=[tile] * len(types),
        out_shape=[jax.ShapeDtypeStruct((rows, model), kind) for kind in types],
        compiler_params=BIG,
        cost_estimate=pl.CostEstimate(flops=0, bytes_accessed=1_000_000, transcendentals=0),
        name=name,
    )(*operands)


def total_of(refs):
    return add_low(*[ref[...] for ref in refs])


def open_kernel(x_ref, a_ref):
    x = x_ref[...].astype(F32)
    inverse = lax.rsqrt(jnp.mean(x * x, axis=-1, keepdims=True) + epsilon)
    a_ref[...] = to_inner((x * inverse).astype(BF16))


def close_attention_kernel(x_ref, *refs):
    hidden_ref, b_ref = refs[-2:]
    hidden = x_ref[...].astype(F32) + total_of(refs[:-2])
    hidden_ref[...] = hidden
    inverse = lax.rsqrt(jnp.mean(hidden * hidden, axis=-1, keepdims=True) + epsilon)
    b_ref[...] = to_inner((hidden * inverse).astype(BF16))


def close_hidden_kernel(dy_ref, hidden_ref, *refs):
    dh_ref, low_ref = refs[-2:]
    dh = dy_ref[...].astype(F32) + norm_back(hidden_ref[...], to_outer(total_of(refs[:-2])))
    dh_ref[...] = dh
    low_ref[...] = dh.astype(BF16)


def close_input_kernel(x_ref, dh_ref, *refs):
    out_ref = refs[-1]
    out_ref[...] = (dh_ref[...] + norm_back(x_ref[...].astype(F32), to_outer(total_of(refs[:-1])))).astype(BF16)


def norm_back(values, scaled):
    inverse = lax.rsqrt(jnp.mean(values * values, axis=-1, keepdims=True) + epsilon)
    normed = values * inverse
    return inverse * (scaled - normed * jnp.mean(scaled * normed, axis=-1, keepdims=True))


def dot_low(left, right, left_dim, right_dim):
    return lax.dot_general(
        left, right, (((left_dim,), (right_dim,)), ((), ())), preferred_element_type=F32
    ).astype(BF16)


def paired_device(
    layer_input, document_ids, cotangent, attention_gain, query_weight, key_weight, value_weight, output_weight,
    feedforward_gain, gate_weight, up_weight, down_weight,
):
    place = Place()
    x_own, dy_own = layer_input[0], cotangent[0]
    tok_count, model = x_own.shape
    block_rows = tok_count // 2
    length = document_ids.shape[1]
    block_count = length // block_rows
    rows = query_weight.shape[0]
    hidden_rows = down_weight.shape[0]

    attn_gain = attention_gain.astype(F32)[:, None]
    ff_gain = feedforward_gain.astype(F32)[:, None]

    mine, sent = head_slices(place, [query_weight, key_weight, value_weight], attn_gain, rows)
    out_half = chip_half(place, output_weight)
    (a_own,) = on_rows(open_kernel, "open_layer", [x_own], [BF16])
    dy_l = swap(dy_own, "zl")
    mine, sent, out_half, a_own, down_late, gate_late, up_late = fence(
        [mine, sent, out_half, a_own, down_weight, gate_weight, up_weight], []
    )

    received = swap(sent, "x")
    out_zh, out_zl = swap(out_half, "zh"), swap(out_half, "zl")
    qkv = in_order(mine, received, place.x)
    down_half = chip_half(place, down_late)
    quarter = down_half.shape[0] // 2
    qkv, a_late, out_zh, out_zl, dy_late, down_half, dy_l = fence(
        [qkv, a_own, out_zh, out_zl, dy_own, down_half, dy_l], []
    )

    gate_up = hidden_slices(place, [gate_late, up_late], ff_gain, hidden_rows)
    by_zh, by_zl = swap(qkv, "zh"), swap(qkv, "zl")
    a_x, a_s = along(a_late)
    out_both = swap(out_zh, "zl")
    by_zh, by_zl, a_x, a_s, dy_late, out_both, gate_up, document_ids, down_half = fence(
        [by_zh, by_zl, a_x, a_s, dy_late, out_both, gate_up, document_ids, down_half], []
    )

    by_both = swap(by_zh, "zl")
    dy_x, dy_s = along(dy_late)
    a_o = opposite(a_x, a_s)
    out_half = in_order(
        in_order(out_half, out_zl, place.zl), in_order(out_zh, out_both, place.zl), place.zh
    ).reshape(4, -1, model)
    documents = document_ids[0]
    first = jnp.sum((documents[None, :] < documents[:, None]).astype(jnp.int32), axis=1)
    qkv = in_order(in_order(qkv, by_zl, place.zl), in_order(by_zh, by_both, place.zl), place.zh)
    first = jnp.stack([first, swap(first, "seq")])
    down_far = [swap(down_half[:quarter], "zh")]
    a_all = jnp.concatenate([a_own, a_x, a_s, *a_o], axis=0)

    def positions(dx, dc):
        holder = (place.x ^ dx) * 2 + (place.core ^ dc)
        return place_of(holder, jnp.arange(tok_count, dtype=jnp.int32), block_rows, block_count // 2)

    qpos = jnp.concatenate([positions(0, 0), positions(1, 0)])
    kpos = jnp.concatenate([positions(0, 0), positions(1, 0), positions(0, 1), positions(1, 1)])
    cosine, sine = rotation(qpos, HEAD_DIM)
    cosine = jnp.concatenate([cosine] * 4, axis=1)
    sine = jnp.concatenate([-sine, sine] * 2, axis=1)
    firsts = first.reshape(2, block_count, block_rows)
    starts = []
    for dx in range(2):
        holder = (place.x ^ dx) * 2 + place.core
        for index in (holder, block_count - 1 - holder):
            starts.append(lax.dynamic_index_in_dim(firsts, index, 1, False))
    start = jnp.concatenate(starts, axis=1)[:, :, None]
    where = (qpos[:, None], start, kpos[None, :])
    tables = (cosine, sine)
    qkv, dy_x, dy_s, dy_l, tables, a_all, down_half, out_half, down_far, gate_up = fence(
        [qkv, dy_x, dy_s, dy_l, tables, a_all, down_half, out_half, down_far, gate_up], []
    )

    qkv = qkv.reshape(model // 2, -1)
    qkv_other = swap(qkv, "core")
    gate_up = share_columns(gate_up)
    dy_ls = swap(dy_l, "seq")
    dy_o = opposite(dy_x, dy_s)
    out_rows = chip_rows(place, out_half, swap(out_half, "core"))
    core = jnp.stack([place.core]).astype(jnp.int32)
    down_far += [swap(down_half[quarter:], "zh")]
    qkv, qkv_other, core, dy_l = fence([qkv, qkv_other, core, dy_l], [])

    q_all, kv_all = project(core, a_all, qkv, qkv_other, *tables)
    q_all, kv_all, down_half, down_far, dy_o, dy_ls, dy_l, where, gate_up = fence(
        [q_all, kv_all, down_half, down_far, dy_o, dy_ls, dy_l, where, gate_up], [out_rows]
    )

    gate_up = lax.all_gather(gate_up, ("core", "zh"), axis=0, tiled=True).reshape(model, -1)
    dy_lx = swap(dy_l, "x")
    kv_other = swap(kv_all, "core")
    o_all, term_s, *term_o = attend(1, q_all, kv_all, kv_other, out_rows, where, None)
    down_half = in_order(down_half, jnp.concatenate(down_far), place.zh)
    down_rows = chip_rows(place, down_half, swap(down_half, "core"))
    term_s, term_o, o_all, down_rows, dy_lx = fence([term_s, term_o, o_all, down_rows, dy_lx], [])

    o_all, own, term_x = attend(0, q_all, kv_all, kv_other, out_rows, where, o_all)
    halves = return_halves(*term_o)
    own, term_x, halves, dy_lx, dy_ls = fence([own, term_x, halves, dy_lx, dy_ls], [])

    sums = return_along(term_x, term_s, *halves)
    hidden, b_own = on_rows(close_attention_kernel, "close_attention", [x_own, own, *sums], [F32, BF16])
    b_own, dy_lx, dy_ls = fence([b_own, dy_lx, dy_ls], [])

    b_x, b_s = along(b_own)
    b_l = swap(b_own, "zl")
    dy_lo = opposite(dy_lx, dy_ls)
    b_x, b_s = fence([b_x, b_s], dy_lo)

    b_o = opposite(b_x, b_s)
    buffers, db0, y0 = hidden_units(0, [b_own, b_x], [dy_own, dy_x], gate_up, down_rows, [None] * 4)
    buffers, b_o, b_l = fence([buffers, b_o, b_l], [])

    b_lx, b_ls = along(b_l)
    buffers, db1, y1 = hidden_units(1, [b_s, *b_o], [dy_s, *dy_o], gate_up, down_rows, buffers)
    buffers, b_lx, b_ls, db1 = fence([buffers, b_lx, b_ls, db1], [])

    b_lo = opposite(b_lx, b_ls)
    near_halves = return_halves(*db1[1:])
    buffers, db2, y2 = hidden_units(2, [b_l, b_lx], [dy_l, dy_lx], gate_up, down_rows, buffers)
    buffers, b_lo, near_halves = fence([buffers, b_lo, near_halves], [])

    near_along = return_along(db0[1], db1[0], *near_halves)
    buffers, db3, y3 = hidden_units(3, [b_ls, *b_lo], [dy_ls, *dy_lo], gate_up, down_rows, buffers)
    z_all, d_all, b_all, dy_all = buffers
    db3, z_all, d_all, near_along = fence([db3, z_all, d_all, near_along], [])

    far_halves = return_halves(*db3[1:])
    down_terms = dot_low(z_all, dy_all, 0, 0)
    d_all, down_terms, far_halves = fence([d_all, down_terms, far_halves], [])

    far_along = return_along(db2[1], db3[0], *far_halves)
    gate_up_terms = dot_low(b_all, d_all, 0, 0)
    down_sums = add_core(place, down_terms.reshape(2, 2, -1, model), 1)
    gate_up_terms, down_sums, y1, near0, far_along = fence([gate_up_terms, down_sums, y1, db0[0], far_along], [])

    down_total = lax.psum_scatter(down_sums, "zh", scatter_dimension=0, tiled=True)[0]
    across = return_across(db2[0], *far_along)
    near_y_halves = return_halves(*y1[1:])
    gate_up_sums = add_core(place, gate_up_terms.reshape(2, 2, 4, rows, -1), 0)
    dh, dh_low = on_rows(
        close_hidden_kernel, "close_hidden", [dy_own, hidden, near0, *near_along, across], [F32, BF16]
    )
    dh_low, gate_up_sums, near_y_halves = fence([dh_low, gate_up_sums, near_y_halves], [])

    gate_up_near = lax.psum_scatter(gate_up_sums, "zh", scatter_dimension=0, tiled=True)[0]
    dh_x, dh_s = along(dh_low)
    dh_x, dh_s, y0, y1, y3 = fence([dh_x, dh_s, y0, y1, y3], [])

    dh_o = opposite(dh_x, dh_s)
    dh_all, dq0, dkv0, dkv_other0 = attend_back(
        0, [dh_low, dh_x], out_rows, q_all, kv_all, kv_other, where, tables, None
    )
    near_y_along = return_along(y0[1], y1[0], *near_y_halves)
    dkv_other0, dh_s, y3 = fence([dkv_other0, dh_s, y3], dh_o)

    dkv_other0 = swap(dkv_other0, "core")
    down_other = swap(down_total, "seq")
    dh_all, dq1, dkv1, dkv_other1 = attend_back(
        1, [dh_s, *dh_o], out_rows, q_all, kv_all, kv_other, where, tables, dh_all
    )
    far_y_halves = return_halves(*y3[1:])
    dkv_other1, dh_all = fence([dkv_other1, dh_all], near_y_along)

    dkv_other1 = swap(dkv_other1, "core")
    d_qkv = join_grads(0, dq0, dkv0, dkv_other0, tables, None)
    out_terms = dot_low(o_all, dh_all, 0, 0)
    d_qkv, dkv_other1, out_terms, far_y_halves, down_other = fence(
        [d_qkv, dkv_other1, out_terms, far_y_halves, down_other], []
    )

    d_qkv = join_grads(1, dq1, dkv1, dkv_other1, tables, d_qkv)
    qkv_terms = dot_low(a_all, d_qkv, 0, 0)
    far_y_along = return_along(y2[1], y3[0], *far_y_halves)
    out_sums = add_core(place, out_terms.reshape(4, 2, -1, model), 1).reshape(2, 2, -1, model)
    qkv_terms, out_sums, d_qkv = fence([qkv_terms, out_sums, d_qkv], [])

    def part(sums, zh, zl):
        return lax.dynamic_slice(sums, (place.zh ^ zh, place.zl ^ zl, 0, 0), (1, 1, *sums.shape[2:]))[0, 0]

    qkv_sums = add_core(place, qkv_terms.reshape(2, 2, 2, 2 * rows, -1), 0)
    own, term_x, term_s, *term_o = input_terms(core, d_qkv, [qkv, qkv_other])
    out_zl = swap(part(out_sums, 1, 1), "zl")
    qkv_sums, out_sums, out_zl, term_o, far_y_along, gate_up_near = fence(
        [qkv_sums, out_sums, out_zl, term_o, far_y_along, gate_up_near], []
    )

    qkv_zl = swap(part(qkv_sums, 1, 1), "zl")
    gate_up_near = share_columns(gate_up_near)
    sums = return_along(term_x, term_s, *return_halves(*term_o))
    out_zh = swap(add_low(part(out_sums, 1, 0), out_zl).astype(BF16), "zh")
    out_zl = swap(part(out_sums, 0, 1), "zl")
    down_grad = own_rows(place, down_total, down_other)
    qkv_zl, gate_up_near, sums = fence([qkv_zl, gate_up_near, sums], [down_grad])

    qkv_zh = swap(add_low(part(qkv_sums, 1, 0), qkv_zl).astype(BF16), "zh")
    qkv_zl = swap(part(qkv_sums, 0, 1), "zl")
    gate_up_far = swap(gate_up_near, "seq")
    (input_grad,) = on_rows(close_input_kernel, "close_input", [x_own, dh, own, *sums], [BF16])
    qkv_zh, qkv_zl, out_zh, out_zl = fence([qkv_zh, qkv_zl, out_zh, out_zl], [input_grad])

    qkv_total = add_low(part(qkv_sums, 0, 0), qkv_zl, qkv_zh).astype(BF16).reshape(2, rows, -1)
    kept = lax.dynamic_index_in_dim(qkv_total, place.x, 0, False)
    received = swap(lax.dynamic_index_in_dim(qkv_total, 1 - place.x, 0, False), "x")
    kept_far, received_far = swap(kept, "seq"), swap(received, "seq")
    y_across = return_across(y2[0], *far_y_along)
    out_total = add_low(part(out_sums, 0, 0), out_zl, out_zh).astype(BF16)
    kept, kept_far, received, received_far, gate_up_far, out_total = fence(
        [kept, kept_far, received, received_far, gate_up_far, out_total], []
    )

    out_other = swap(out_total, "seq")
    output_grad = own_rows(place, out_total, out_other)

    layer_output = add_low(hidden, y0[0], *near_y_along, y_across).astype(BF16)
    pieces = in_order(in_order(kept, received, place.x), in_order(kept_far, received_far, place.x), place.seq)
    (query_grad, key_grad, value_grad), attn_gain_grad = finish_columns(
        pieces, [query_weight, key_weight, value_weight], attn_gain, rows, False
    )
    (gate_grad, up_grad), ff_gain_grad = finish_columns(
        in_order(gate_up_near, gate_up_far, place.seq), [gate_weight, up_weight], ff_gain, hidden_rows, True
    )
    return (
        layer_output[None], input_grad[None], attn_gain_grad, query_grad, key_grad, value_grad, output_grad,
        ff_gain_grad, gate_grad, up_grad, down_grad,
    )


def paired(mesh):
    fine = Mesh(mesh.devices.reshape(2, 2, 2, 2, 2), ("seq", "x", "core", "zh", "zl"))
    tokens = P(("seq", "zh", "zl"), ("x", "core"), None)
    matrix, vector = P(("x", "core", "zh", "zl"), None), P(("x", "core", "zh", "zl"))
    return jax.shard_map(
        paired_device,
        mesh=fine,
        in_specs=(tokens, P(("seq", "zh", "zl"), None), tokens, vector) + (matrix,) * 4 + (vector,) + (matrix,) * 3,
        out_specs=(tokens, tokens, vector) + (matrix,) * 4 + (vector,) + (matrix,) * 3,
        check_vma=False,
    )


def solution(mesh):
    if tuple(mesh.shape[axis] for axis in ("seq", "ctx", "fsdp")) == (2, 4, 4):
        return paired(mesh)
    return gathered(mesh)
```

```python
import functools
import math

import jax
import jax.numpy as jnp
from jax import lax
from jax.experimental import pallas as pl
from jax.experimental.pallas import tpu as pltpu
from jax.sharding import Mesh, PartitionSpec as P

HEADS = 32
HEAD_DIM = 64


epsilon = 1e-05
rotary_base = 130000.0
masked_score = -1e30


def norm_scale(values, gain):
    inverse = lax.rsqrt(jnp.mean(values * values, axis=-1, keepdims=True) + epsilon)
    return values * inverse * gain


def rotation(positions, head_size):
    half_dim = head_size // 2
    frequency = rotary_base ** (-(jnp.arange(half_dim, dtype=jnp.float32) * 2.0) / head_size)
    angles = positions.astype(jnp.float32)[:, None] * frequency[None, :]
    return (jnp.cos(angles), jnp.sin(angles))


def rotate(values, cosine, sine_table):
    half_dim = values.shape[-1] // 2
    front_part = values[..., :half_dim]
    second = values[..., half_dim:]
    cos_wide = cosine[:, None, :]
    sin_wide = sine_table[:, None, :]
    return jnp.concatenate(
        [front_part * cos_wide - second * sin_wide, second * cos_wide + front_part * sin_wide],
        axis=-1,
    )


def place_of(holder, offset, block_rows, ctx_count):
    return jnp.where(
        offset < block_rows,
        holder * block_rows + offset,
        (2 * ctx_count - 1 - holder) * block_rows + offset - block_rows,
    )


def per_device(
    layer_input,
    document_ids,
    cotangent,
    attention_gain,
    query_weight,
    key_weight,
    value_weight,
    output_weight,
    feedforward_gain,
    gate_weight,
    up_weight,
    down_weight,
):
    ctx_count = lax.axis_size("ctx")
    device = lax.axis_index("ctx")
    inputs = layer_input[0].astype(jnp.float32)
    upstream = cotangent[0]
    tok_count = inputs.shape[0]
    model_width = inputs.shape[1]
    block_rows = tok_count // 2
    group_heads = math.gcd(8, HEADS)
    group_count = HEADS // group_heads
    group_width = group_heads * HEAD_DIM
    key_count = ctx_count * tok_count
    local_pos = place_of(device, jnp.arange(tok_count, dtype=jnp.int32), block_rows, ctx_count)
    key_index = jnp.arange(key_count, dtype=jnp.int32)
    key_pos = place_of(key_index // tok_count, key_index % tok_count, block_rows, ctx_count)
    documents = document_ids[0]
    same_doc = jnp.take(documents, local_pos)[:, None] == jnp.take(documents, key_pos)[None, :]
    allowed = (key_pos[None, :] <= local_pos[:, None]) & same_doc
    cosine, sine_table = rotation(local_pos, HEAD_DIM)
    attention_set = (
        lax.all_gather(attention_gain, ("ctx", "fsdp"), axis=0, tiled=True),
        lax.all_gather(query_weight, ("ctx", "fsdp"), axis=0, tiled=True),
        lax.all_gather(key_weight, ("ctx", "fsdp"), axis=0, tiled=True),
        lax.all_gather(value_weight, ("ctx", "fsdp"), axis=0, tiled=True),
        lax.all_gather(output_weight, ("ctx", "fsdp"), axis=0, tiled=True),
    )
    attn_gain_full = attention_set[0].astype(jnp.float32)
    normed_low = norm_scale(inputs, attn_gain_full).astype(jnp.bfloat16)
    query_pre = jnp.dot(normed_low, attention_set[1], preferred_element_type=jnp.float32)
    key_pre = jnp.dot(normed_low, attention_set[2], preferred_element_type=jnp.float32)
    value_pre = jnp.dot(normed_low, attention_set[3], preferred_element_type=jnp.float32)
    queries = (
        rotate(query_pre.reshape(tok_count, HEADS, HEAD_DIM), cosine, sine_table)
        .reshape(tok_count, model_width)
        .astype(jnp.bfloat16)
    )
    keys_local = (
        rotate(key_pre.reshape(tok_count, HEADS, HEAD_DIM), cosine, sine_table)
        .reshape(tok_count, model_width)
        .astype(jnp.bfloat16)
    )
    values_local = value_pre.astype(jnp.bfloat16)
    all_keys, all_values = (
        lax.all_gather(keys_local, "ctx", axis=0, tiled=True),
        lax.all_gather(values_local, "ctx", axis=0, tiled=True),
    )

    def group_parts(group_index):
        column_start = group_index * group_width
        query_part = lax.dynamic_slice_in_dim(queries, column_start, group_width, 1).reshape(
            tok_count, group_heads, HEAD_DIM
        )
        key_part = lax.dynamic_slice_in_dim(all_keys, column_start, group_width, 1).reshape(
            key_count, group_heads, HEAD_DIM
        )
        value_part = lax.dynamic_slice_in_dim(all_values, column_start, group_width, 1).reshape(
            key_count, group_heads, HEAD_DIM
        )
        scores = (
            jnp.einsum("qhd,khd->hqk", query_part, key_part, preferred_element_type=jnp.float32)
            * 0.125
        )
        scores = jnp.where(allowed[None], scores, masked_score)
        return (query_part, key_part, value_part, scores)

    def group_forward(group_index):
        query_part, key_part, value_part, scores = group_parts(group_index)
        row_peak = jnp.max(scores, axis=-1, keepdims=True)
        exponent = jnp.exp(scores - row_peak)
        row_total = jnp.sum(exponent, axis=-1, keepdims=True)
        softmax_weights = exponent / row_total
        log_total = row_peak[..., 0] + jnp.log(row_total[..., 0])
        attended = jnp.einsum(
            "hqk,khd->qhd",
            softmax_weights.astype(jnp.bfloat16),
            value_part,
            preferred_element_type=jnp.float32,
        )
        return (attended.reshape(tok_count, group_width), log_total)

    group_index_all = jnp.arange(group_count, dtype=jnp.int32)
    attended_groups, log_totals = lax.map(group_forward, group_index_all)
    attended_low = (
        jnp.transpose(attended_groups, (1, 0, 2))
        .reshape(tok_count, model_width)
        .astype(jnp.bfloat16)
    )
    hidden = inputs + jnp.dot(attended_low, attention_set[4], preferred_element_type=jnp.float32)
    feedforward_set = (
        lax.all_gather(feedforward_gain, ("ctx", "fsdp"), axis=0, tiled=True),
        lax.all_gather(gate_weight, ("ctx", "fsdp"), axis=0, tiled=True),
        lax.all_gather(up_weight, ("ctx", "fsdp"), axis=0, tiled=True),
        lax.all_gather(down_weight, ("ctx", "fsdp"), axis=0, tiled=True),
    )
    mlp_low = norm_scale(hidden, feedforward_set[0].astype(jnp.float32)).astype(jnp.bfloat16)
    gate_pre = jnp.dot(mlp_low, feedforward_set[1], preferred_element_type=jnp.float32)
    up_pre = jnp.dot(mlp_low, feedforward_set[2], preferred_element_type=jnp.float32)
    product_low = (jax.nn.silu(gate_pre) * up_pre).astype(jnp.bfloat16)
    layer_output = (
        hidden + jnp.dot(product_low, feedforward_set[3], preferred_element_type=jnp.float32)
    ).astype(jnp.bfloat16)
    feedforward_back = (
        lax.all_gather(feedforward_gain, ("ctx", "fsdp"), axis=0, tiled=True),
        lax.all_gather(gate_weight, ("ctx", "fsdp"), axis=0, tiled=True),
        lax.all_gather(up_weight, ("ctx", "fsdp"), axis=0, tiled=True),
        lax.all_gather(down_weight, ("ctx", "fsdp"), axis=0, tiled=True),
    )
    attention_back = (
        lax.all_gather(attention_gain, ("ctx", "fsdp"), axis=0, tiled=True),
        lax.all_gather(query_weight, ("ctx", "fsdp"), axis=0, tiled=True),
        lax.all_gather(key_weight, ("ctx", "fsdp"), axis=0, tiled=True),
        lax.all_gather(value_weight, ("ctx", "fsdp"), axis=0, tiled=True),
        lax.all_gather(output_weight, ("ctx", "fsdp"), axis=0, tiled=True),
    )
    piece = product_low
    down_shard = lax.psum_scatter(
        jnp.einsum("tf,td->fd", piece, upstream, preferred_element_type=jnp.float32),
        ("ctx", "fsdp"),
        scatter_dimension=0,
        tiled=True,
    )
    product_grad = jnp.einsum(
        "td,fd->tf", upstream, feedforward_back[3], preferred_element_type=jnp.float32
    )
    silu_out, silu_pullback = jax.vjp(
        lambda gate_in, up_in: jax.nn.silu(gate_in) * up_in, gate_pre, up_pre
    )
    gate_grad, up_grad = silu_pullback(product_grad)
    gate_grad_low = gate_grad.astype(jnp.bfloat16)
    up_grad_low = up_grad.astype(jnp.bfloat16)
    joined_grads = jnp.concatenate([gate_grad_low, up_grad_low], axis=1)
    piece = mlp_low
    joined_shard = lax.psum_scatter(
        jnp.einsum("td,tf->df", piece, joined_grads, preferred_element_type=jnp.float32),
        ("ctx", "fsdp"),
        scatter_dimension=0,
        tiled=True,
    )
    ff_width = gate_weight.shape[1]
    gate_shard = joined_shard[:, :ff_width]
    up_shard = joined_shard[:, ff_width:]
    mlp_normed_grad = jnp.einsum(
        "tf,df->td", gate_grad_low, feedforward_back[1], preferred_element_type=jnp.float32
    )
    mlp_normed_grad = mlp_normed_grad + jnp.einsum(
        "tf,df->td", up_grad_low, feedforward_back[2], preferred_element_type=jnp.float32
    )
    mlp_norm_out, mlp_norm_pullback = jax.vjp(
        norm_scale, hidden, feedforward_back[0].astype(jnp.float32)
    )
    hidden_from_norm, ff_gain_term = mlp_norm_pullback(mlp_normed_grad)
    hidden_grad = upstream.astype(jnp.float32) + hidden_from_norm
    hidden_low = hidden_grad.astype(jnp.bfloat16)
    output_term = jnp.einsum(
        "td,te->de", attended_low, hidden_low, preferred_element_type=jnp.float32
    )
    attended_grad_low = jnp.einsum(
        "te,de->td", hidden_low, attention_back[4], preferred_element_type=jnp.float32
    ).astype(jnp.bfloat16)

    def group_backward(operands):
        group_index, log_total = operands
        query_part, key_part, value_part, scores = group_parts(group_index)
        softmax_weights = jnp.exp(scores - log_total[:, :, None])
        column_start = group_index * group_width
        grad_part = lax.dynamic_slice_in_dim(
            attended_grad_low, column_start, group_width, 1
        ).reshape(tok_count, group_heads, HEAD_DIM)
        value_grad = jnp.einsum(
            "hqk,qhd->khd",
            softmax_weights.astype(jnp.bfloat16),
            grad_part,
            preferred_element_type=jnp.float32,
        )
        weight_grad = jnp.einsum(
            "qhd,khd->hqk", grad_part, value_part, preferred_element_type=jnp.float32
        )
        row_inner = jnp.sum(weight_grad * softmax_weights, axis=-1, keepdims=True)
        score_grad = (softmax_weights * (weight_grad - row_inner)).astype(jnp.bfloat16)
        query_grad = (
            jnp.einsum("hqk,khd->qhd", score_grad, key_part, preferred_element_type=jnp.float32)
            * 0.125
        )
        key_grad = (
            jnp.einsum("hqk,qhd->khd", score_grad, query_part, preferred_element_type=jnp.float32)
            * 0.125
        )
        return (
            query_grad.reshape(tok_count, group_width),
            key_grad.reshape(key_count, group_width),
            value_grad.reshape(key_count, group_width),
        )

    query_groups, key_groups, value_groups = lax.map(group_backward, (group_index_all, log_totals))
    query_grad_all = jnp.transpose(query_groups, (1, 0, 2)).reshape(tok_count, model_width)
    key_grad_all = jnp.transpose(key_groups, (1, 0, 2)).reshape(key_count, model_width)
    value_grad_all = jnp.transpose(value_groups, (1, 0, 2)).reshape(key_count, model_width)
    key_grad_local, value_grad_local = (
        lax.psum_scatter(
            key_grad_all.astype(jnp.bfloat16), "ctx", scatter_dimension=0, tiled=True
        ).astype(jnp.float32),
        lax.psum_scatter(
            value_grad_all.astype(jnp.bfloat16), "ctx", scatter_dimension=0, tiled=True
        ).astype(jnp.float32),
    )
    negative_sine = -sine_table
    query_pre_grad = (
        rotate(query_grad_all.reshape(tok_count, HEADS, HEAD_DIM), cosine, negative_sine)
        .reshape(tok_count, model_width)
        .astype(jnp.bfloat16)
    )
    key_pre_grad = (
        rotate(key_grad_local.reshape(tok_count, HEADS, HEAD_DIM), cosine, negative_sine)
        .reshape(tok_count, model_width)
        .astype(jnp.bfloat16)
    )
    value_pre_grad = value_grad_local.astype(jnp.bfloat16)
    query_term = jnp.einsum(
        "td,te->de", normed_low, query_pre_grad, preferred_element_type=jnp.float32
    )
    key_term = jnp.einsum("td,te->de", normed_low, key_pre_grad, preferred_element_type=jnp.float32)
    value_term = jnp.einsum(
        "td,te->de", normed_low, value_pre_grad, preferred_element_type=jnp.float32
    )
    attn_normed_grad = jnp.einsum(
        "te,de->td", query_pre_grad, attention_back[1], preferred_element_type=jnp.float32
    )
    attn_normed_grad = attn_normed_grad + jnp.einsum(
        "te,de->td", key_pre_grad, attention_back[2], preferred_element_type=jnp.float32
    )
    attn_normed_grad = attn_normed_grad + jnp.einsum(
        "te,de->td", value_pre_grad, attention_back[3], preferred_element_type=jnp.float32
    )
    attn_norm_out, attn_norm_pullback = jax.vjp(
        norm_scale, inputs, attention_back[0].astype(jnp.float32)
    )
    inputs_from_norm, attn_gain_term = attn_norm_pullback(attn_normed_grad)
    input_grad = (hidden_grad + inputs_from_norm).astype(jnp.bfloat16)
    attn_shards = (
        lax.psum_scatter(attn_gain_term, ("ctx", "fsdp"), scatter_dimension=0, tiled=True),
        lax.psum_scatter(ff_gain_term, ("ctx", "fsdp"), scatter_dimension=0, tiled=True),
        lax.psum_scatter(query_term, ("ctx", "fsdp"), scatter_dimension=0, tiled=True),
        lax.psum_scatter(key_term, ("ctx", "fsdp"), scatter_dimension=0, tiled=True),
        lax.psum_scatter(value_term, ("ctx", "fsdp"), scatter_dimension=0, tiled=True),
        lax.psum_scatter(output_term, ("ctx", "fsdp"), scatter_dimension=0, tiled=True),
    )
    summed = (
        lax.psum(attn_shards[0].astype(jnp.bfloat16), "seq").astype(jnp.float32),
        lax.psum(attn_shards[2].astype(jnp.bfloat16), "seq").astype(jnp.float32),
        lax.psum(attn_shards[3].astype(jnp.bfloat16), "seq").astype(jnp.float32),
        lax.psum(attn_shards[4].astype(jnp.bfloat16), "seq").astype(jnp.float32),
        lax.psum(attn_shards[5].astype(jnp.bfloat16), "seq").astype(jnp.float32),
        lax.psum(attn_shards[1].astype(jnp.bfloat16), "seq").astype(jnp.float32),
        lax.psum(gate_shard.astype(jnp.bfloat16), "seq").astype(jnp.float32),
        lax.psum(up_shard.astype(jnp.bfloat16), "seq").astype(jnp.float32),
        lax.psum(down_shard.astype(jnp.bfloat16), "seq").astype(jnp.float32),
    )
    return (
        layer_output[None],
        input_grad[None],
        summed[0],
        summed[1],
        summed[2],
        summed[3],
        summed[4],
        summed[5],
        summed[6],
        summed[7],
        summed[8],
    )


def gathered(mesh):
    return jax.shard_map(
        per_device,
        mesh=mesh,
        in_specs=(
            P(("seq", "fsdp"), "ctx", None),
            P(("seq", "fsdp"), None),
            P(("seq", "fsdp"), "ctx", None),
            P(("ctx", "fsdp")),
            P(("ctx", "fsdp"), None),
            P(("ctx", "fsdp"), None),
            P(("ctx", "fsdp"), None),
            P(("ctx", "fsdp"), None),
            P(("ctx", "fsdp")),
            P(("ctx", "fsdp"), None),
            P(("ctx", "fsdp"), None),
            P(("ctx", "fsdp"), None),
        ),
        out_specs=(
            P(("seq", "fsdp"), "ctx", None),
            P(("seq", "fsdp"), "ctx", None),
            P(("ctx", "fsdp")),
            P(("ctx", "fsdp"), None),
            P(("ctx", "fsdp"), None),
            P(("ctx", "fsdp"), None),
            P(("ctx", "fsdp"), None),
            P(("ctx", "fsdp")),
            P(("ctx", "fsdp"), None),
            P(("ctx", "fsdp"), None),
            P(("ctx", "fsdp"), None),
        ),
        check_vma=False,
    )


HIDDEN_PIECES = 2
BIG = pltpu.CompilerParams(vmem_limit_bytes=56 * 1024 * 1024)
BF16 = jnp.bfloat16
F32 = jnp.float32


def swap(value, axis):
    return lax.ppermute(value, axis, [(0, 1), (1, 0)])


def fence(late, early):
    return list(lax.optimization_barrier((tuple(late), tuple(early)))[0])


def opposite(along_x, along_seq):
    half = along_x.shape[0] // 2
    return [swap(along_seq[:half], "x"), swap(along_x[half:], "seq")]


def along(block):
    return [swap(block, "x"), swap(block, "seq")]


def add_low(first, *others):
    total = first.astype(F32)
    for other in others:
        total = total + other.astype(F32)
    return total


def return_halves(upper, lower):
    return [swap(upper, "x"), swap(lower, "seq")]


def return_along(to_x, to_seq, by_x, by_seq):
    half = to_x.shape[0] // 2
    to_seq = jnp.concatenate([add_low(to_seq[:half], by_x).astype(BF16), to_seq[half:]], axis=0)
    to_x = jnp.concatenate([to_x[:half], add_low(to_x[half:], by_seq).astype(BF16)], axis=0)
    return [swap(to_x, "x"), swap(to_seq, "seq")]


def return_across(own, by_x, by_seq):
    return swap(add_low(own, by_x, by_seq).astype(BF16), "zl")


def in_order(mine, other, place):
    first = place == 0
    return jnp.stack([jnp.where(first, mine, other), jnp.where(first, other, mine)])


def pair_up(mine, axis):
    return in_order(mine, swap(mine, axis), lax.axis_index(axis))


def slot(count, blocks, joined, w, block):
    return block * count + w if joined else w * blocks + block


def slices_kernel(count, blocks, joined, table_ref, *refs):
    gain, out = refs[-2][...], refs[-1]
    width = refs[0].shape[1]
    for w in range(count):
        for block in range(blocks):
            at = slot(count, blocks, joined, w, block) * width
            out[0, :, at : at + width] = (refs[blocks * w + block][...].astype(F32) * gain).astype(BF16)


def column_slices(table, chips, blocks, column, weights, gain, width, joined):
    rows = weights[0].shape[0]

    def column_spec(block):
        return pl.BlockSpec((rows, width), lambda t, table: (0, column(t, block, table)))

    wide = blocks * width * len(weights)
    return pl.pallas_call(
        functools.partial(slices_kernel, len(weights), blocks, joined),
        grid_spec=pltpu.PrefetchScalarGridSpec(
            num_scalar_prefetch=1,
            grid=(chips,),
            in_specs=[column_spec(block) for _ in weights for block in range(blocks)]
            + [pl.BlockSpec((rows, 1), lambda t, table: (0, 0))],
            out_specs=pl.BlockSpec((1, rows, wide), lambda t, table: (t, 0, 0)),
        ),
        out_shape=jax.ShapeDtypeStruct((chips, rows, wide), BF16),
        compiler_params=BIG,
        cost_estimate=pl.CostEstimate(flops=0, bytes_accessed=1_000_000, transcendentals=0),
        name="column_slices",
    )(table, *[w for w in weights for _ in range(blocks)], gain)


def hidden_slices(place, weights, gain, width):
    def column(t, zh, table):
        return (((t % 2) * 2 + table[0]) * 2 + zh) * 2 + t // 2

    table = jnp.stack([place.seq]).astype(jnp.int32)
    return column_slices(table, 4, 2, column, weights, gain, width, True)


def head_slices(place, weights, gain, width):
    def column(t, z, table):
        return ((table[1] + t - 2 * table[1] * t) * 2 + table[0]) * 4 + z

    table = jnp.stack([place.seq, place.x]).astype(jnp.int32)
    return column_slices(table, 2, 4, column, weights, gain, width, False)


def share_columns(slices):
    return lax.all_to_all(slices, ("zl", "x"), split_axis=0, concat_axis=0, tiled=True)


def chip_half(place, weight):
    half = weight.shape[0] // 2
    moved = lax.ppermute(
        lax.dynamic_slice_in_dim(weight, (1 - place.core) * half, half, 0), ("seq", "core"), [(0, 1), (3, 2)]
    )
    own = lax.dynamic_slice_in_dim(weight, place.core * half, half, 0)
    return jnp.where(place.core == place.seq, own, moved)


def chip_rows(place, mine, other):
    first = place.core == 0
    halves = jnp.stack([jnp.where(first, mine, other), jnp.where(first, other, mine)], axis=1)
    return halves.reshape(-1, mine.shape[-1])


def add_core(place, parts, axis):
    received = swap(lax.dynamic_index_in_dim(parts, 1 - place.core, axis, False), "core")
    return add_low(lax.dynamic_index_in_dim(parts, place.core, axis, False), received).astype(BF16)


def to_far(place, sums):
    return lax.dynamic_index_in_dim(sums, 1 - place.zh, 0, False)


def add_far(place, sums, received):
    return add_low(lax.dynamic_index_in_dim(sums, place.zh, 0, False), received).astype(BF16)


def own_rows(place, total, other):
    mine = place.core == place.seq
    received = swap(jnp.where(mine, other, total), "core")
    kept = jnp.where(mine, total, other)
    first = place.core == 0
    return jnp.concatenate([jnp.where(first, kept, received), jnp.where(first, received, kept)]).astype(F32)


def finish_kernel(count, seq_ref, *refs):
    near, far, weights = refs[:count], refs[count : 2 * count], refs[2 * count : 3 * count]
    gain, outs = refs[3 * count], refs[3 * count + 1 :]
    j = pl.program_id(0)
    use_near = (j // 2) % 2 == seq_ref[0]
    total = None
    for i in range(count):
        grad = jnp.where(use_near, near[i][...], far[i][...]).astype(F32)
        pieces = [grad[k, 0] for k in range(2)] if grad.ndim == 4 else [grad[0]]
        grad = jnp.concatenate(pieces, axis=1)
        outs[i][...] = grad * gain[...]
        term = grad * weights[i][...].astype(F32)
        total = term if total is None else total + term

    @pl.when(j == 0)
    def _():
        outs[count][...] = jnp.zeros_like(outs[count])

    outs[count][...] += total


def finish_columns(place, near, far, weights, gain, width, joined):
    count, rows = len(weights), weights[0].shape[0]

    def piece_spec(w):
        def index(j, seq):
            x, zh = j // 4, j % 2
            return (0, x, 0, slot(count, 2, joined, w, zh)) if joined else (x, 0, w * 2 + zh)

        return pl.BlockSpec((2, 1, rows, width) if joined else (1, rows, 2 * width), index)

    column_spec = pl.BlockSpec((rows, 2 * width), lambda j, seq: (0, j))
    pieces = [piece_spec(w) for w in range(count)]
    outs = pl.pallas_call(
        functools.partial(finish_kernel, count),
        grid_spec=pltpu.PrefetchScalarGridSpec(
            num_scalar_prefetch=1,
            grid=(8,),
            in_specs=pieces * 2 + [column_spec] * count + [pl.BlockSpec((rows, 1), lambda j, seq: (0, 0))],
            out_specs=[column_spec] * count + [pl.BlockSpec((rows, 2 * width), lambda j, seq: (0, 0))],
        ),
        out_shape=[jax.ShapeDtypeStruct((rows, 16 * width), F32)] * count
        + [jax.ShapeDtypeStruct((rows, 2 * width), F32)],
        compiler_params=BIG,
        cost_estimate=pl.CostEstimate(flops=0, bytes_accessed=1_000_000, transcendentals=0),
        name="finish_columns",
    )(jnp.stack([place.seq]).astype(jnp.int32), *[near] * count, *[far] * count, *weights, gain)
    return outs[:count], jnp.sum(outs[count], axis=1)


class Place:
    def __init__(self):
        self.seq = lax.axis_index("seq")
        self.x = lax.axis_index("x")
        self.core = lax.axis_index("core")
        self.zh = lax.axis_index("zh")
        self.zl = lax.axis_index("zl")


def block_columns(value, source):
    wide = value.shape[1] // 16
    return jnp.concatenate([value[:, i * wide : (i + 1) * wide] for i in source], axis=1)


def to_inner(value):
    return block_columns(value, [x * 8 + z for z in range(8) for x in (0, 1)])


def to_outer(value):
    return block_columns(value, [z * 2 + x for x in (0, 1) for z in range(8)])


def turn(value, cosine, sine):
    lane = lax.broadcasted_iota(jnp.int32, value.shape, 1)
    partner = jnp.where(lane % HEAD_DIM < HEAD_DIM // 2, pltpu.roll(value, 96, 1), pltpu.roll(value, 32, 1))
    return value * cosine + partner * sine


def project_kernel(core_ref, a_ref, a2_ref, w_ref, w2_ref, cos_ref, sin_ref, q_ref, kv_ref):
    joined = jnp.dot(a_ref[...], w_ref[...], preferred_element_type=F32)
    joined = joined + jnp.dot(a2_ref[...], w2_ref[...], preferred_element_type=F32)
    wide = q_ref.shape[1]
    cosine, sine = cos_ref[...], sin_ref[...]
    for i in range(wide // 128):
        at = slice(i * 128, (i + 1) * 128)
        q_ref[:, at] = turn(joined[:, at], cosine, sine).astype(BF16)
        kv_ref[:, at] = turn(joined[:, wide + i * 128 : wide + (i + 1) * 128], cosine, sine).astype(BF16)
    kv_ref[:, wide:] = joined[:, 2 * wide :].astype(BF16)


def whole_spec(array):
    return pl.BlockSpec(array.shape, lambda i: (0,) * array.ndim)


def project(core, a_all, weight, weight_other, cosine, sine):
    tokens, model = a_all.shape
    wide = weight.shape[1] // 3
    tile, half = cosine.shape[0], model // 2
    by_tile = lambda columns: pl.BlockSpec((tile, columns), lambda i, core: (i, 0))
    whole = lambda array: pl.BlockSpec(array.shape, lambda i, core: (0, 0))
    return pl.pallas_call(
        project_kernel,
        grid_spec=pltpu.PrefetchScalarGridSpec(
            num_scalar_prefetch=1,
            grid=(tokens // tile,),
            in_specs=[
                pl.BlockSpec((tile, half), lambda i, core: (i, core[0])),
                pl.BlockSpec((tile, half), lambda i, core: (i, 1 - core[0])),
                whole(weight), whole(weight_other), whole(cosine), whole(sine),
            ],
            out_specs=[by_tile(wide), by_tile(2 * wide)],
        ),
        out_shape=[jax.ShapeDtypeStruct((tokens, columns), BF16) for columns in (wide, 2 * wide)],
        compiler_params=BIG,
        cost_estimate=pl.CostEstimate(flops=0, bytes_accessed=1_000_000, transcendentals=0),
        name="project",
    )(core, a_all, a_all, weight, weight_other, cosine, sine)


def head_lanes(value, odd):
    lane = lax.broadcasted_iota(jnp.int32, value.shape, 1)
    return jnp.where((lane >= HEAD_DIM) == odd, value, jnp.zeros_like(value))


def probabilities(query, key, mask):
    scores = lax.dot_general(query, key, (((1,), (1,)), ((), ())), preferred_element_type=F32) * 0.125
    scores = jnp.where(mask, scores, masked_score)
    weights = jnp.exp(scores - jnp.max(scores, axis=-1, keepdims=True))
    return weights * (1.0 / jnp.sum(weights, axis=-1, keepdims=True))


def allowed_keys(qpos_ref, start_ref, kpos_ref):
    kpos = kpos_ref[...]
    return (kpos <= qpos_ref[...]) & (kpos >= start_ref[0])


def attend_kernel(q_ref, kv_ref, kv2_ref, out_ref, qpos_ref, start_ref, kpos_ref, o_ref, *term_refs):
    mask = allowed_keys(qpos_ref, start_ref, kpos_ref)
    wide = q_ref.shape[1]
    for pair in range(wide // 128):
        at = slice(pair * 128, (pair + 1) * 128)
        value_at = slice(wide + pair * 128, wide + (pair + 1) * 128)
        query = q_ref[:, at]
        key = jnp.concatenate([kv_ref[:, at], kv2_ref[:, at]], axis=0)
        value = jnp.concatenate([kv_ref[:, value_at], kv2_ref[:, value_at]], axis=0)
        total = None
        for odd in (False, True):
            weights = probabilities(head_lanes(query, odd), key, mask).astype(BF16)
            term = jnp.dot(weights, head_lanes(value, odd), preferred_element_type=F32)
            total = term if total is None else total + term
        o_ref[:, at] = total.astype(BF16)
    spill(term_refs, jnp.dot(o_ref[...], out_ref[...], preferred_element_type=F32).astype(BF16))


def fill(refs, target):
    at = 0
    for ref in refs:
        target[at : at + ref.shape[0]] = ref[...]
        at += ref.shape[0]


def spill(refs, value):
    at = 0
    for ref in refs:
        ref[...] = value[at : at + ref.shape[0]]
        at += ref.shape[0]


def at_step(step, action, refs, value):
    for k, group in enumerate((refs[:2], refs[2:])):

        @pl.when(step == k)
        def _(group=group):
            action(group, value)


def square_shapes(half, model):
    return [(half, model)] * 3 + [(half // 2, model)] * 2


def whole_shape(shape, **options):
    return pl.BlockSpec(shape, lambda i: (0, 0), **options)


def square_specs(half, model, **options):
    return [whole_shape(shape, **options) for shape in square_shapes(half, model)]


def sequence_shapes(sequence, half, model):
    return square_shapes(half, model)[2 * sequence : 2 + 3 * sequence]


def attend(sequence, q_all, kv_all, kv_other, out_rows, where, o_all):
    (tokens, wide), model = q_all.shape, out_rows.shape[1]
    rows = tokens // 2
    qpos, start, kpos = where
    at = lambda i: (sequence, 0)
    in_specs = [
        pl.BlockSpec((rows, wide), at),
        pl.BlockSpec((rows, 2 * wide), at),
        pl.BlockSpec((rows, 2 * wide), at),
        whole_spec(out_rows),
        whole_spec(qpos),
        pl.BlockSpec((1, rows, 1), lambda i: (sequence, 0, 0)),
        whole_spec(kpos),
    ]
    shapes = sequence_shapes(sequence, rows // 2, model)
    return into(
        attend_kernel, "attend", [q_all, kv_all, kv_other, out_rows, qpos, start, kpos], in_specs,
        [(tokens, wide)] + shapes, [pl.BlockSpec((rows, wide), at)] + [whole_shape(shape) for shape in shapes],
        [o_all], (1,),
    )


def into(kernel, name, operands, in_specs, shapes, out_specs, buffers, grid, types=None):
    count = len(operands)
    given = [b for b in buffers if b is not None]
    types = types or [BF16] * len(shapes)

    def body(*refs):
        return kernel(*refs[:count], *refs[count + len(given) :])

    return pl.pallas_call(
        body,
        grid=grid,
        in_specs=in_specs + [pl.BlockSpec(memory_space=pl.ANY)] * len(given),
        out_specs=out_specs,
        out_shape=[jax.ShapeDtypeStruct(shape, kind) for shape, kind in zip(shapes, types)],
        input_output_aliases={count + i: i for i in range(len(given))},
        compiler_params=BIG,
        cost_estimate=pl.CostEstimate(flops=0, bytes_accessed=1_000_000, transcendentals=0),
        name=name,
    )(*operands, *given)


def hidden_kernel(count, *refs):
    (b_refs, dy_refs), (w_ref, down_ref, z_ref, d_ref, b_ref, dy_ref) = (
        (refs[:count], refs[count : 2 * count]),
        refs[2 * count : 2 * count + 6],
    )
    db_refs, y_refs = refs[2 * count + 6 : 3 * count + 6], refs[3 * count + 6 :]
    fill(b_refs, b_ref)
    fill(dy_refs, dy_ref)
    piece = z_ref.shape[1] // HIDDEN_PIECES
    for i in range(HIDDEN_PIECES):
        at = slice(i * piece, (i + 1) * piece)
        gate_at, up_at = slice(2 * i * piece, (2 * i + 1) * piece), slice((2 * i + 1) * piece, (2 * i + 2) * piece)
        both = jnp.dot(b_ref[...], w_ref[:, 2 * i * piece : 2 * (i + 1) * piece], preferred_element_type=F32)
        gate, up = both[:, :piece], both[:, piece:]
        dz = lax.dot_general(dy_ref[...], down_ref[at, :], (((1,), (1,)), ((), ())), preferred_element_type=F32)
        sig = jax.nn.sigmoid(gate)
        silu = gate * sig
        z_ref[:, at] = (silu * up).astype(BF16)
        d_ref[:, gate_at] = (dz * up * sig * (1.0 + gate * (1.0 - sig))).astype(BF16)
        d_ref[:, up_at] = (dz * silu).astype(BF16)
    db = lax.dot_general(d_ref[...], w_ref[...], (((1,), (1,)), ((), ())), preferred_element_type=F32).astype(BF16)
    y = jnp.dot(z_ref[...], down_ref[...], preferred_element_type=F32).astype(BF16)

    spill(db_refs, db)
    spill(y_refs, y)


def hidden_units(index, b_blocks, dy_blocks, weight, down, buffers):
    model, width = weight.shape[0], down.shape[0]
    shapes = [block.shape for block in b_blocks]
    rows = sum(shape[0] for shape in shapes)
    once = dict(pipeline_mode=pl.Buffered(1))
    own = lambda columns: pl.BlockSpec((rows, columns), lambda i: (index, 0))
    operands = [*b_blocks, *dy_blocks, weight, down]
    out = into(
        functools.partial(hidden_kernel, len(shapes)), "hidden_units", operands,
        [whole_shape(a.shape, **once) for a in operands],
        [(4 * rows, width), (4 * rows, 2 * width), (4 * rows, model), (4 * rows, model)] + shapes * 2,
        [own(width), own(2 * width), own(model), own(model)] + [whole_shape(shape) for shape in shapes * 2],
        buffers, (1,),
    )
    return list(out[:4]), list(out[4 : 4 + len(shapes)]), list(out[4 + len(shapes) :])


def attend_back_kernel(count, *refs):
    out_ref, q_ref, kv_ref, kv2_ref, qpos_ref, start_ref, kpos_ref, cos_ref, sin_ref = refs[count : count + 9]
    dh_ref, dq_ref, dkv_ref, dkv2_ref = refs[count + 9 :]
    mask = allowed_keys(qpos_ref, start_ref, kpos_ref)
    rows, wide = q_ref.shape
    fill(refs[:count], dh_ref)
    do = lax.dot_general(
        dh_ref[...], out_ref[...], (((1,), (1,)), ((), ())), preferred_element_type=F32
    ).astype(BF16)
    for pair in range(wide // 128):
        at = slice(pair * 128, (pair + 1) * 128)
        value_at = slice(wide + pair * 128, wide + (pair + 1) * 128)
        query, grad = q_ref[:, at], do[:, at]
        key = jnp.concatenate([kv_ref[:, at], kv2_ref[:, at]], axis=0)
        value = jnp.concatenate([kv_ref[:, value_at], kv2_ref[:, value_at]], axis=0)
        dq = dk = dv = 0.0
        for odd in (False, True):
            query_one, grad_one = head_lanes(query, odd), head_lanes(grad, odd)
            weights = probabilities(query_one, key, mask)
            dp = lax.dot_general(grad_one, value, (((1,), (1,)), ((), ())), preferred_element_type=F32)
            inner = jnp.sum(dp * weights, axis=-1, keepdims=True)
            ds = (weights * (dp - inner)).astype(BF16)
            low = weights.astype(BF16)
            dq = dq + jnp.dot(ds, head_lanes(key, odd), preferred_element_type=F32)
            dk = dk + lax.dot_general(ds, query_one, (((0,), (0,)), ((), ())), preferred_element_type=F32)
            dv = dv + lax.dot_general(low, grad_one, (((0,), (0,)), ((), ())), preferred_element_type=F32)
        dq_ref[:, at] = turn(dq * 0.125, cos_ref[...], -sin_ref[...]).astype(BF16)
        dkv_ref[:, at] = dk[:rows] * 0.125
        dkv2_ref[:, at] = (dk[rows:] * 0.125).astype(BF16)
        dkv_ref[:, value_at] = dv[:rows]
        dkv2_ref[:, value_at] = dv[rows:].astype(BF16)


def attend_back(sequence, dh_blocks, out_rows, q_all, kv_all, kv_other, where, tables, dh_all):
    model, (tokens, wide) = dh_blocks[0].shape[1], q_all.shape
    rows = tokens // 2
    qpos, start, kpos = where
    at = lambda i: (sequence, 0)
    in_specs = [whole_spec(block) for block in dh_blocks] + [
        whole_spec(out_rows),
        pl.BlockSpec((rows, wide), at),
        pl.BlockSpec((rows, 2 * wide), at),
        pl.BlockSpec((rows, 2 * wide), at),
        whole_spec(qpos),
        pl.BlockSpec((1, rows, 1), lambda i: (sequence, 0, 0)),
        whole_spec(kpos), whole_spec(tables[0]), whole_spec(tables[1]),
    ]
    return into(
        functools.partial(attend_back_kernel, len(dh_blocks)), "attend_back",
        [*dh_blocks, out_rows, q_all, kv_all, kv_other, qpos, start, kpos, *tables],
        in_specs, [(tokens, model), (rows, wide), (rows, 2 * wide), (rows, 2 * wide)],
        [pl.BlockSpec((rows, model), at)] + [whole_shape((rows, n * wide)) for n in (1, 2, 2)],
        [dh_all], (1,), types=[BF16, BF16, F32, BF16],
    )


def join_kernel(dq_ref, dkv_ref, dkv2_ref, cos_ref, sin_ref, out_ref):
    wide = dq_ref.shape[1]
    out_ref[:, :wide] = dq_ref[...]
    for i in range(wide // 128):
        at = slice(i * 128, (i + 1) * 128)
        dk = dkv_ref[:, at] + dkv2_ref[:, at].astype(F32)
        out_ref[:, wide + i * 128 : wide + (i + 1) * 128] = turn(dk, cos_ref[...], -sin_ref[...]).astype(BF16)
    out_ref[:, 2 * wide :] = (dkv_ref[:, wide:] + dkv2_ref[:, wide:].astype(F32)).astype(BF16)


def join_grads(sequence, dq, dkv, dkv_other, tables, d_qkv):
    rows, wide = dq.shape
    operands = [dq, dkv, dkv_other, *tables]
    (d_qkv,) = into(
        join_kernel, "join_grads", operands, [whole_spec(a) for a in operands],
        [(2 * rows, 3 * wide)], [pl.BlockSpec((rows, 3 * wide), lambda i: (sequence, 0))], [d_qkv], (1,),
    )
    return d_qkv


def input_terms_kernel(d_ref, w_ref, w2_ref, core_ref, *term_refs):
    mine, other = (
        lax.dot_general(d_ref[...], ref[...], (((1,), (1,)), ((), ())), preferred_element_type=F32).astype(BF16)
        for ref in (w_ref, w2_ref)
    )
    first = core_ref[0] == 0
    terms = jnp.concatenate([jnp.where(first, mine, other), jnp.where(first, other, mine)], axis=1)
    at_step(pl.program_id(0), spill, term_refs, terms)


def input_terms(core, d_qkv, weights):
    tokens, wide = d_qkv.shape
    model = 2 * weights[0].shape[0]
    return into(
        input_terms_kernel, "input_terms", [d_qkv, *weights, core],
        [pl.BlockSpec((tokens // 2, wide), lambda i: (i, 0)), whole_spec(weights[0]), whole_spec(weights[1]),
         pl.BlockSpec(memory_space=pltpu.SMEM)],
        square_shapes(tokens // 4, model), square_specs(tokens // 4, model), [], (2,),
    )


def on_rows(kernel, name, operands, types):
    rows, model = operands[0].shape
    tile = pl.BlockSpec((rows // 3, model), lambda i: (i, 0))
    return pl.pallas_call(
        kernel,
        grid=(3,),
        in_specs=[tile] * len(operands),
        out_specs=[tile] * len(types),
        out_shape=[jax.ShapeDtypeStruct((rows, model), kind) for kind in types],
        compiler_params=BIG,
        cost_estimate=pl.CostEstimate(flops=0, bytes_accessed=1_000_000, transcendentals=0),
        name=name,
    )(*operands)


def total_of(refs):
    return add_low(*[ref[...] for ref in refs])


def open_kernel(x_ref, a_ref):
    x = x_ref[...].astype(F32)
    inverse = lax.rsqrt(jnp.mean(x * x, axis=-1, keepdims=True) + epsilon)
    a_ref[...] = to_inner((x * inverse).astype(BF16))


def close_attention_kernel(x_ref, *refs):
    hidden_ref, b_ref = refs[-2:]
    hidden = x_ref[...].astype(F32) + total_of(refs[:-2])
    hidden_ref[...] = hidden
    inverse = lax.rsqrt(jnp.mean(hidden * hidden, axis=-1, keepdims=True) + epsilon)
    b_ref[...] = to_inner((hidden * inverse).astype(BF16))


def close_hidden_kernel(dy_ref, hidden_ref, *refs):
    dh_ref, low_ref = refs[-2:]
    dh = dy_ref[...].astype(F32) + norm_back(hidden_ref[...], to_outer(total_of(refs[:-2])))
    dh_ref[...] = dh
    low_ref[...] = dh.astype(BF16)


def close_input_kernel(x_ref, dh_ref, *refs):
    out_ref = refs[-1]
    out_ref[...] = (dh_ref[...] + norm_back(x_ref[...].astype(F32), to_outer(total_of(refs[:-1])))).astype(BF16)


def norm_back(values, scaled):
    inverse = lax.rsqrt(jnp.mean(values * values, axis=-1, keepdims=True) + epsilon)
    normed = values * inverse
    return inverse * (scaled - normed * jnp.mean(scaled * normed, axis=-1, keepdims=True))


def dot_low(left, right, left_dim, right_dim):
    return lax.dot_general(
        left, right, (((left_dim,), (right_dim,)), ((), ())), preferred_element_type=F32
    ).astype(BF16)


def paired_device(
    layer_input, document_ids, cotangent, attention_gain, query_weight, key_weight, value_weight, output_weight,
    feedforward_gain, gate_weight, up_weight, down_weight,
):
    place = Place()
    x_own, dy_own = layer_input[0], cotangent[0]
    tok_count, model = x_own.shape
    block_rows = tok_count // 2
    length = document_ids.shape[1]
    block_count = length // block_rows
    rows = query_weight.shape[0]
    hidden_rows = down_weight.shape[0]

    attn_gain = attention_gain.astype(F32)[:, None]
    ff_gain = feedforward_gain.astype(F32)[:, None]

    documents = document_ids[0]
    first = jnp.sum((documents[None, :] < documents[:, None]).astype(jnp.int32), axis=1)
    mine, sent = head_slices(place, [query_weight, key_weight, value_weight], attn_gain, rows)
    out_half = chip_half(place, output_weight)
    dy_l = swap(dy_own, "zl")
    first = jnp.stack([first, swap(first, "seq")])
    mine, sent, out_half, x_late, down_late, gate_late, up_late = fence(
        [mine, sent, out_half, x_own, down_weight, gate_weight, up_weight], []
    )
    (a_own,) = on_rows(open_kernel, "open_layer", [x_late], [BF16])

    received = swap(sent, "x")
    out_zh, out_zl = swap(out_half, "zh"), swap(out_half, "zl")
    qkv = in_order(mine, received, place.x)
    down_half = chip_half(place, down_late)
    quarter = down_half.shape[0] * 3 // 4
    qkv, a_own, out_zh, out_zl, dy_late, down_half, dy_l, first = fence(
        [qkv, a_own, out_zh, out_zl, dy_own, down_half, dy_l, first], []
    )

    gate_up = hidden_slices(place, [gate_late, up_late], ff_gain, hidden_rows)
    by_zh, by_zl = swap(qkv, "zh"), swap(qkv, "zl")
    a_x, a_s = along(a_own)
    out_both = swap(out_zh, "zl")
    by_zh, by_zl, a_x, a_s, dy_late, out_both, gate_up, down_half = fence(
        [by_zh, by_zl, a_x, a_s, dy_late, out_both, gate_up, down_half], []
    )

    by_both = swap(by_zh, "zl")
    dy_x, dy_s = along(dy_late)
    a_o = opposite(a_x, a_s)
    out_half = in_order(
        in_order(out_half, out_zl, place.zl), in_order(out_zh, out_both, place.zl), place.zh
    ).reshape(4, -1, model)
    qkv = in_order(in_order(qkv, by_zl, place.zl), in_order(by_zh, by_both, place.zl), place.zh)
    a_all = jnp.concatenate([a_own, a_x, a_s, *a_o], axis=0)

    def positions(dx, dc):
        holder = (place.x ^ dx) * 2 + (place.core ^ dc)
        return place_of(holder, jnp.arange(tok_count, dtype=jnp.int32), block_rows, block_count // 2)

    qpos = jnp.concatenate([positions(0, 0), positions(1, 0)])
    kpos = jnp.concatenate([positions(0, 0), positions(1, 0), positions(0, 1), positions(1, 1)])
    cosine, sine = rotation(qpos, HEAD_DIM)
    cosine = jnp.concatenate([cosine] * 4, axis=1)
    sine = jnp.concatenate([-sine, sine] * 2, axis=1)
    firsts = first.reshape(2, block_count, block_rows)
    starts = []
    for dx in range(2):
        holder = (place.x ^ dx) * 2 + place.core
        for index in (holder, block_count - 1 - holder):
            starts.append(lax.dynamic_index_in_dim(firsts, index, 1, False))
    start = jnp.concatenate(starts, axis=1)[:, :, None]
    where = (qpos[:, None], start, kpos[None, :])
    tables = (cosine, sine)
    qkv, dy_l, tables, a_all, down_half, out_half, gate_up = fence(
        [qkv, dy_l, tables, a_all, down_half, out_half, gate_up], []
    )

    qkv = qkv.reshape(model // 2, -1)
    qkv_other = swap(qkv, "core")
    gate_up = share_columns(gate_up)
    down_far = [swap(down_half[:quarter], "zh")]
    out_rows = chip_rows(place, out_half, swap(out_half, "core"))
    core = jnp.stack([place.core]).astype(jnp.int32)
    qkv, qkv_other, core, dy_l, down_half, down_far = fence(
        [qkv, qkv_other, core, dy_l, down_half, down_far], []
    )

    q_all, kv_all = project(core, a_all, qkv, qkv_other, *tables)
    down_far += [swap(down_half[quarter:], "zh")]
    q_all, kv_all, down_half, down_far, dy_x, dy_s, dy_l, where, gate_up = fence(
        [q_all, kv_all, down_half, down_far, dy_x, dy_s, dy_l, where, gate_up], [out_rows]
    )

    gate_up = lax.all_gather(gate_up, ("core", "zh"), axis=0, tiled=True).reshape(model, -1)
    dy_o = opposite(dy_x, dy_s)
    kv_other = swap(kv_all, "core")
    o_all, term_s, *term_o = attend(1, q_all, kv_all, kv_other, out_rows, where, None)
    down_half = in_order(down_half, jnp.concatenate(down_far), place.zh)
    down_rows = chip_rows(place, down_half, swap(down_half, "core"))
    term_s, term_o, o_all, down_rows, dy_l = fence([term_s, term_o, o_all, down_rows, dy_l], dy_o)

    o_all, own, term_x = attend(0, q_all, kv_all, kv_other, out_rows, where, o_all)
    halves = return_halves(*term_o)
    own, term_x, halves, dy_l = fence([own, term_x, halves, dy_l], [])

    sums = return_along(term_x, term_s, *halves)
    hidden, b_own = on_rows(close_attention_kernel, "close_attention", [x_own, own, *sums], [F32, BF16])
    b_own, dy_l = fence([b_own, dy_l], [])

    b_x, b_s = along(b_own)
    b_l = swap(b_own, "zl")
    dy_lx, dy_ls = along(dy_l)
    b_x, b_s, dy_lx, dy_ls = fence([b_x, b_s, dy_lx, dy_ls], [])

    b_o = opposite(b_x, b_s)
    buffers, db0, y0 = hidden_units(0, [b_own, b_x], [dy_own, dy_x], gate_up, down_rows, [None] * 4)
    dy_lo = opposite(dy_lx, dy_ls)
    buffers, b_o, b_l = fence([buffers, b_o, b_l], dy_lo)

    b_lx, b_ls = along(b_l)
    buffers, db1, y1 = hidden_units(1, [b_s, *b_o], [dy_s, *dy_o], gate_up, down_rows, buffers)
    buffers, b_lx, b_ls, db1 = fence([buffers, b_lx, b_ls, db1], [])

    b_lo = opposite(b_lx, b_ls)
    near_halves = return_halves(*db1[1:])
    buffers, db2, y2 = hidden_units(2, [b_l, b_lx], [dy_l, dy_lx], gate_up, down_rows, buffers)
    buffers, b_lo, near_halves = fence([buffers, b_lo, near_halves], [])

    near_along = return_along(db0[1], db1[0], *near_halves)
    buffers, db3, y3 = hidden_units(3, [b_ls, *b_lo], [dy_ls, *dy_lo], gate_up, down_rows, buffers)
    z_all, d_all, b_all, dy_all = buffers
    db3, z_all, d_all, near_along = fence([db3, z_all, d_all, near_along], [])

    far_halves = return_halves(*db3[1:])
    down_terms = dot_low(z_all, dy_all, 0, 0)
    d_all, down_terms, far_halves = fence([d_all, down_terms, far_halves], [])

    far_along = return_along(db2[1], db3[0], *far_halves)
    gate_up_terms = dot_low(b_all, d_all, 0, 0)
    down_sums = add_core(place, down_terms.reshape(2, 2, -1, model), 1)
    gate_up_terms, down_sums, y0, y1, near0, far_along = fence(
        [gate_up_terms, down_sums, y0, y1, db0[0], far_along], []
    )

    down_total = lax.psum_scatter(down_sums, "zh", scatter_dimension=0, tiled=True)[0]
    across = return_across(db2[0], *far_along)
    near_y_along = return_along(y0[1], y1[0], *return_halves(*y1[1:]))
    gate_up_sums = add_core(place, gate_up_terms.reshape(2, 2, 4, rows, -1), 0)
    dh, dh_low = on_rows(
        close_hidden_kernel, "close_hidden", [dy_own, hidden, near0, *near_along, across], [F32, BF16]
    )
    dh_low, gate_up_sums, near_y_along = fence([dh_low, gate_up_sums, near_y_along], [])

    gate_up_near = lax.psum_scatter(gate_up_sums, "zh", scatter_dimension=0, tiled=True)[0]
    dh_x, dh_s = along(dh_low)
    dh_x, dh_s, y3 = fence([dh_x, dh_s, y3], [])

    dh_o = opposite(dh_x, dh_s)
    dh_all, dq0, dkv0, dkv_other0 = attend_back(
        0, [dh_low, dh_x], out_rows, q_all, kv_all, kv_other, where, tables, None
    )
    dkv_other0, dh_s, y3 = fence([dkv_other0, dh_s, y3], dh_o)

    dkv_other0 = swap(dkv_other0, "core")
    down_other = swap(down_total, "seq")
    dh_all, dq1, dkv1, dkv_other1 = attend_back(
        1, [dh_s, *dh_o], out_rows, q_all, kv_all, kv_other, where, tables, dh_all
    )
    far_y_halves = return_halves(*y3[1:])
    dkv_other1, dh_all = fence([dkv_other1, dh_all], [])

    dkv_other1 = swap(dkv_other1, "core")
    d_qkv = join_grads(0, dq0, dkv0, dkv_other0, tables, None)
    out_terms = dot_low(o_all, dh_all, 0, 0)
    d_qkv, dkv_other1, out_terms, far_y_halves, down_other = fence(
        [d_qkv, dkv_other1, out_terms, far_y_halves, down_other], []
    )

    d_qkv = join_grads(1, dq1, dkv1, dkv_other1, tables, d_qkv)
    qkv_terms = dot_low(a_all, d_qkv, 0, 0)
    far_y_along = return_along(y2[1], y3[0], *far_y_halves)
    out_sums = add_core(place, out_terms.reshape(4, 2, -1, model), 1).reshape(2, 2, -1, model)
    qkv_terms, out_sums, d_qkv = fence([qkv_terms, out_sums, d_qkv], [])

    def part(sums, zh, zl):
        return lax.dynamic_slice(sums, (place.zh ^ zh, place.zl ^ zl, 0, 0), (1, 1, *sums.shape[2:]))[0, 0]

    qkv_sums = add_core(place, qkv_terms.reshape(2, 2, 2, 2 * rows, -1), 0)
    own, term_x, term_s, *term_o = input_terms(core, d_qkv, [qkv, qkv_other])
    out_zl = swap(part(out_sums, 1, 1), "zl")
    qkv_sums, out_sums, out_zl, term_o, far_y_along, gate_up_near = fence(
        [qkv_sums, out_sums, out_zl, term_o, far_y_along, gate_up_near], []
    )

    qkv_zl = swap(part(qkv_sums, 1, 1), "zl")
    gate_up_near = share_columns(gate_up_near)
    sums = return_along(term_x, term_s, *return_halves(*term_o))
    down_grad = own_rows(place, down_total, down_other)
    qkv_zl, gate_up_near, sums, out_zl = fence([qkv_zl, gate_up_near, sums, out_zl], [down_grad])

    qkv_zh = swap(add_low(part(qkv_sums, 1, 0), qkv_zl).astype(BF16), "zh")
    qkv_zl = swap(part(qkv_sums, 0, 1), "zl")
    gate_up_far = swap(gate_up_near, "seq")
    (input_grad,) = on_rows(close_input_kernel, "close_input", [x_own, dh, own, *sums], [BF16])
    qkv_zh, qkv_zl, out_zl, out_sums = fence([qkv_zh, qkv_zl, out_zl, out_sums], [input_grad])

    qkv_total = add_low(part(qkv_sums, 0, 0), qkv_zl, qkv_zh).astype(BF16).reshape(2, rows, -1)
    kept = lax.dynamic_index_in_dim(qkv_total, place.x, 0, False)
    received = swap(lax.dynamic_index_in_dim(qkv_total, 1 - place.x, 0, False), "x")
    kept_far, received_far = swap(kept, "seq"), swap(received, "seq")
    out_zh = swap(add_low(part(out_sums, 1, 0), out_zl).astype(BF16), "zh")
    out_zl = swap(part(out_sums, 0, 1), "zl")
    (gate_grad, up_grad), ff_gain_grad = finish_columns(
        place, *[v.reshape(2, 2, rows, -1) for v in (gate_up_near, gate_up_far)], [gate_weight, up_weight], ff_gain,
        hidden_rows, True,
    )
    kept, kept_far, received, received_far, out_zh, out_zl, far_y_along = fence(
        [kept, kept_far, received, received_far, out_zh, out_zl, far_y_along], [ff_gain_grad]
    )

    y_across = return_across(y2[0], *far_y_along)
    out_total = add_low(part(out_sums, 0, 0), out_zl, out_zh).astype(BF16)
    out_other = swap(out_total, "seq")
    output_grad = own_rows(place, out_total, out_other)

    (query_grad, key_grad, value_grad), attn_gain_grad = finish_columns(
        place, in_order(kept, received, place.x), in_order(kept_far, received_far, place.x),
        [query_weight, key_weight, value_weight], attn_gain, rows, False,
    )
    layer_output = add_low(hidden, y0[0], *near_y_along, y_across).astype(BF16)
    return (
        layer_output[None], input_grad[None], attn_gain_grad, query_grad, key_grad, value_grad, output_grad,
        ff_gain_grad, gate_grad, up_grad, down_grad,
    )


def paired(mesh):
    fine = Mesh(mesh.devices.reshape(2, 2, 2, 2, 2), ("seq", "x", "core", "zh", "zl"))
    tokens = P(("seq", "zh", "zl"), ("x", "core"), None)
    matrix, vector = P(("x", "core", "zh", "zl"), None), P(("x", "core", "zh", "zl"))
    return jax.shard_map(
        paired_device,
        mesh=fine,
        in_specs=(tokens, P(("seq", "zh", "zl"), None), tokens, vector) + (matrix,) * 4 + (vector,) + (matrix,) * 3,
        out_specs=(tokens, tokens, vector) + (matrix,) * 4 + (vector,) + (matrix,) * 3,
        check_vma=False,
    )


def solution(mesh):
    if tuple(mesh.shape[axis] for axis in ("seq", "ctx", "fsdp")) == (2, 4, 4):
        return paired(mesh)
    return gathered(mesh)
```

```python
import functools
import math

import jax
import jax.numpy as jnp
from jax import lax
from jax.experimental import pallas as pl
from jax.experimental.pallas import tpu as pltpu
from jax.sharding import Mesh, PartitionSpec as P

HEADS = 32
HEAD_DIM = 64


epsilon = 1e-05
rotary_base = 130000.0
masked_score = -1e30


def norm_scale(values, gain):
    inverse = lax.rsqrt(jnp.mean(values * values, axis=-1, keepdims=True) + epsilon)
    return values * inverse * gain


def rotation(positions, head_size):
    half_dim = head_size // 2
    frequency = rotary_base ** (-(jnp.arange(half_dim, dtype=jnp.float32) * 2.0) / head_size)
    angles = positions.astype(jnp.float32)[:, None] * frequency[None, :]
    return (jnp.cos(angles), jnp.sin(angles))


def rotate(values, cosine, sine_table):
    half_dim = values.shape[-1] // 2
    front_part = values[..., :half_dim]
    second = values[..., half_dim:]
    cos_wide = cosine[:, None, :]
    sin_wide = sine_table[:, None, :]
    return jnp.concatenate(
        [front_part * cos_wide - second * sin_wide, second * cos_wide + front_part * sin_wide],
        axis=-1,
    )


def place_of(holder, offset, block_rows, ctx_count):
    return jnp.where(
        offset < block_rows,
        holder * block_rows + offset,
        (2 * ctx_count - 1 - holder) * block_rows + offset - block_rows,
    )


def per_device(
    layer_input,
    document_ids,
    cotangent,
    attention_gain,
    query_weight,
    key_weight,
    value_weight,
    output_weight,
    feedforward_gain,
    gate_weight,
    up_weight,
    down_weight,
):
    ctx_count = lax.axis_size("ctx")
    device = lax.axis_index("ctx")
    inputs = layer_input[0].astype(jnp.float32)
    upstream = cotangent[0]
    tok_count = inputs.shape[0]
    model_width = inputs.shape[1]
    block_rows = tok_count // 2
    group_heads = math.gcd(8, HEADS)
    group_count = HEADS // group_heads
    group_width = group_heads * HEAD_DIM
    key_count = ctx_count * tok_count
    local_pos = place_of(device, jnp.arange(tok_count, dtype=jnp.int32), block_rows, ctx_count)
    key_index = jnp.arange(key_count, dtype=jnp.int32)
    key_pos = place_of(key_index // tok_count, key_index % tok_count, block_rows, ctx_count)
    documents = document_ids[0]
    same_doc = jnp.take(documents, local_pos)[:, None] == jnp.take(documents, key_pos)[None, :]
    allowed = (key_pos[None, :] <= local_pos[:, None]) & same_doc
    cosine, sine_table = rotation(local_pos, HEAD_DIM)
    attention_set = (
        lax.all_gather(attention_gain, ("ctx", "fsdp"), axis=0, tiled=True),
        lax.all_gather(query_weight, ("ctx", "fsdp"), axis=0, tiled=True),
        lax.all_gather(key_weight, ("ctx", "fsdp"), axis=0, tiled=True),
        lax.all_gather(value_weight, ("ctx", "fsdp"), axis=0, tiled=True),
        lax.all_gather(output_weight, ("ctx", "fsdp"), axis=0, tiled=True),
    )
    attn_gain_full = attention_set[0].astype(jnp.float32)
    normed_low = norm_scale(inputs, attn_gain_full).astype(jnp.bfloat16)
    query_pre = jnp.dot(normed_low, attention_set[1], preferred_element_type=jnp.float32)
    key_pre = jnp.dot(normed_low, attention_set[2], preferred_element_type=jnp.float32)
    value_pre = jnp.dot(normed_low, attention_set[3], preferred_element_type=jnp.float32)
    queries = (
        rotate(query_pre.reshape(tok_count, HEADS, HEAD_DIM), cosine, sine_table)
        .reshape(tok_count, model_width)
        .astype(jnp.bfloat16)
    )
    keys_local = (
        rotate(key_pre.reshape(tok_count, HEADS, HEAD_DIM), cosine, sine_table)
        .reshape(tok_count, model_width)
        .astype(jnp.bfloat16)
    )
    values_local = value_pre.astype(jnp.bfloat16)
    all_keys, all_values = (
        lax.all_gather(keys_local, "ctx", axis=0, tiled=True),
        lax.all_gather(values_local, "ctx", axis=0, tiled=True),
    )

    def group_parts(group_index):
        column_start = group_index * group_width
        query_part = lax.dynamic_slice_in_dim(queries, column_start, group_width, 1).reshape(
            tok_count, group_heads, HEAD_DIM
        )
        key_part = lax.dynamic_slice_in_dim(all_keys, column_start, group_width, 1).reshape(
            key_count, group_heads, HEAD_DIM
        )
        value_part = lax.dynamic_slice_in_dim(all_values, column_start, group_width, 1).reshape(
            key_count, group_heads, HEAD_DIM
        )
        scores = (
            jnp.einsum("qhd,khd->hqk", query_part, key_part, preferred_element_type=jnp.float32)
            * 0.125
        )
        scores = jnp.where(allowed[None], scores, masked_score)
        return (query_part, key_part, value_part, scores)

    def group_forward(group_index):
        query_part, key_part, value_part, scores = group_parts(group_index)
        row_peak = jnp.max(scores, axis=-1, keepdims=True)
        exponent = jnp.exp(scores - row_peak)
        row_total = jnp.sum(exponent, axis=-1, keepdims=True)
        softmax_weights = exponent / row_total
        log_total = row_peak[..., 0] + jnp.log(row_total[..., 0])
        attended = jnp.einsum(
            "hqk,khd->qhd",
            softmax_weights.astype(jnp.bfloat16),
            value_part,
            preferred_element_type=jnp.float32,
        )
        return (attended.reshape(tok_count, group_width), log_total)

    group_index_all = jnp.arange(group_count, dtype=jnp.int32)
    attended_groups, log_totals = lax.map(group_forward, group_index_all)
    attended_low = (
        jnp.transpose(attended_groups, (1, 0, 2))
        .reshape(tok_count, model_width)
        .astype(jnp.bfloat16)
    )
    hidden = inputs + jnp.dot(attended_low, attention_set[4], preferred_element_type=jnp.float32)
    feedforward_set = (
        lax.all_gather(feedforward_gain, ("ctx", "fsdp"), axis=0, tiled=True),
        lax.all_gather(gate_weight, ("ctx", "fsdp"), axis=0, tiled=True),
        lax.all_gather(up_weight, ("ctx", "fsdp"), axis=0, tiled=True),
        lax.all_gather(down_weight, ("ctx", "fsdp"), axis=0, tiled=True),
    )
    mlp_low = norm_scale(hidden, feedforward_set[0].astype(jnp.float32)).astype(jnp.bfloat16)
    gate_pre = jnp.dot(mlp_low, feedforward_set[1], preferred_element_type=jnp.float32)
    up_pre = jnp.dot(mlp_low, feedforward_set[2], preferred_element_type=jnp.float32)
    product_low = (jax.nn.silu(gate_pre) * up_pre).astype(jnp.bfloat16)
    layer_output = (
        hidden + jnp.dot(product_low, feedforward_set[3], preferred_element_type=jnp.float32)
    ).astype(jnp.bfloat16)
    feedforward_back = (
        lax.all_gather(feedforward_gain, ("ctx", "fsdp"), axis=0, tiled=True),
        lax.all_gather(gate_weight, ("ctx", "fsdp"), axis=0, tiled=True),
        lax.all_gather(up_weight, ("ctx", "fsdp"), axis=0, tiled=True),
        lax.all_gather(down_weight, ("ctx", "fsdp"), axis=0, tiled=True),
    )
    attention_back = (
        lax.all_gather(attention_gain, ("ctx", "fsdp"), axis=0, tiled=True),
        lax.all_gather(query_weight, ("ctx", "fsdp"), axis=0, tiled=True),
        lax.all_gather(key_weight, ("ctx", "fsdp"), axis=0, tiled=True),
        lax.all_gather(value_weight, ("ctx", "fsdp"), axis=0, tiled=True),
        lax.all_gather(output_weight, ("ctx", "fsdp"), axis=0, tiled=True),
    )
    piece = product_low
    down_shard = lax.psum_scatter(
        jnp.einsum("tf,td->fd", piece, upstream, preferred_element_type=jnp.float32),
        ("ctx", "fsdp"),
        scatter_dimension=0,
        tiled=True,
    )
    product_grad = jnp.einsum(
        "td,fd->tf", upstream, feedforward_back[3], preferred_element_type=jnp.float32
    )
    silu_out, silu_pullback = jax.vjp(
        lambda gate_in, up_in: jax.nn.silu(gate_in) * up_in, gate_pre, up_pre
    )
    gate_grad, up_grad = silu_pullback(product_grad)
    gate_grad_low = gate_grad.astype(jnp.bfloat16)
    up_grad_low = up_grad.astype(jnp.bfloat16)
    joined_grads = jnp.concatenate([gate_grad_low, up_grad_low], axis=1)
    piece = mlp_low
    joined_shard = lax.psum_scatter(
        jnp.einsum("td,tf->df", piece, joined_grads, preferred_element_type=jnp.float32),
        ("ctx", "fsdp"),
        scatter_dimension=0,
        tiled=True,
    )
    ff_width = gate_weight.shape[1]
    gate_shard = joined_shard[:, :ff_width]
    up_shard = joined_shard[:, ff_width:]
    mlp_normed_grad = jnp.einsum(
        "tf,df->td", gate_grad_low, feedforward_back[1], preferred_element_type=jnp.float32
    )
    mlp_normed_grad = mlp_normed_grad + jnp.einsum(
        "tf,df->td", up_grad_low, feedforward_back[2], preferred_element_type=jnp.float32
    )
    mlp_norm_out, mlp_norm_pullback = jax.vjp(
        norm_scale, hidden, feedforward_back[0].astype(jnp.float32)
    )
    hidden_from_norm, ff_gain_term = mlp_norm_pullback(mlp_normed_grad)
    hidden_grad = upstream.astype(jnp.float32) + hidden_from_norm
    hidden_low = hidden_grad.astype(jnp.bfloat16)
    output_term = jnp.einsum(
        "td,te->de", attended_low, hidden_low, preferred_element_type=jnp.float32
    )
    attended_grad_low = jnp.einsum(
        "te,de->td", hidden_low, attention_back[4], preferred_element_type=jnp.float32
    ).astype(jnp.bfloat16)

    def group_backward(operands):
        group_index, log_total = operands
        query_part, key_part, value_part, scores = group_parts(group_index)
        softmax_weights = jnp.exp(scores - log_total[:, :, None])
        column_start = group_index * group_width
        grad_part = lax.dynamic_slice_in_dim(
            attended_grad_low, column_start, group_width, 1
        ).reshape(tok_count, group_heads, HEAD_DIM)
        value_grad = jnp.einsum(
            "hqk,qhd->khd",
            softmax_weights.astype(jnp.bfloat16),
            grad_part,
            preferred_element_type=jnp.float32,
        )
        weight_grad = jnp.einsum(
            "qhd,khd->hqk", grad_part, value_part, preferred_element_type=jnp.float32
        )
        row_inner = jnp.sum(weight_grad * softmax_weights, axis=-1, keepdims=True)
        score_grad = (softmax_weights * (weight_grad - row_inner)).astype(jnp.bfloat16)
        query_grad = (
            jnp.einsum("hqk,khd->qhd", score_grad, key_part, preferred_element_type=jnp.float32)
            * 0.125
        )
        key_grad = (
            jnp.einsum("hqk,qhd->khd", score_grad, query_part, preferred_element_type=jnp.float32)
            * 0.125
        )
        return (
            query_grad.reshape(tok_count, group_width),
            key_grad.reshape(key_count, group_width),
            value_grad.reshape(key_count, group_width),
        )

    query_groups, key_groups, value_groups = lax.map(group_backward, (group_index_all, log_totals))
    query_grad_all = jnp.transpose(query_groups, (1, 0, 2)).reshape(tok_count, model_width)
    key_grad_all = jnp.transpose(key_groups, (1, 0, 2)).reshape(key_count, model_width)
    value_grad_all = jnp.transpose(value_groups, (1, 0, 2)).reshape(key_count, model_width)
    key_grad_local, value_grad_local = (
        lax.psum_scatter(
            key_grad_all.astype(jnp.bfloat16), "ctx", scatter_dimension=0, tiled=True
        ).astype(jnp.float32),
        lax.psum_scatter(
            value_grad_all.astype(jnp.bfloat16), "ctx", scatter_dimension=0, tiled=True
        ).astype(jnp.float32),
    )
    negative_sine = -sine_table
    query_pre_grad = (
        rotate(query_grad_all.reshape(tok_count, HEADS, HEAD_DIM), cosine, negative_sine)
        .reshape(tok_count, model_width)
        .astype(jnp.bfloat16)
    )
    key_pre_grad = (
        rotate(key_grad_local.reshape(tok_count, HEADS, HEAD_DIM), cosine, negative_sine)
        .reshape(tok_count, model_width)
        .astype(jnp.bfloat16)
    )
    value_pre_grad = value_grad_local.astype(jnp.bfloat16)
    query_term = jnp.einsum(
        "td,te->de", normed_low, query_pre_grad, preferred_element_type=jnp.float32
    )
    key_term = jnp.einsum("td,te->de", normed_low, key_pre_grad, preferred_element_type=jnp.float32)
    value_term = jnp.einsum(
        "td,te->de", normed_low, value_pre_grad, preferred_element_type=jnp.float32
    )
    attn_normed_grad = jnp.einsum(
        "te,de->td", query_pre_grad, attention_back[1], preferred_element_type=jnp.float32
    )
    attn_normed_grad = attn_normed_grad + jnp.einsum(
        "te,de->td", key_pre_grad, attention_back[2], preferred_element_type=jnp.float32
    )
    attn_normed_grad = attn_normed_grad + jnp.einsum(
        "te,de->td", value_pre_grad, attention_back[3], preferred_element_type=jnp.float32
    )
    attn_norm_out, attn_norm_pullback = jax.vjp(
        norm_scale, inputs, attention_back[0].astype(jnp.float32)
    )
    inputs_from_norm, attn_gain_term = attn_norm_pullback(attn_normed_grad)
    input_grad = (hidden_grad + inputs_from_norm).astype(jnp.bfloat16)
    attn_shards = (
        lax.psum_scatter(attn_gain_term, ("ctx", "fsdp"), scatter_dimension=0, tiled=True),
        lax.psum_scatter(ff_gain_term, ("ctx", "fsdp"), scatter_dimension=0, tiled=True),
        lax.psum_scatter(query_term, ("ctx", "fsdp"), scatter_dimension=0, tiled=True),
        lax.psum_scatter(key_term, ("ctx", "fsdp"), scatter_dimension=0, tiled=True),
        lax.psum_scatter(value_term, ("ctx", "fsdp"), scatter_dimension=0, tiled=True),
        lax.psum_scatter(output_term, ("ctx", "fsdp"), scatter_dimension=0, tiled=True),
    )
    summed = (
        lax.psum(attn_shards[0].astype(jnp.bfloat16), "seq").astype(jnp.float32),
        lax.psum(attn_shards[2].astype(jnp.bfloat16), "seq").astype(jnp.float32),
        lax.psum(attn_shards[3].astype(jnp.bfloat16), "seq").astype(jnp.float32),
        lax.psum(attn_shards[4].astype(jnp.bfloat16), "seq").astype(jnp.float32),
        lax.psum(attn_shards[5].astype(jnp.bfloat16), "seq").astype(jnp.float32),
        lax.psum(attn_shards[1].astype(jnp.bfloat16), "seq").astype(jnp.float32),
        lax.psum(gate_shard.astype(jnp.bfloat16), "seq").astype(jnp.float32),
        lax.psum(up_shard.astype(jnp.bfloat16), "seq").astype(jnp.float32),
        lax.psum(down_shard.astype(jnp.bfloat16), "seq").astype(jnp.float32),
    )
    return (
        layer_output[None],
        input_grad[None],
        summed[0],
        summed[1],
        summed[2],
        summed[3],
        summed[4],
        summed[5],
        summed[6],
        summed[7],
        summed[8],
    )


def gathered(mesh):
    return jax.shard_map(
        per_device,
        mesh=mesh,
        in_specs=(
            P(("seq", "fsdp"), "ctx", None),
            P(("seq", "fsdp"), None),
            P(("seq", "fsdp"), "ctx", None),
            P(("ctx", "fsdp")),
            P(("ctx", "fsdp"), None),
            P(("ctx", "fsdp"), None),
            P(("ctx", "fsdp"), None),
            P(("ctx", "fsdp"), None),
            P(("ctx", "fsdp")),
            P(("ctx", "fsdp"), None),
            P(("ctx", "fsdp"), None),
            P(("ctx", "fsdp"), None),
        ),
        out_specs=(
            P(("seq", "fsdp"), "ctx", None),
            P(("seq", "fsdp"), "ctx", None),
            P(("ctx", "fsdp")),
            P(("ctx", "fsdp"), None),
            P(("ctx", "fsdp"), None),
            P(("ctx", "fsdp"), None),
            P(("ctx", "fsdp"), None),
            P(("ctx", "fsdp")),
            P(("ctx", "fsdp"), None),
            P(("ctx", "fsdp"), None),
            P(("ctx", "fsdp"), None),
        ),
        check_vma=False,
    )


HIDDEN_PIECES = 2
BIG = pltpu.CompilerParams(vmem_limit_bytes=56 * 1024 * 1024)
BF16 = jnp.bfloat16
F32 = jnp.float32


def swap(value, axis):
    return lax.ppermute(value, axis, [(0, 1), (1, 0)])


def fence(late, early):
    return list(lax.optimization_barrier((tuple(late), tuple(early)))[0])


def opposite(along_x, along_seq):
    half = along_x.shape[0] // 2
    return [swap(along_seq[:half], "x"), swap(along_x[half:], "seq")]


def along(block):
    return [swap(block, "x"), swap(block, "seq")]


def add_low(first, *others):
    total = first.astype(F32)
    for other in others:
        total = total + other.astype(F32)
    return total


def return_halves(upper, lower):
    return [swap(upper, "x"), swap(lower, "seq")]


def return_along(to_x, to_seq, by_x, by_seq):
    half = to_x.shape[0] // 2
    to_seq = jnp.concatenate([add_low(to_seq[:half], by_x).astype(BF16), to_seq[half:]], axis=0)
    to_x = jnp.concatenate([to_x[:half], add_low(to_x[half:], by_seq).astype(BF16)], axis=0)
    return [swap(to_x, "x"), swap(to_seq, "seq")]


def return_across(own, by_x, by_seq):
    return swap(add_low(own, by_x, by_seq).astype(BF16), "zl")


def in_order(mine, other, place):
    first = place == 0
    return jnp.stack([jnp.where(first, mine, other), jnp.where(first, other, mine)])


def pair_up(mine, axis):
    return in_order(mine, swap(mine, axis), lax.axis_index(axis))


def slot(count, blocks, joined, w, block):
    return block * count + w if joined else w * blocks + block


def slices_kernel(count, blocks, joined, table_ref, *refs):
    gain, out = refs[-2][...], refs[-1]
    width = refs[0].shape[1]
    for w in range(count):
        for block in range(blocks):
            at = slot(count, blocks, joined, w, block) * width
            out[0, :, at : at + width] = (refs[blocks * w + block][...].astype(F32) * gain).astype(BF16)


def column_slices(table, chips, blocks, column, weights, gain, width, joined):
    rows = weights[0].shape[0]

    def column_spec(block):
        return pl.BlockSpec((rows, width), lambda t, table: (0, column(t, block, table)))

    wide = blocks * width * len(weights)
    return pl.pallas_call(
        functools.partial(slices_kernel, len(weights), blocks, joined),
        grid_spec=pltpu.PrefetchScalarGridSpec(
            num_scalar_prefetch=1,
            grid=(chips,),
            in_specs=[column_spec(block) for _ in weights for block in range(blocks)]
            + [pl.BlockSpec((rows, 1), lambda t, table: (0, 0))],
            out_specs=pl.BlockSpec((1, rows, wide), lambda t, table: (t, 0, 0)),
        ),
        out_shape=jax.ShapeDtypeStruct((chips, rows, wide), BF16),
        compiler_params=BIG,
        cost_estimate=pl.CostEstimate(flops=0, bytes_accessed=1_000_000, transcendentals=0),
        name="column_slices",
    )(table, *[w for w in weights for _ in range(blocks)], gain)


def hidden_slices(place, weights, gain, width):
    def column(t, zh, table):
        return (((t % 2) * 2 + table[0]) * 2 + zh) * 2 + t // 2

    table = jnp.stack([place.seq]).astype(jnp.int32)
    return column_slices(table, 4, 2, column, weights, gain, width, True)


def head_slices(place, weights, gain, width):
    def column(t, z, table):
        return ((table[1] + t - 2 * table[1] * t) * 2 + table[0]) * 4 + z

    table = jnp.stack([place.seq, place.x]).astype(jnp.int32)
    return column_slices(table, 2, 4, column, weights, gain, width, False)


def share_columns(slices):
    return lax.all_to_all(slices, ("zl", "x"), split_axis=0, concat_axis=0, tiled=True)


def chip_half(place, weight):
    half = weight.shape[0] // 2
    moved = lax.ppermute(
        lax.dynamic_slice_in_dim(weight, (1 - place.core) * half, half, 0), ("seq", "core"), [(0, 1), (3, 2)]
    )
    own = lax.dynamic_slice_in_dim(weight, place.core * half, half, 0)
    return jnp.where(place.core == place.seq, own, moved)


def chip_rows(place, mine, other):
    first = place.core == 0
    halves = jnp.stack([jnp.where(first, mine, other), jnp.where(first, other, mine)], axis=1)
    return halves.reshape(-1, mine.shape[-1])


def add_core(place, parts, axis):
    received = swap(lax.dynamic_index_in_dim(parts, 1 - place.core, axis, False), "core")
    return add_low(lax.dynamic_index_in_dim(parts, place.core, axis, False), received).astype(BF16)


def to_far(place, sums):
    return lax.dynamic_index_in_dim(sums, 1 - place.zh, 0, False)


def add_far(place, sums, received):
    return add_low(lax.dynamic_index_in_dim(sums, place.zh, 0, False), received).astype(BF16)


def own_rows(place, total, other):
    mine = place.core == place.seq
    received = swap(jnp.where(mine, other, total), "core")
    kept = jnp.where(mine, total, other)
    first = place.core == 0
    return jnp.concatenate([jnp.where(first, kept, received), jnp.where(first, received, kept)]).astype(F32)


def finish_kernel(count, seq_ref, *refs):
    near, far, weights = refs[:count], refs[count : 2 * count], refs[2 * count : 3 * count]
    gain, outs = refs[3 * count], refs[3 * count + 1 :]
    j = pl.program_id(0)
    use_near = (j // 2) % 2 == seq_ref[0]
    total = None
    for i in range(count):
        grad = jnp.where(use_near, near[i][...], far[i][...]).astype(F32)
        pieces = [grad[k, 0] for k in range(2)] if grad.ndim == 4 else [grad[0]]
        grad = jnp.concatenate(pieces, axis=1)
        outs[i][...] = grad * gain[...]
        term = grad * weights[i][...].astype(F32)
        total = term if total is None else total + term

    @pl.when(j == 0)
    def _():
        outs[count][...] = jnp.zeros_like(outs[count])

    outs[count][...] += total


def finish_columns(place, near, far, weights, gain, width, joined):
    count, rows = len(weights), weights[0].shape[0]

    def piece_spec(w):
        def index(j, seq):
            x, zh = j // 4, j % 2
            return (0, x, 0, slot(count, 2, joined, w, zh)) if joined else (x, 0, w * 2 + zh)

        return pl.BlockSpec((2, 1, rows, width) if joined else (1, rows, 2 * width), index)

    column_spec = pl.BlockSpec((rows, 2 * width), lambda j, seq: (0, j))
    pieces = [piece_spec(w) for w in range(count)]
    outs = pl.pallas_call(
        functools.partial(finish_kernel, count),
        grid_spec=pltpu.PrefetchScalarGridSpec(
            num_scalar_prefetch=1,
            grid=(8,),
            in_specs=pieces * 2 + [column_spec] * count + [pl.BlockSpec((rows, 1), lambda j, seq: (0, 0))],
            out_specs=[column_spec] * count + [pl.BlockSpec((rows, 2 * width), lambda j, seq: (0, 0))],
        ),
        out_shape=[jax.ShapeDtypeStruct((rows, 16 * width), F32)] * count
        + [jax.ShapeDtypeStruct((rows, 2 * width), F32)],
        compiler_params=BIG,
        cost_estimate=pl.CostEstimate(flops=0, bytes_accessed=1_000_000, transcendentals=0),
        name="finish_columns",
    )(jnp.stack([place.seq]).astype(jnp.int32), *[near] * count, *[far] * count, *weights, gain)
    return outs[:count], jnp.sum(outs[count], axis=1)


class Place:
    def __init__(self):
        self.seq = lax.axis_index("seq")
        self.x = lax.axis_index("x")
        self.core = lax.axis_index("core")
        self.zh = lax.axis_index("zh")
        self.zl = lax.axis_index("zl")


def block_columns(value, source):
    wide = value.shape[1] // 16
    return jnp.concatenate([value[:, i * wide : (i + 1) * wide] for i in source], axis=1)


def to_inner(value):
    return block_columns(value, [x * 8 + z for z in range(8) for x in (0, 1)])


def to_outer(value):
    return block_columns(value, [z * 2 + x for x in (0, 1) for z in range(8)])


def turn(value, cosine, sine):
    lane = lax.broadcasted_iota(jnp.int32, value.shape, 1)
    partner = jnp.where(lane % HEAD_DIM < HEAD_DIM // 2, pltpu.roll(value, 96, 1), pltpu.roll(value, 32, 1))
    return value * cosine + partner * sine


def project_kernel(core_ref, a_ref, a2_ref, w_ref, w2_ref, cos_ref, sin_ref, q_ref, kv_ref):
    joined = jnp.dot(a_ref[...], w_ref[...], preferred_element_type=F32)
    joined = joined + jnp.dot(a2_ref[...], w2_ref[...], preferred_element_type=F32)
    wide = q_ref.shape[1]
    cosine, sine = cos_ref[...], sin_ref[...]
    for i in range(wide // 128):
        at = slice(i * 128, (i + 1) * 128)
        q_ref[:, at] = turn(joined[:, at], cosine, sine).astype(BF16)
        kv_ref[:, at] = turn(joined[:, wide + i * 128 : wide + (i + 1) * 128], cosine, sine).astype(BF16)
    kv_ref[:, wide:] = joined[:, 2 * wide :].astype(BF16)


def whole_spec(array):
    return pl.BlockSpec(array.shape, lambda i: (0,) * array.ndim)


def project(core, a_all, weight, weight_other, cosine, sine):
    tokens, model = a_all.shape
    wide = weight.shape[1] // 3
    tile, half = cosine.shape[0], model // 2
    by_tile = lambda columns: pl.BlockSpec((tile, columns), lambda i, core: (i, 0))
    whole = lambda array: pl.BlockSpec(array.shape, lambda i, core: (0, 0))
    return pl.pallas_call(
        project_kernel,
        grid_spec=pltpu.PrefetchScalarGridSpec(
            num_scalar_prefetch=1,
            grid=(tokens // tile,),
            in_specs=[
                pl.BlockSpec((tile, half), lambda i, core: (i, core[0])),
                pl.BlockSpec((tile, half), lambda i, core: (i, 1 - core[0])),
                whole(weight), whole(weight_other), whole(cosine), whole(sine),
            ],
            out_specs=[by_tile(wide), by_tile(2 * wide)],
        ),
        out_shape=[jax.ShapeDtypeStruct((tokens, columns), BF16) for columns in (wide, 2 * wide)],
        compiler_params=BIG,
        cost_estimate=pl.CostEstimate(flops=0, bytes_accessed=1_000_000, transcendentals=0),
        name="project",
    )(core, a_all, a_all, weight, weight_other, cosine, sine)


def head_lanes(value, odd):
    lane = lax.broadcasted_iota(jnp.int32, value.shape, 1)
    return jnp.where((lane >= HEAD_DIM) == odd, value, jnp.zeros_like(value))


def probabilities(query, key, mask):
    scores = lax.dot_general(query, key, (((1,), (1,)), ((), ())), preferred_element_type=F32) * 0.125
    scores = jnp.where(mask, scores, masked_score)
    weights = jnp.exp(scores - jnp.max(scores, axis=-1, keepdims=True))
    return weights * (1.0 / jnp.sum(weights, axis=-1, keepdims=True))


def allowed_keys(qpos_ref, start_ref, kpos_ref):
    kpos = kpos_ref[...]
    return (kpos <= qpos_ref[...]) & (kpos >= start_ref[0])


def attend_kernel(q_ref, kv_ref, kv2_ref, out_ref, qpos_ref, start_ref, kpos_ref, o_ref, *term_refs):
    mask = allowed_keys(qpos_ref, start_ref, kpos_ref)
    wide = q_ref.shape[1]
    for pair in range(wide // 128):
        at = slice(pair * 128, (pair + 1) * 128)
        value_at = slice(wide + pair * 128, wide + (pair + 1) * 128)
        query = q_ref[:, at]
        key = jnp.concatenate([kv_ref[:, at], kv2_ref[:, at]], axis=0)
        value = jnp.concatenate([kv_ref[:, value_at], kv2_ref[:, value_at]], axis=0)
        total = None
        for odd in (False, True):
            weights = probabilities(head_lanes(query, odd), key, mask).astype(BF16)
            term = jnp.dot(weights, head_lanes(value, odd), preferred_element_type=F32)
            total = term if total is None else total + term
        o_ref[:, at] = total.astype(BF16)
    spill(term_refs, jnp.dot(o_ref[...], out_ref[...], preferred_element_type=F32).astype(BF16))


def fill(refs, target):
    at = 0
    for ref in refs:
        target[at : at + ref.shape[0]] = ref[...]
        at += ref.shape[0]


def spill(refs, value):
    at = 0
    for ref in refs:
        ref[...] = value[at : at + ref.shape[0]]
        at += ref.shape[0]


def at_step(step, action, refs, value):
    for k, group in enumerate((refs[:2], refs[2:])):

        @pl.when(step == k)
        def _(group=group):
            action(group, value)


def square_shapes(half, model):
    return [(half, model)] * 3 + [(half // 2, model)] * 2


def whole_shape(shape, **options):
    return pl.BlockSpec(shape, lambda i: (0, 0), **options)


def square_specs(half, model, **options):
    return [whole_shape(shape, **options) for shape in square_shapes(half, model)]


def sequence_shapes(sequence, half, model):
    return square_shapes(half, model)[2 * sequence : 2 + 3 * sequence]


def attend(sequence, q_all, kv_all, kv_other, out_rows, where, o_all):
    (tokens, wide), model = q_all.shape, out_rows.shape[1]
    rows = tokens // 2
    qpos, start, kpos = where
    at = lambda i: (sequence, 0)
    in_specs = [
        pl.BlockSpec((rows, wide), at),
        pl.BlockSpec((rows, 2 * wide), at),
        pl.BlockSpec((rows, 2 * wide), at),
        whole_spec(out_rows),
        whole_spec(qpos),
        pl.BlockSpec((1, rows, 1), lambda i: (sequence, 0, 0)),
        whole_spec(kpos),
    ]
    shapes = sequence_shapes(sequence, rows // 2, model)
    return into(
        attend_kernel, "attend", [q_all, kv_all, kv_other, out_rows, qpos, start, kpos], in_specs,
        [(tokens, wide)] + shapes, [pl.BlockSpec((rows, wide), at)] + [whole_shape(shape) for shape in shapes],
        [o_all], (1,),
    )


def into(kernel, name, operands, in_specs, shapes, out_specs, buffers, grid, types=None):
    count = len(operands)
    given = [b for b in buffers if b is not None]
    types = types or [BF16] * len(shapes)

    def body(*refs):
        return kernel(*refs[:count], *refs[count + len(given) :])

    return pl.pallas_call(
        body,
        grid=grid,
        in_specs=in_specs + [pl.BlockSpec(memory_space=pl.ANY)] * len(given),
        out_specs=out_specs,
        out_shape=[jax.ShapeDtypeStruct(shape, kind) for shape, kind in zip(shapes, types)],
        input_output_aliases={count + i: i for i in range(len(given))},
        compiler_params=BIG,
        cost_estimate=pl.CostEstimate(flops=0, bytes_accessed=1_000_000, transcendentals=0),
        name=name,
    )(*operands, *given)


def hidden_kernel(count, *refs):
    (b_refs, dy_refs), (w_ref, down_ref, z_ref, d_ref, b_ref, dy_ref) = (
        (refs[:count], refs[count : 2 * count]),
        refs[2 * count : 2 * count + 6],
    )
    db_refs, y_refs = refs[2 * count + 6 : 3 * count + 6], refs[3 * count + 6 :]
    fill(b_refs, b_ref)
    fill(dy_refs, dy_ref)
    piece = z_ref.shape[1] // HIDDEN_PIECES
    for i in range(HIDDEN_PIECES):
        at = slice(i * piece, (i + 1) * piece)
        gate_at, up_at = slice(2 * i * piece, (2 * i + 1) * piece), slice((2 * i + 1) * piece, (2 * i + 2) * piece)
        both = jnp.dot(b_ref[...], w_ref[:, 2 * i * piece : 2 * (i + 1) * piece], preferred_element_type=F32)
        gate, up = both[:, :piece], both[:, piece:]
        dz = lax.dot_general(dy_ref[...], down_ref[at, :], (((1,), (1,)), ((), ())), preferred_element_type=F32)
        sig = jax.nn.sigmoid(gate)
        silu = gate * sig
        z_ref[:, at] = (silu * up).astype(BF16)
        d_ref[:, gate_at] = (dz * up * sig * (1.0 + gate * (1.0 - sig))).astype(BF16)
        d_ref[:, up_at] = (dz * silu).astype(BF16)
    db = lax.dot_general(d_ref[...], w_ref[...], (((1,), (1,)), ((), ())), preferred_element_type=F32).astype(BF16)
    y = jnp.dot(z_ref[...], down_ref[...], preferred_element_type=F32).astype(BF16)

    spill(db_refs, db)
    spill(y_refs, y)


def hidden_units(index, b_blocks, dy_blocks, weight, down, buffers):
    model, width = weight.shape[0], down.shape[0]
    shapes = [block.shape for block in b_blocks]
    rows = sum(shape[0] for shape in shapes)
    once = dict(pipeline_mode=pl.Buffered(1))
    own = lambda columns: pl.BlockSpec((rows, columns), lambda i: (index, 0))
    operands = [*b_blocks, *dy_blocks, weight, down]
    out = into(
        functools.partial(hidden_kernel, len(shapes)), "hidden_units", operands,
        [whole_shape(a.shape, **once) for a in operands],
        [(4 * rows, width), (4 * rows, 2 * width), (4 * rows, model), (4 * rows, model)] + shapes * 2,
        [own(width), own(2 * width), own(model), own(model)] + [whole_shape(shape) for shape in shapes * 2],
        buffers, (1,),
    )
    return list(out[:4]), list(out[4 : 4 + len(shapes)]), list(out[4 + len(shapes) :])


def attend_back_kernel(count, *refs):
    out_ref, q_ref, kv_ref, kv2_ref, qpos_ref, start_ref, kpos_ref, cos_ref, sin_ref = refs[count : count + 9]
    dh_ref, dq_ref, dkv_ref, dkv2_ref = refs[count + 9 :]
    mask = allowed_keys(qpos_ref, start_ref, kpos_ref)
    rows, wide = q_ref.shape
    fill(refs[:count], dh_ref)
    do = lax.dot_general(
        dh_ref[...], out_ref[...], (((1,), (1,)), ((), ())), preferred_element_type=F32
    ).astype(BF16)
    for pair in range(wide // 128):
        at = slice(pair * 128, (pair + 1) * 128)
        value_at = slice(wide + pair * 128, wide + (pair + 1) * 128)
        query, grad = q_ref[:, at], do[:, at]
        key = jnp.concatenate([kv_ref[:, at], kv2_ref[:, at]], axis=0)
        value = jnp.concatenate([kv_ref[:, value_at], kv2_ref[:, value_at]], axis=0)
        dq = dk = dv = 0.0
        for odd in (False, True):
            query_one, grad_one = head_lanes(query, odd), head_lanes(grad, odd)
            weights = probabilities(query_one, key, mask)
            dp = lax.dot_general(grad_one, value, (((1,), (1,)), ((), ())), preferred_element_type=F32)
            inner = jnp.sum(dp * weights, axis=-1, keepdims=True)
            ds = (weights * (dp - inner)).astype(BF16)
            low = weights.astype(BF16)
            dq = dq + jnp.dot(ds, head_lanes(key, odd), preferred_element_type=F32)
            dk = dk + lax.dot_general(ds, query_one, (((0,), (0,)), ((), ())), preferred_element_type=F32)
            dv = dv + lax.dot_general(low, grad_one, (((0,), (0,)), ((), ())), preferred_element_type=F32)
        dq_ref[:, at] = turn(dq * 0.125, cos_ref[...], -sin_ref[...]).astype(BF16)
        dkv_ref[:, at] = dk[:rows] * 0.125
        dkv2_ref[:, at] = (dk[rows:] * 0.125).astype(BF16)
        dkv_ref[:, value_at] = dv[:rows]
        dkv2_ref[:, value_at] = dv[rows:].astype(BF16)


def attend_back(sequence, dh_blocks, out_rows, q_all, kv_all, kv_other, where, tables, dh_all):
    model, (tokens, wide) = dh_blocks[0].shape[1], q_all.shape
    rows = tokens // 2
    qpos, start, kpos = where
    at = lambda i: (sequence, 0)
    in_specs = [whole_spec(block) for block in dh_blocks] + [
        whole_spec(out_rows),
        pl.BlockSpec((rows, wide), at),
        pl.BlockSpec((rows, 2 * wide), at),
        pl.BlockSpec((rows, 2 * wide), at),
        whole_spec(qpos),
        pl.BlockSpec((1, rows, 1), lambda i: (sequence, 0, 0)),
        whole_spec(kpos), whole_spec(tables[0]), whole_spec(tables[1]),
    ]
    return into(
        functools.partial(attend_back_kernel, len(dh_blocks)), "attend_back",
        [*dh_blocks, out_rows, q_all, kv_all, kv_other, qpos, start, kpos, *tables],
        in_specs, [(tokens, model), (rows, wide), (rows, 2 * wide), (rows, 2 * wide)],
        [pl.BlockSpec((rows, model), at)] + [whole_shape((rows, n * wide)) for n in (1, 2, 2)],
        [dh_all], (1,), types=[BF16, BF16, F32, BF16],
    )


def join_kernel(dq_ref, dkv_ref, dkv2_ref, cos_ref, sin_ref, out_ref):
    wide = dq_ref.shape[1]
    out_ref[:, :wide] = dq_ref[...]
    for i in range(wide // 128):
        at = slice(i * 128, (i + 1) * 128)
        dk = dkv_ref[:, at] + dkv2_ref[:, at].astype(F32)
        out_ref[:, wide + i * 128 : wide + (i + 1) * 128] = turn(dk, cos_ref[...], -sin_ref[...]).astype(BF16)
    out_ref[:, 2 * wide :] = (dkv_ref[:, wide:] + dkv2_ref[:, wide:].astype(F32)).astype(BF16)


def join_grads(sequence, dq, dkv, dkv_other, tables, d_qkv):
    rows, wide = dq.shape
    operands = [dq, dkv, dkv_other, *tables]
    (d_qkv,) = into(
        join_kernel, "join_grads", operands, [whole_spec(a) for a in operands],
        [(2 * rows, 3 * wide)], [pl.BlockSpec((rows, 3 * wide), lambda i: (sequence, 0))], [d_qkv], (1,),
    )
    return d_qkv


def input_terms_kernel(d_ref, w_ref, w2_ref, core_ref, *term_refs):
    mine, other = (
        lax.dot_general(d_ref[...], ref[...], (((1,), (1,)), ((), ())), preferred_element_type=F32).astype(BF16)
        for ref in (w_ref, w2_ref)
    )
    first = core_ref[0] == 0
    terms = jnp.concatenate([jnp.where(first, mine, other), jnp.where(first, other, mine)], axis=1)
    at_step(pl.program_id(0), spill, term_refs, terms)


def input_terms(core, d_qkv, weights):
    tokens, wide = d_qkv.shape
    model = 2 * weights[0].shape[0]
    return into(
        input_terms_kernel, "input_terms", [d_qkv, *weights, core],
        [pl.BlockSpec((tokens // 2, wide), lambda i: (i, 0)), whole_spec(weights[0]), whole_spec(weights[1]),
         pl.BlockSpec(memory_space=pltpu.SMEM)],
        square_shapes(tokens // 4, model), square_specs(tokens // 4, model), [], (2,),
    )


def on_rows(kernel, name, operands, types):
    rows, model = operands[0].shape
    tile = pl.BlockSpec((rows // 3, model), lambda i: (i, 0))
    return pl.pallas_call(
        kernel,
        grid=(3,),
        in_specs=[tile] * len(operands),
        out_specs=[tile] * len(types),
        out_shape=[jax.ShapeDtypeStruct((rows, model), kind) for kind in types],
        compiler_params=BIG,
        cost_estimate=pl.CostEstimate(flops=0, bytes_accessed=1_000_000, transcendentals=0),
        name=name,
    )(*operands)


def total_of(refs):
    return add_low(*[ref[...] for ref in refs])


def open_kernel(x_ref, a_ref):
    x = x_ref[...].astype(F32)
    inverse = lax.rsqrt(jnp.mean(x * x, axis=-1, keepdims=True) + epsilon)
    a_ref[...] = to_inner((x * inverse).astype(BF16))


def close_attention_kernel(x_ref, *refs):
    hidden_ref, b_ref = refs[-2:]
    hidden = x_ref[...].astype(F32) + total_of(refs[:-2])
    hidden_ref[...] = hidden
    inverse = lax.rsqrt(jnp.mean(hidden * hidden, axis=-1, keepdims=True) + epsilon)
    b_ref[...] = to_inner((hidden * inverse).astype(BF16))


def close_hidden_kernel(dy_ref, hidden_ref, *refs):
    dh_ref, low_ref = refs[-2:]
    dh = dy_ref[...].astype(F32) + norm_back(hidden_ref[...], to_outer(total_of(refs[:-2])))
    dh_ref[...] = dh
    low_ref[...] = dh.astype(BF16)


def close_input_kernel(x_ref, dh_ref, *refs):
    out_ref = refs[-1]
    out_ref[...] = (dh_ref[...] + norm_back(x_ref[...].astype(F32), to_outer(total_of(refs[:-1])))).astype(BF16)


def norm_back(values, scaled):
    inverse = lax.rsqrt(jnp.mean(values * values, axis=-1, keepdims=True) + epsilon)
    normed = values * inverse
    return inverse * (scaled - normed * jnp.mean(scaled * normed, axis=-1, keepdims=True))


def dot_low(left, right, left_dim, right_dim):
    return lax.dot_general(
        left, right, (((left_dim,), (right_dim,)), ((), ())), preferred_element_type=F32
    ).astype(BF16)


def paired_device(
    layer_input, document_ids, cotangent, attention_gain, query_weight, key_weight, value_weight, output_weight,
    feedforward_gain, gate_weight, up_weight, down_weight,
):
    place = Place()
    x_own, dy_own = layer_input[0], cotangent[0]
    tok_count, model = x_own.shape
    block_rows = tok_count // 2
    length = document_ids.shape[1]
    block_count = length // block_rows
    rows = query_weight.shape[0]
    hidden_rows = down_weight.shape[0]

    attn_gain = attention_gain.astype(F32)[:, None]
    ff_gain = feedforward_gain.astype(F32)[:, None]

    documents = document_ids[0]
    first = jnp.sum((documents[None, :] < documents[:, None]).astype(jnp.int32), axis=1)
    mine, sent = head_slices(place, [query_weight, key_weight, value_weight], attn_gain, rows)
    out_half = chip_half(place, output_weight)
    dy_l = swap(dy_own, "zl")
    first = jnp.stack([first, swap(first, "seq")])
    mine, sent, out_half, x_late, down_late, gate_late, up_late = fence(
        [mine, sent, out_half, x_own, down_weight, gate_weight, up_weight], []
    )
    (a_own,) = on_rows(open_kernel, "open_layer", [x_late], [BF16])

    received = swap(sent, "x")
    out_zh, out_zl = swap(out_half, "zh"), swap(out_half, "zl")
    qkv = in_order(mine, received, place.x)
    down_half = chip_half(place, down_late)
    quarter = down_half.shape[0] * 3 // 4
    qkv, a_own, out_zh, out_zl, dy_late, down_half, dy_l, first = fence(
        [qkv, a_own, out_zh, out_zl, dy_own, down_half, dy_l, first], []
    )

    gate_up = hidden_slices(place, [gate_late, up_late], ff_gain, hidden_rows)
    by_zh, by_zl = swap(qkv, "zh"), swap(qkv, "zl")
    a_x, a_s = along(a_own)
    out_both = swap(out_zh, "zl")
    by_zh, by_zl, a_x, a_s, dy_late, out_both, gate_up, down_half = fence(
        [by_zh, by_zl, a_x, a_s, dy_late, out_both, gate_up, down_half], []
    )

    by_both = swap(by_zh, "zl")
    dy_x, dy_s = along(dy_late)
    a_o = opposite(a_x, a_s)
    out_half = in_order(
        in_order(out_half, out_zl, place.zl), in_order(out_zh, out_both, place.zl), place.zh
    ).reshape(4, -1, model)
    qkv = in_order(in_order(qkv, by_zl, place.zl), in_order(by_zh, by_both, place.zl), place.zh)
    a_all = jnp.concatenate([a_own, a_x, a_s, *a_o], axis=0)

    def positions(dx, dc):
        holder = (place.x ^ dx) * 2 + (place.core ^ dc)
        return place_of(holder, jnp.arange(tok_count, dtype=jnp.int32), block_rows, block_count // 2)

    qpos = jnp.concatenate([positions(0, 0), positions(1, 0)])
    kpos = jnp.concatenate([positions(0, 0), positions(1, 0), positions(0, 1), positions(1, 1)])
    cosine, sine = rotation(qpos, HEAD_DIM)
    cosine = jnp.concatenate([cosine] * 4, axis=1)
    sine = jnp.concatenate([-sine, sine] * 2, axis=1)
    firsts = first.reshape(2, block_count, block_rows)
    starts = []
    for dx in range(2):
        holder = (place.x ^ dx) * 2 + place.core
        for index in (holder, block_count - 1 - holder):
            starts.append(lax.dynamic_index_in_dim(firsts, index, 1, False))
    start = jnp.concatenate(starts, axis=1)[:, :, None]
    where = (qpos[:, None], start, kpos[None, :])
    tables = (cosine, sine)
    qkv, dy_l, tables, a_all, down_half, out_half, gate_up = fence(
        [qkv, dy_l, tables, a_all, down_half, out_half, gate_up], []
    )

    qkv = qkv.reshape(model // 2, -1)
    qkv_other = swap(qkv, "core")
    gate_up = share_columns(gate_up)
    down_far = [swap(down_half[:quarter], "zh")]
    out_rows = chip_rows(place, out_half, swap(out_half, "core"))
    core = jnp.stack([place.core]).astype(jnp.int32)
    qkv, qkv_other, core, dy_l, down_half, down_far = fence(
        [qkv, qkv_other, core, dy_l, down_half, down_far], []
    )

    q_all, kv_all = project(core, a_all, qkv, qkv_other, *tables)
    down_far += [swap(down_half[quarter:], "zh")]
    q_all, kv_all, down_half, down_far, dy_x, dy_s, dy_l, where, gate_up = fence(
        [q_all, kv_all, down_half, down_far, dy_x, dy_s, dy_l, where, gate_up], [out_rows]
    )

    gate_up = lax.all_gather(gate_up, ("core", "zh"), axis=0, tiled=True).reshape(model, -1)
    dy_o = opposite(dy_x, dy_s)
    kv_other = swap(kv_all, "core")
    o_all, term_s, *term_o = attend(1, q_all, kv_all, kv_other, out_rows, where, None)
    down_half = in_order(down_half, jnp.concatenate(down_far), place.zh)
    down_rows = chip_rows(place, down_half, swap(down_half, "core"))
    term_s, term_o, o_all, down_rows, dy_l = fence([term_s, term_o, o_all, down_rows, dy_l], dy_o)

    o_all, own, term_x = attend(0, q_all, kv_all, kv_other, out_rows, where, o_all)
    halves = return_halves(*term_o)
    own, term_x, halves, dy_l = fence([own, term_x, halves, dy_l], [])

    sums = return_along(term_x, term_s, *halves)
    hidden, b_own = on_rows(close_attention_kernel, "close_attention", [x_own, own, *sums], [F32, BF16])
    b_own, dy_l = fence([b_own, dy_l], [])

    b_x, b_s = along(b_own)
    b_l = swap(b_own, "zl")
    dy_lx, dy_ls = along(dy_l)
    b_x, b_s, dy_lx, dy_ls = fence([b_x, b_s, dy_lx, dy_ls], [])

    b_o = opposite(b_x, b_s)
    buffers, db0, y0 = hidden_units(0, [b_own, b_x], [dy_own, dy_x], gate_up, down_rows, [None] * 4)
    dy_lo = opposite(dy_lx, dy_ls)
    buffers, b_o, b_l = fence([buffers, b_o, b_l], dy_lo)

    b_lx, b_ls = along(b_l)
    buffers, db1, y1 = hidden_units(1, [b_s, *b_o], [dy_s, *dy_o], gate_up, down_rows, buffers)
    buffers, b_lx, b_ls, db1 = fence([buffers, b_lx, b_ls, db1], [])

    b_lo = opposite(b_lx, b_ls)
    near_halves = return_halves(*db1[1:])
    buffers, db2, y2 = hidden_units(2, [b_l, b_lx], [dy_l, dy_lx], gate_up, down_rows, buffers)
    buffers, b_lo, near_halves = fence([buffers, b_lo, near_halves], [])

    near_along = return_along(db0[1], db1[0], *near_halves)
    buffers, db3, y3 = hidden_units(3, [b_ls, *b_lo], [dy_ls, *dy_lo], gate_up, down_rows, buffers)
    z_all, d_all, b_all, dy_all = buffers
    db3, z_all, d_all, near_along = fence([db3, z_all, d_all, near_along], [])

    far_halves = return_halves(*db3[1:])
    down_terms = dot_low(z_all, dy_all, 0, 0)
    d_all, down_terms, far_halves = fence([d_all, down_terms, far_halves], [])

    far_along = return_along(db2[1], db3[0], *far_halves)
    gate_up_terms = dot_low(b_all, d_all, 0, 0)
    down_sums = add_core(place, down_terms.reshape(2, 2, -1, model), 1)
    gate_up_terms, down_sums, y0, y1, near0, far_along = fence(
        [gate_up_terms, down_sums, y0, y1, db0[0], far_along], []
    )

    down_total = lax.psum_scatter(down_sums, "zh", scatter_dimension=0, tiled=True)[0]
    across = return_across(db2[0], *far_along)
    near_y_along = return_along(y0[1], y1[0], *return_halves(*y1[1:]))
    gate_up_sums = add_core(place, gate_up_terms.reshape(2, 2, 4, rows, -1), 0)
    across, gate_up_sums = fence([across, gate_up_sums], [])
    dh, dh_low = on_rows(
        close_hidden_kernel, "close_hidden", [dy_own, hidden, near0, *near_along, across], [F32, BF16]
    )
    dh_low, gate_up_sums, near_y_along = fence([dh_low, gate_up_sums, near_y_along], [])

    gate_up_near = lax.psum_scatter(gate_up_sums, "zh", scatter_dimension=0, tiled=True)[0]
    dh_x, dh_s = along(dh_low)
    dh_x, dh_s, y3 = fence([dh_x, dh_s, y3], [])

    dh_o = opposite(dh_x, dh_s)
    dh_all, dq0, dkv0, dkv_other0 = attend_back(
        0, [dh_low, dh_x], out_rows, q_all, kv_all, kv_other, where, tables, None
    )
    dkv_other0, dh_s, y3 = fence([dkv_other0, dh_s, y3], dh_o)

    dkv_other0 = swap(dkv_other0, "core")
    down_other = swap(down_total, "seq")
    dh_all, dq1, dkv1, dkv_other1 = attend_back(
        1, [dh_s, *dh_o], out_rows, q_all, kv_all, kv_other, where, tables, dh_all
    )
    far_y_halves = return_halves(*y3[1:])
    dkv_other1, dh_all = fence([dkv_other1, dh_all], [])

    dkv_other1 = swap(dkv_other1, "core")
    d_qkv = join_grads(0, dq0, dkv0, dkv_other0, tables, None)
    out_terms = dot_low(o_all, dh_all, 0, 0)
    d_qkv, dkv_other1, out_terms, far_y_halves, down_other = fence(
        [d_qkv, dkv_other1, out_terms, far_y_halves, down_other], []
    )

    d_qkv = join_grads(1, dq1, dkv1, dkv_other1, tables, d_qkv)
    qkv_terms = dot_low(a_all, d_qkv, 0, 0)
    far_y_along = return_along(y2[1], y3[0], *far_y_halves)
    out_sums = add_core(place, out_terms.reshape(4, 2, -1, model), 1).reshape(2, 2, -1, model)
    qkv_terms, out_sums, d_qkv = fence([qkv_terms, out_sums, d_qkv], [])

    def part(sums, zh, zl):
        return lax.dynamic_slice(sums, (place.zh ^ zh, place.zl ^ zl, 0, 0), (1, 1, *sums.shape[2:]))[0, 0]

    qkv_sums = add_core(place, qkv_terms.reshape(2, 2, 2, 2 * rows, -1), 0)
    own, term_x, term_s, *term_o = input_terms(core, d_qkv, [qkv, qkv_other])
    out_zl = swap(part(out_sums, 1, 1), "zl")
    qkv_sums, out_sums, out_zl, term_o, far_y_along, gate_up_near = fence(
        [qkv_sums, out_sums, out_zl, term_o, far_y_along, gate_up_near], []
    )

    qkv_zl = swap(part(qkv_sums, 1, 1), "zl")
    gate_up_near = share_columns(gate_up_near)
    by_seq = jnp.concatenate([swap(half, "seq") for half in term_o])
    sums = [swap(add_low(term_x, by_seq).astype(BF16), "x"), swap(term_s, "seq")]
    down_grad = own_rows(place, down_total, down_other)
    qkv_zl, gate_up_near, sums, out_zl = fence([qkv_zl, gate_up_near, sums, out_zl], [down_grad])

    qkv_zh = swap(add_low(part(qkv_sums, 1, 0), qkv_zl).astype(BF16), "zh")
    qkv_zl = swap(part(qkv_sums, 0, 1), "zl")
    gate_up_far = swap(gate_up_near, "seq")
    (input_grad,) = on_rows(close_input_kernel, "close_input", [x_own, dh, own, *sums], [BF16])
    qkv_zh, qkv_zl, out_zl, out_sums = fence([qkv_zh, qkv_zl, out_zl, out_sums], [input_grad])

    qkv_total = add_low(part(qkv_sums, 0, 0), qkv_zl, qkv_zh).astype(BF16).reshape(2, rows, -1)
    kept = lax.dynamic_index_in_dim(qkv_total, place.x, 0, False)
    received = swap(lax.dynamic_index_in_dim(qkv_total, 1 - place.x, 0, False), "x")
    kept_far, received_far = swap(kept, "seq"), swap(received, "seq")
    out_zh = swap(add_low(part(out_sums, 1, 0), out_zl).astype(BF16), "zh")
    out_zl = swap(part(out_sums, 0, 1), "zl")
    (gate_grad, up_grad), ff_gain_grad = finish_columns(
        place, *[v.reshape(2, 2, rows, -1) for v in (gate_up_near, gate_up_far)], [gate_weight, up_weight], ff_gain,
        hidden_rows, True,
    )
    y_across = return_across(y2[0], *far_y_along)
    kept, kept_far, received, received_far, out_zl = fence(
        [kept, kept_far, received, received_far, out_zl], [ff_gain_grad]
    )

    out_total = add_low(part(out_sums, 0, 0), out_zl, out_zh).astype(BF16)
    out_other = swap(out_total, "seq")
    (query_grad, key_grad, value_grad), attn_gain_grad = finish_columns(
        place, in_order(kept, received, place.x), in_order(kept_far, received_far, place.x),
        [query_weight, key_weight, value_weight], attn_gain, rows, False,
    )
    (out_other,) = fence([out_other], [attn_gain_grad])
    output_grad = own_rows(place, out_total, out_other)
    layer_output = add_low(hidden, y0[0], *near_y_along, y_across).astype(BF16)
    return (
        layer_output[None], input_grad[None], attn_gain_grad, query_grad, key_grad, value_grad, output_grad,
        ff_gain_grad, gate_grad, up_grad, down_grad,
    )


def paired(mesh):
    fine = Mesh(mesh.devices.reshape(2, 2, 2, 2, 2), ("seq", "x", "core", "zh", "zl"))
    tokens = P(("seq", "zh", "zl"), ("x", "core"), None)
    matrix, vector = P(("x", "core", "zh", "zl"), None), P(("x", "core", "zh", "zl"))
    return jax.shard_map(
        paired_device,
        mesh=fine,
        in_specs=(tokens, P(("seq", "zh", "zl"), None), tokens, vector) + (matrix,) * 4 + (vector,) + (matrix,) * 3,
        out_specs=(tokens, tokens, vector) + (matrix,) * 4 + (vector,) + (matrix,) * 3,
        check_vma=False,
    )


def solution(mesh):
    if tuple(mesh.shape[axis] for axis in ("seq", "ctx", "fsdp")) == (2, 4, 4):
        return paired(mesh)
    return gathered(mesh)
```
